32 devices in a mesh: dp: 4 (over z), fsdp: 8 (over y, x, core).
Axes of the slice: x: 2, y: 2, z: 4, core: 2. Of those that a mesh axis runs over, the one named last changes fastest.
Arguments:
- tokens: bfloat16 [64, 640, 768], P(('dp', 'fsdp')), may hold values from -6 to 6
- cotangent: bfloat16 [64, 640, 768], P(('dp', 'fsdp')), may hold values from -6 to 6
- seg_lengths: int32 [64], P(('dp', 'fsdp')), may hold values from 5 to 128, as said below
- alignment: int32 [64, 512], P(('dp', 'fsdp')), may hold values from 0 to 127, as said below
- query_weight: bfloat16 [768, 768], P(('dp', 'fsdp')), may hold values from -0.3125 to 0.3125
- query_bias: bfloat16 [768], P(('dp', 'fsdp')), may hold values from -3 to 3
- key_weight: bfloat16 [768, 768], P(('dp', 'fsdp')), may hold values from -0.21875 to 0.21875
- value_weight: bfloat16 [768, 768], P(('dp', 'fsdp')), may hold values from -0.21875 to 0.21875
- value_bias: bfloat16 [768], P(('dp', 'fsdp')), may hold values from -3 to 3
- out_weight: bfloat16 [768, 768], P(('dp', 'fsdp')), may hold values from -0.625 to 0.625
- out_bias: bfloat16 [768], P(('dp', 'fsdp')), may hold values from -3 to 3
- first_gain: bfloat16 [768], P(('dp', 'fsdp')), may hold values from 0.25 to 1.75
- first_shift: bfloat16 [768], P(('dp', 'fsdp')), may hold values from -2 to 2
- inner_weight: bfloat16 [768, 3072], P(('dp', 'fsdp')), may hold values from -0.21875 to 0.21875
- inner_bias: bfloat16 [3072], P(('dp', 'fsdp')), may hold values from -3 to 3
- outer_weight: bfloat16 [3072, 768], P(('dp', 'fsdp')), may hold values from -0.21875 to 0.21875
- outer_bias: bfloat16 [768], P(('dp', 'fsdp')), may hold values from -3 to 3
- second_gain: bfloat16 [768], P(('dp', 'fsdp')), may hold values from 0.25 to 1.75
- second_shift: bfloat16 [768], P(('dp', 'fsdp')), may hold values from -2 to 2
Outputs:
- encoded: bfloat16 [64, 640, 768], P(('dp', 'fsdp'))
- grad_tokens: bfloat16 [64, 640, 768], P(('dp', 'fsdp'))
- grad_query_weight: float32 [768, 768], P(('dp', 'fsdp'))
- grad_query_bias: float32 [768], P(('dp', 'fsdp'))
- grad_key_weight: float32 [768, 768], P(('dp', 'fsdp'))
- grad_value_weight: float32 [768, 768], P(('dp', 'fsdp'))
- grad_value_bias: float32 [768], P(('dp', 'fsdp'))
- grad_out_weight: float32 [768, 768], P(('dp', 'fsdp'))
- grad_out_bias: float32 [768], P(('dp', 'fsdp'))
- grad_first_gain: float32 [768], P(('dp', 'fsdp'))
- grad_first_shift: float32 [768], P(('dp', 'fsdp'))
- grad_inner_weight: float32 [768, 3072], P(('dp', 'fsdp'))
- grad_inner_bias: float32 [3072], P(('dp', 'fsdp'))
- grad_outer_weight: float32 [3072, 768], P(('dp', 'fsdp'))
- grad_outer_bias: float32 [768], P(('dp', 'fsdp'))
- grad_second_gain: float32 [768], P(('dp', 'fsdp'))
- grad_second_shift: float32 [768], P(('dp', 'fsdp'))
The draws below stay inside these ranges and needn't reach their ends.
Inputs may be any that keep to these rules, and one draw needn't show every extreme that they name: `seg_lengths`: one document has exactly 128 segment tokens and another exactly 5. `alignment`: each text token names a segment below its document's segment count.
All inputs are finite; a program needn't handle non-finite values.
Results may differ from the reference program's by a relative error of at most 0.017.
Values may be sent and summed in bfloat16 or wider, within the bound.
A program may use at most 192 MiB of HBM per device.

```python
import jax
import jax.numpy as jnp
from jax import lax

D = 768
HEADS = 12
HEAD_DIM = 64
FF = 3072
TEXT = 512
SEG = 128
SLOTS = 640
DOCS = 64


def document_lengths(key):
    keys = jax.random.split(jax.random.fold_in(key, 101), 5)
    span = SEG - 4
    first_draw = jax.random.randint(keys[0], (DOCS,), 0, span)
    second_draw = jax.random.randint(keys[1], (DOCS,), 0, span)
    third_draw = jax.random.randint(keys[2], (DOCS,), 0, span)
    lengths = 5 + first_draw * second_draw * third_draw // (span * span)
    longest = jax.random.randint(keys[3], (), 0, DOCS)
    shortest = (longest + 1 + jax.random.randint(keys[4], (), 0, DOCS - 1)) % DOCS
    positions = jnp.arange(DOCS, dtype=jnp.int32)
    lengths = jnp.where(positions == longest, SEG, jnp.where(positions == shortest, 5, lengths))
    return (lengths.astype(jnp.int32), longest)


def draw_seg_lengths(key, part):
    lengths, longest = document_lengths(key)
    return lengths


def draw_alignment(key, part):
    lengths, longest = document_lengths(key)
    key = jax.random.fold_in(key, 7)
    raw_bits = jax.random.randint(key, (DOCS, TEXT), 0, 2 ** 30)
    aligned = raw_bits % lengths[:, None]
    row_ids = jnp.arange(DOCS, dtype=jnp.int32)[:, None]
    col_ids = jnp.arange(TEXT, dtype=jnp.int32)[None, :]
    aligned = jnp.where((row_ids == longest) & (col_ids == TEXT - 1), SEG - 1, aligned)
    return aligned.astype(jnp.int32)


def levels(rng, shape, cuts, smallest, largest):
    gain = 1.0
    for axis_at, blocks in cuts:
        steps = jax.random.uniform(jax.random.fold_in(jax.random.fold_in(rng, 6), axis_at), (blocks,), jnp.float32, smallest / len(cuts), largest / len(cuts))
        gain = gain * jnp.repeat(jnp.exp(steps), shape[axis_at] // blocks).reshape((-1,) + (1,) * (len(shape) - 1 - axis_at))
    return gain


def normal_values(key, shape, deviation, most, cuts=(), held_as=jnp.bfloat16):
    array = deviation * jax.random.normal(key, shape, jnp.float32)
    if cuts:
        array = array * levels(key, shape, cuts, -0.22, 0.18)
    return jnp.clip(array, -most, most).astype(held_as)


def setup_inputs(seed: int = 0) -> dict:
    arg_keys = jax.random.split(jax.random.key(seed), 20)
    return {
        "tokens": normal_values(arg_keys[0], (DOCS, SLOTS, D), 1.0, 6.0, ((0, 32),)),
        "cotangent": normal_values(arg_keys[1], (DOCS, SLOTS, D), 1.0, 6.0, ((0, 32),)),
        "seg_lengths": draw_seg_lengths(jax.random.fold_in(arg_keys[19], 71), 0),
        "alignment": draw_alignment(jax.random.fold_in(arg_keys[19], 71), 0),
        "query_weight": normal_values(arg_keys[4], (D, D), (D // 2) ** -0.5, 0.3125, ((0, 32),)),
        "query_bias": normal_values(arg_keys[5], (D,), 0.5, 3.0, ((0, 32),)),
        "key_weight": normal_values(arg_keys[6], (D, D), D ** -0.5, 0.21875, ((0, 32),)),
        "value_weight": normal_values(arg_keys[7], (D, D), D ** -0.5, 0.21875, ((0, 32),)),
        "value_bias": normal_values(arg_keys[8], (D,), 0.5, 3.0, ((0, 32),)),
        "out_weight": normal_values(arg_keys[9], (D, D), (D // 8) ** -0.5, 0.625, ((0, 32),)),
        "out_bias": normal_values(arg_keys[10], (D,), 0.5, 3.0, ((0, 32),)),
        "first_gain": jnp.clip(1.0 + 0.15 * jax.random.normal(arg_keys[11], (D,), jnp.float32), 0.25, 1.75).astype(jnp.bfloat16),
        "first_shift": normal_values(arg_keys[12], (D,), 0.3, 2.0, ((0, 32),)),
        "inner_weight": normal_values(arg_keys[13], (D, FF), D ** -0.5, 0.21875, ((0, 32),)),
        "inner_bias": normal_values(arg_keys[14], (FF,), 0.5, 3.0, ((0, 32),)),
        "outer_weight": normal_values(arg_keys[15], (FF, D), (FF // 4) ** -0.5, 0.21875, ((0, 32),)),
        "outer_bias": normal_values(arg_keys[16], (D,), 0.5, 3.0, ((0, 32),)),
        "second_gain": jnp.clip(1.0 + 0.15 * jax.random.normal(arg_keys[17], (D,), jnp.float32), 0.25, 1.75).astype(jnp.bfloat16),
        "second_shift": normal_values(arg_keys[18], (D,), 0.3, 2.0, ((0, 32),)),
    }


@jax.custom_vjp
def low(v):
    return lax.optimization_barrier(v.astype(jnp.bfloat16)).astype(jnp.float32)

@jax.custom_vjp
def low_back(v):
    return v

def low_keep(v):
    return (low(v), None)

def low_pass(kept, grad):
    return (grad,)

def back_keep(v):
    return (v, None)

def back_low(kept, grad):
    return (low(grad),)
low.defvjp(low_keep, low_pass)
low_back.defvjp(back_keep, back_low)
norm_eps = 1e-05
masked_score = -1000000000.0

def exact_einsum(form, left_side, right_side):
    return jnp.einsum(form, left_side, right_side, precision=lax.Precision.HIGHEST)

def layer_norm(values_in, gain_vec, shift_vec):
    centred = values_in - lax.optimization_barrier(jnp.mean(values_in, axis=-1, keepdims=True))
    variance = lax.optimization_barrier(jnp.mean(centred * centred, axis=-1, keepdims=True))
    return centred * lax.rsqrt(variance + norm_eps) * gain_vec + shift_vec

def attend_document(packed):
    query_rows, key_rows, value_rows, valid_keys = packed
    slot_count = query_rows.shape[0]
    query_heads = query_rows.reshape(slot_count, HEADS, HEAD_DIM)
    key_heads = key_rows.reshape(slot_count, HEADS, HEAD_DIM)
    value_heads = value_rows.reshape(slot_count, HEADS, HEAD_DIM)
    scores = low_back(exact_einsum('qhd,khd->hqk', query_heads, key_heads) * HEAD_DIM ** (-0.5))
    scores = jnp.where(valid_keys[None, None, :], scores, masked_score)
    probs_low = low(jax.nn.softmax(scores, axis=-1))
    mixed_heads = exact_einsum('hqk,khd->qhd', probs_low, value_heads)
    return mixed_heads.reshape(slot_count, HEADS * HEAD_DIM)

def forward(tokens_f, params, member, counts, valid_keys):
    query_weight, query_bias, key_weight, value_weight, value_bias, out_weight, out_bias, first_gain, first_shift, inner_weight, inner_bias, outer_weight, outer_bias, second_gain, second_shift = params
    pooled = exact_einsum('bst,btd->bsd', member, tokens_f[:, :TEXT]) / counts[:, :, None]
    base = tokens_f + jnp.concatenate([jnp.zeros_like(tokens_f[:, :TEXT]), pooled], axis=1)
    base_low = low(base)
    query_rows = low(low_back(exact_einsum('bsd,de->bse', base_low, query_weight) + query_bias))
    key_rows = low(low_back(exact_einsum('bsd,de->bse', base_low, key_weight)))
    value_rows = low(low_back(exact_einsum('bsd,de->bse', base_low, value_weight) + value_bias))
    attended = lax.map(jax.checkpoint(attend_document), (query_rows, key_rows, value_rows, valid_keys))
    attended = low(low_back(attended))
    branch = low_back(exact_einsum('bsd,de->bse', attended, out_weight) + out_bias)
    normed = layer_norm(base + branch, first_gain, first_shift)
    pre_act = low_back(exact_einsum('bsd,df->bsf', low(normed), inner_weight) + inner_bias)
    act_low = low(jax.nn.gelu(pre_act, approximate=False))
    mlp_out = low_back(exact_einsum('bsf,fd->bsd', act_low, outer_weight) + outer_bias)
    return layer_norm(normed + mlp_out, second_gain, second_shift)

def reference(tokens, cotangent, seg_lengths, alignment, query_weight, query_bias, key_weight, value_weight, value_bias, out_weight, out_bias, first_gain, first_shift, inner_weight, inner_bias, outer_weight, outer_bias, second_gain, second_shift):
    segment_ids = jnp.arange(SEG, dtype=jnp.int32)
    member = (alignment[:, None, :] == segment_ids[None, :, None]).astype(jnp.float32)
    counts = jnp.maximum(lax.optimization_barrier(jnp.sum(member, axis=-1)), 1.0)
    slot_ids = jnp.arange(TEXT + SEG, dtype=jnp.int32)
    valid_keys = slot_ids[None, :] < TEXT + seg_lengths[:, None]
    params = tuple((weight_arg.astype(jnp.float32) for weight_arg in (query_weight, query_bias, key_weight, value_weight, value_bias, out_weight, out_bias, first_gain, first_shift, inner_weight, inner_bias, outer_weight, outer_bias, second_gain, second_shift)))

    def forward_all(tokens_f, *weights):
        return forward(tokens_f, weights, member, counts, valid_keys)
    encoded, pullback = jax.vjp(forward_all, tokens.astype(jnp.float32), *params)
    gradients = pullback(cotangent.astype(jnp.float32))
    return (encoded.astype(jnp.bfloat16), gradients[0].astype(jnp.bfloat16), gradients[1], gradients[2], gradients[3], gradients[4], gradients[5], gradients[6], gradients[7], gradients[8], gradients[9], gradients[10], gradients[11], gradients[12], gradients[13], gradients[14], gradients[15])
```

```python
import functools
import jax
import jax.numpy as jnp
from jax import lax
from jax.experimental import pallas as pl
from jax.experimental.pallas import tpu as pltpu
from jax.sharding import PartitionSpec as P

MESH = pl.DeviceIdType.MESH
ANY = pl.BlockSpec(memory_space=pl.ANY)
VMEM = pl.BlockSpec(memory_space=pltpu.VMEM)
PLANES = 4
CHIPS = 16


class Place:
    def __init__(self):
        self.z = lax.axis_index("dp")
        self.f = lax.axis_index("fsdp")
        self.core = self.f % 2
        self.x = (self.f // 2) % 2
        self.y = self.f // 4
        self.sib = self.f + 1 - 2 * self.core
        self.xn = self.f + 2 - 4 * self.x
        self.yn = self.f + 4 - 8 * self.y
        self.spot = self.f // 2
        self.spot_x = self.xn // 2
        self.spot_y = self.yn // 2
        self.spot_d = 3 - self.spot

    def plane(self, back):
        return (self.z + PLANES - back) % PLANES

    def ahead(self, step):
        return (self.z + step) % PLANES

    def barrier(self):
        bar = pltpu.get_barrier_semaphore()
        for other in self.partners():
            pl.semaphore_signal(bar, inc=1, device_id=other, device_id_type=MESH)
        pl.semaphore_wait(bar, 3 + PLANES - 1)

    def partners(self):
        return [(self.z, self.sib), (self.z, self.xn), (self.z, self.yn)] + [
            (self.ahead(k), self.f) for k in range(1, PLANES)
        ]


def remote(src, dst, send, recv, dev):
    return pltpu.make_async_remote_copy(
        src_ref=src, dst_ref=dst, send_sem=send, recv_sem=recv, device_id=dev, device_id_type=MESH
    )


class Gather:
    SEMS = 3 + 4 + 4 + 4 + 4 + 4

    def __init__(self, place, full, own, send, recv, local, width=None):
        self.p, self.full, self.own = place, full, own
        self.send, self.recv, self.local = send, recv, local
        self.half = None if width is None else width // 2
        self.rows = own.shape[0]
        self.started = []

    def view(self, chip, r0=0, r1=None, core=None):
        core = self.p.core if core is None else core
        r1 = self.rows if r1 is None else r1
        if self.half is None:
            return self.full.at[chip, core, pl.ds(r0, r1 - r0), :]
        cols = pl.ds(pl.multiple_of(core * self.half, 128), self.half)
        return self.full.at[chip, pl.ds(r0, r1 - r0), cols]

    def block(self, plane, core):
        if self.half is None:
            return self.full.at[pl.ds(4 * plane, 4), core]
        cols = pl.ds(pl.multiple_of(core * self.half, 128), self.half)
        return self.full.at[pl.ds(4 * plane, 4), :, cols]

    def cut(self, back):
        if self.rows == 96:
            return 48
        return 32 if back % 2 == 0 else 16

    def copy(self, src, dst, index, dev):
        c = remote(src, dst, self.send.at[index], self.recv.at[index], dev)
        return c

    def start(self, src, dst, index, dev):
        c = self.copy(src, dst, index, dev)
        c.start()
        self.started.append(c)

    def chip(self, back, spot):
        return 4 * self.p.plane(back) + spot

    def along_z(self):
        p = self.p
        mine = self.view(self.chip(0, p.spot))
        c = pltpu.make_async_copy(self.own, mine, self.local)
        c.start()
        self.own_copy = c
        for k in range(1, PLANES):
            self.start(self.own, mine, k - 1, (p.ahead(k), p.f))

    def to_neighbours(self, back):
        p = self.p
        piece = self.view(self.chip(back, p.spot))
        if back:
            self.copy(piece, piece, back - 1, (p.z, p.f)).wait_recv()
        src = piece if back else self.own
        self.start(src, piece, 3 + back, (p.z, p.xn))
        self.start(src, piece, 7 + back, (p.z, p.yn))

    def to_diagonal(self, back):
        p, cut = self.p, self.cut(back)
        cx, cy = self.chip(back, p.spot_x), self.chip(back, p.spot_y)
        full_x, full_y = self.view(cx), self.view(cy)
        self.copy(full_x, full_x, 3 + back, (p.z, p.xn)).wait_recv()
        part = self.view(cx, 0, cut)
        self.start(part, part, 11 + back, (p.z, p.yn))
        self.copy(full_y, full_y, 7 + back, (p.z, p.yn)).wait_recv()
        part = self.view(cy, cut, self.rows)
        self.start(part, part, 15 + back, (p.z, p.xn))

    def to_core(self, back):
        p, cut = self.p, self.cut(back)
        cd = self.chip(back, p.spot_d)
        a, b = self.view(cd, 0, cut), self.view(cd, cut, self.rows)
        self.copy(a, a, 11 + back, (p.z, p.yn)).wait_recv()
        self.copy(b, b, 15 + back, (p.z, p.xn)).wait_recv()
        if back == 0:
            self.own_copy.wait()
        blk = self.block(p.plane(back), p.core)
        self.start(blk, blk, 19 + back, (p.z, p.sib))

    def finish(self):
        p = self.p
        for back in range(PLANES):
            blk = self.block(p.plane(back), 1 - p.core)
            self.copy(blk, blk, 19 + back, (p.z, p.sib)).wait_recv()

    def drain(self):
        for c in self.started:
            c.wait_send()


def build_own(place, shard, land, own):
    half = own.shape[1]
    first = place.core == 0
    for c0 in range(0, half, 128):
        mine = shard[:, pl.ds(pl.multiple_of(place.core * half + c0, 128), 128)]
        other = land[:, c0 : c0 + 128]
        top = jnp.where(first, mine, other)
        bottom = jnp.where(first, other, mine)
        own[:, c0 : c0 + 128] = jnp.concatenate([top, bottom], axis=0).astype(own.dtype)


class Pair:
    def __init__(self, place, shard, land, own, send, recv):
        half = own.shape[1]
        src = shard.at[:, pl.ds(pl.multiple_of((1 - place.core) * half, 128), half)]
        self.c = remote(src, land, send, recv, (place.z, place.sib))
        self.args = (place, shard, land, own)

    def start(self):
        self.c.start()

    def done(self):
        self.c.wait()
        build_own(*self.args)


def gather_steps(groups, pairs):
    g0, g1, g2 = groups
    steps = []

    def begin():
        for pr in pairs:
            pr.start()
        pairs[0].done()
        g0.along_z()
        g0.to_neighbours(0)
        pairs[1].done()
        g1.along_z()

    steps.append(begin)
    for k in (1, 2, 3):
        steps.append(functools.partial(g0.to_neighbours, k))
    steps.append(functools.partial(g1.to_neighbours, 0))
    steps.append(g2.along_z)
    for k in range(4):
        steps.append(functools.partial(g0.to_diagonal, k))
    for k in (1, 2, 3):
        steps.append(functools.partial(g1.to_neighbours, k))
    for k in range(4):
        steps.append(functools.partial(g0.to_core, k))
    steps.append(functools.partial(g2.to_neighbours, 0))
    steps.append(g0.finish)
    for k in range(4):
        steps.append(functools.partial(g1.to_diagonal, k))
    for k in (1, 2, 3):
        steps.append(functools.partial(g2.to_neighbours, k))
    for k in range(4):
        steps.append(functools.partial(g1.to_core, k))
    for k in range(4):
        steps.append(functools.partial(g2.to_diagonal, k))
    for k in range(4):
        steps.append(functools.partial(g2.to_core, k))
    steps.append(g1.finish)
    steps.append(g2.finish)
    for g in groups:
        steps.append(g.drain)
    return steps


def gather_kernel(s0, s1, s2, w0, w1, w2, land0, land1, own0, own1, pair_sem, local, send, recv):
    place = Place()
    place.barrier()
    pairs = [
        Pair(place, s0, land0, own0, pair_sem.at[0], pair_sem.at[1]),
        Pair(place, s1, land1, own1, pair_sem.at[2], pair_sem.at[3]),
    ]
    groups = [
        Gather(place, w0, own0, send.at[0], recv.at[0], local.at[0], w0.shape[2]),
        Gather(place, w1, own1, send.at[1], recv.at[1], local.at[1], w1.shape[2]),
        Gather(place, w2, s2, send.at[2], recv.at[2], local.at[2]),
    ]
    for step in gather_steps(groups, pairs):
        step()


def gather_all(s0, s1, s2):
    n0, n1 = s0.shape[1], s1.shape[1]
    bf = jnp.bfloat16
    return pl.pallas_call(
        gather_kernel,
        out_shape=(
            jax.ShapeDtypeStruct((CHIPS, 48, n0), bf),
            jax.ShapeDtypeStruct((CHIPS, 48, n1), bf),
            jax.ShapeDtypeStruct((CHIPS, 2, 96, s2.shape[1]), bf),
        ),
        in_specs=[VMEM] * 3,
        out_specs=[ANY] * 3,
        scratch_shapes=[
            pltpu.VMEM((24, n0 // 2), jnp.float32),
            pltpu.VMEM((24, n1 // 2), jnp.float32),
            pltpu.VMEM((48, n0 // 2), bf),
            pltpu.VMEM((48, n1 // 2), bf),
            pltpu.SemaphoreType.DMA((4,)),
            pltpu.SemaphoreType.DMA((3,)),
            pltpu.SemaphoreType.DMA((3, Gather.SEMS)),
            pltpu.SemaphoreType.DMA((3, Gather.SEMS)),
        ],
        compiler_params=pltpu.CompilerParams(
            collective_id=0, has_side_effects=True, vmem_limit_bytes=56 * 2**20
        ),
    )(s0, s1, s2)


class Scatter:
    SEMS = 4 + 4 + 4 + 4 + 4 + 3 + 1

    def __init__(self, place, full, bufs, out, send, recv, local, width=None):
        self.p, self.full, self.out = place, full, out
        self.sums, self.from_core, self.la, self.lb, self.lx, self.ly, self.lz = bufs[:7]
        if width is not None:
            self.total, self.last = bufs[7:]
        self.send, self.recv, self.local = send, recv, local
        self.half = None if width is None else width // 2
        self.rows = self.sums.shape[1]
        self.started = []

    @staticmethod
    def scratch(rows, cols, two_rows):
        bf = jnp.bfloat16
        shapes = [
            pltpu.VMEM((CHIPS, rows, cols), bf),
            pltpu.VMEM((CHIPS, rows, cols), bf),
            pltpu.VMEM((4, rows - 16, cols), bf),
            pltpu.VMEM((4, rows - 16, cols), bf),
            pltpu.VMEM((4, rows, cols), bf),
            pltpu.VMEM((4, rows, cols), bf),
            pltpu.VMEM((3, rows, cols), bf),
        ]
        if two_rows:
            shapes += [pltpu.VMEM((rows, cols), jnp.float32), pltpu.VMEM((rows // 2, cols), jnp.float32)]
        return shapes

    cut = Gather.cut
    chip = Gather.chip
    copy = Gather.copy
    start = Gather.start
    drain = Gather.drain
    block = Gather.block

    def from_sibling(self, back):
        p = self.p
        blk = pl.ds(4 * p.plane(back), 4)
        c = pltpu.make_async_copy(self.block(p.plane(back), p.core), self.sums.at[blk], self.local.at[back])
        c.start()
        self.start(self.block(p.plane(back), 1 - p.core), self.from_core.at[blk], back, (p.z, p.sib))

    def to_diagonal(self, back):
        p, cut, rows = self.p, self.cut(back), self.rows
        blk = pl.ds(4 * p.plane(back), 4)
        pltpu.make_async_copy(self.block(p.plane(back), p.core), self.sums.at[blk], self.local.at[back]).wait()
        self.copy(self.from_core.at[blk], self.from_core.at[blk], back, (p.z, p.sib)).wait_recv()
        for j in range(4):
            at = 4 * p.plane(back) + j
            self.sums[at] = self.sums[at] + self.from_core[at]
        cd = self.chip(back, p.spot_d)
        self.start(self.sums.at[cd, pl.ds(0, cut)], self.la.at[back, pl.ds(0, cut)], 4 + back, (p.z, p.xn))
        self.start(self.sums.at[cd, pl.ds(cut, rows - cut)], self.lb.at[back, pl.ds(0, rows - cut)], 8 + back, (p.z, p.yn))

    def to_neighbours(self, back):
        p, cut, rows = self.p, self.cut(back), self.rows
        cx, cy = self.chip(back, p.spot_x), self.chip(back, p.spot_y)
        a, b = self.la.at[back, pl.ds(0, cut)], self.lb.at[back, pl.ds(0, rows - cut)]
        self.copy(a, a, 4 + back, (p.z, p.xn)).wait_recv()
        self.sums[cy, 0:cut] = self.sums[cy, 0:cut] + a[...]
        self.start(self.sums.at[cy], self.ly.at[back], 16 + back, (p.z, p.yn))
        self.copy(b, b, 8 + back, (p.z, p.yn)).wait_recv()
        self.sums[cx, cut:rows] = self.sums[cx, cut:rows] + b[...]
        self.start(self.sums.at[cx], self.lx.at[back], 12 + back, (p.z, p.xn))

    def along_z(self, back):
        p = self.p
        c0 = self.chip(back, p.spot)
        lx, ly = self.lx.at[back], self.ly.at[back]
        self.copy(lx, lx, 12 + back, (p.z, p.xn)).wait_recv()
        self.copy(ly, ly, 16 + back, (p.z, p.yn)).wait_recv()
        f = jnp.float32
        got = self.sums[c0].astype(f) + lx[...].astype(f) + ly[...].astype(f)
        self.sums[c0] = got.astype(jnp.bfloat16)
        if back:
            self.start(self.sums.at[c0], self.lz.at[back - 1], 20 + back - 1, (p.plane(back), p.f))

    def owner(self):
        p = self.p
        f = jnp.float32
        for k in range(3):
            self.copy(self.lz.at[k], self.lz.at[k], 20 + k, (p.z, p.f)).wait_recv()
        c0 = self.chip(0, p.spot)
        total = self.sums[c0].astype(f)
        for k in range(3):
            total = total + self.lz[k].astype(f)
        if self.half is None:
            self.out[...] = total
            return
        self.total[...] = total
        rows = self.rows // 2
        theirs = pl.ds(pl.multiple_of((1 - p.core) * rows, 8), rows)
        self.start(self.total.at[theirs], self.last, 23, (p.z, p.sib))

    def finish(self):
        if self.half is None:
            return
        p, half = self.p, self.half
        rows = self.rows // 2
        self.copy(self.last, self.last, 23, (p.z, p.sib)).wait_recv()
        mine = pl.ds(pl.multiple_of(p.core * rows, 8), rows)
        self.out[:, pl.ds(pl.multiple_of(p.core * half, 128), half)] = self.total[mine]
        self.out[:, pl.ds(pl.multiple_of((1 - p.core) * half, 128), half)] = self.last[...]


def scatter_steps(groups):
    stages = [[], [], [], [], []]
    seq = []
    for i, g in enumerate(groups):
        for s, fn in enumerate((g.from_sibling, g.to_diagonal, g.to_neighbours, g.along_z)):
            for k in (3, 2, 1, 0):
                seq.append((i + s, i, s, functools.partial(fn, k)))
        seq.append((i + 4, i, 4, g.owner))
        seq.append((i + 5, i, 5, g.finish))
    seq.sort(key=lambda t: (t[0], -t[2] if t[2] < 1 else 0, t[1]))
    steps = [t[3] for t in seq]
    for g in groups:
        steps.append(g.drain)
    return steps


def scatter_kernel(kinds, *refs):
    n = len(kinds)
    fulls, outs, rest = refs[:n], refs[n : 2 * n], list(refs[2 * n :])
    local, send, recv = rest[-3:]
    place = Place()
    place.barrier()
    groups, at = [], 0
    for i, width in enumerate(kinds):
        count = 7 if width is None else 9
        groups.append(Scatter(place, fulls[i], rest[at : at + count], outs[i], send.at[i], recv.at[i], local.at[i], width))
        at += count
    for step in scatter_steps(groups):
        step()


def scatter_all(grads, cid):
    kinds, outs, scratch = [], [], []
    for g in grads:
        if g.ndim == 3:
            kinds.append(g.shape[2])
            outs.append(jax.ShapeDtypeStruct((24, g.shape[2]), jnp.float32))
            scratch += Scatter.scratch(48, g.shape[2] // 2, True)
        else:
            kinds.append(None)
            outs.append(jax.ShapeDtypeStruct((96, g.shape[3]), jnp.float32))
            scratch += Scatter.scratch(96, g.shape[3], False)
    n = len(kinds)
    return pl.pallas_call(
        functools.partial(scatter_kernel, tuple(kinds)),
        out_shape=tuple(outs),
        in_specs=[ANY] * n,
        out_specs=tuple([VMEM] * n),
        scratch_shapes=scratch
        + [pltpu.SemaphoreType.DMA((n, 4)), pltpu.SemaphoreType.DMA((n, Scatter.SEMS)), pltpu.SemaphoreType.DMA((n, Scatter.SEMS))],
        compiler_params=pltpu.CompilerParams(
            collective_id=cid, has_side_effects=True, vmem_limit_bytes=56 * 2**20
        ),
    )(*grads)


HEADS = 12
HEAD_DIM = 64


norm_eps = 1e-05
masked_score = -1000000000.0
half_root = 0.7071067811865476
density_scale = 0.3989422804014327


def norm_parts(values_in):
    centred = values_in - jnp.mean(values_in, axis=-1, keepdims=True)
    inverse = lax.rsqrt(jnp.mean(centred * centred, axis=-1, keepdims=True) + norm_eps)
    return (centred * inverse, inverse)


def norm_back(grad_hat, normed_hat, inverse):
    return inverse * (
        grad_hat
        - jnp.mean(grad_hat, axis=-1, keepdims=True)
        - normed_hat * jnp.mean(grad_hat * normed_hat, axis=-1, keepdims=True)
    )


def gelu_slope(pre_act):
    return (
        0.5 * (1.0 + lax.erf(pre_act * half_root))
        + pre_act * jnp.exp(-0.5 * pre_act * pre_act) * density_scale
    )


def apply_weight(left_rows, weight_mat):
    return jnp.einsum("bsd,de->bse", left_rows, weight_mat, preferred_element_type=jnp.float32)


def apply_transposed(left_rows, weight_mat):
    return jnp.einsum("bse,de->bsd", left_rows, weight_mat, preferred_element_type=jnp.float32)


def weight_grad(left_rows, right_rows):
    return jnp.einsum("bsd,bse->de", left_rows, right_rows, preferred_element_type=jnp.float32)


def column_sum(rows_low):
    return jnp.sum(rows_low, axis=(0, 1), dtype=jnp.float32)


def split_heads(rows_in):
    return rows_in.reshape(rows_in.shape[0], HEADS, HEAD_DIM)


def score_block(query_rows, key_rows, valid_keys):
    scores = jnp.einsum(
        "qhd,khd->hqk",
        split_heads(query_rows),
        split_heads(key_rows),
        preferred_element_type=jnp.float32,
    ) * HEAD_DIM ** (-0.5)
    return jnp.where(valid_keys[None, None, :], scores, masked_score)


def attend_forward(packed):
    query_rows, key_rows, value_rows, valid_keys = packed
    scores = score_block(query_rows, key_rows, valid_keys)
    row_top = jnp.max(scores, axis=-1, keepdims=True)
    expo = jnp.exp(scores - row_top)
    total = jnp.sum(expo, axis=-1, keepdims=True)
    probs_low = (expo / total).astype(jnp.bfloat16)
    mixed = jnp.einsum(
        "hqk,khd->qhd", probs_low, split_heads(value_rows), preferred_element_type=jnp.float32
    )
    return (mixed.reshape(query_rows.shape[0], HEADS * HEAD_DIM), row_top + jnp.log(total))


def attend_backward(packed):
    query_rows, key_rows, value_rows, valid_keys, log_total, grad_mixed = packed
    slot_count = query_rows.shape[0]
    scores = score_block(query_rows, key_rows, valid_keys)
    probs = jnp.exp(scores - log_total)
    grad_heads = split_heads(grad_mixed)
    grad_probs = jnp.einsum(
        "qhd,khd->hqk", grad_heads, split_heads(value_rows), preferred_element_type=jnp.float32
    )
    grad_value = jnp.einsum(
        "hqk,qhd->khd", probs.astype(jnp.bfloat16), grad_heads, preferred_element_type=jnp.float32
    )
    grad_scores = probs * (grad_probs - jnp.sum(probs * grad_probs, axis=-1, keepdims=True))
    grad_scores_low = grad_scores.astype(jnp.bfloat16)
    grad_query = jnp.einsum(
        "hqk,khd->qhd", grad_scores_low, split_heads(key_rows), preferred_element_type=jnp.float32
    ) * HEAD_DIM ** (-0.5)
    grad_key = jnp.einsum(
        "hqk,qhd->khd", grad_scores_low, split_heads(query_rows), preferred_element_type=jnp.float32
    ) * HEAD_DIM ** (-0.5)
    width = HEADS * HEAD_DIM
    return (
        grad_query.reshape(slot_count, width).astype(jnp.bfloat16),
        grad_key.reshape(slot_count, width).astype(jnp.bfloat16),
        grad_value.reshape(slot_count, width).astype(jnp.bfloat16),
    )


def own_kernels(shard_rows):
    return lax.axis_size("dp") == PLANES and lax.axis_size("fsdp") == 8 and shard_rows == 24


def gather_params(qkv, rest, outer, vectors, inner_bias):
    rows = outer.shape[0] // 4
    columns = [v[:, None] for v in vectors] + [inner_bias.reshape(rows, 4)]
    pad = jnp.zeros((rows, 256 - len(vectors) - 4), jnp.bfloat16)
    s0 = jnp.concatenate(list(qkv) + columns + [pad], axis=1)
    s1 = jnp.concatenate(list(rest), axis=1)
    if own_kernels(rows):
        w0, w1, w2 = gather_all(s0.astype(jnp.float32), s1.astype(jnp.float32), outer)
    else:
        w0, w1, w2 = (lax.all_gather(s, ("dp", "fsdp"), axis=0, tiled=True) for s in (s0, s1, outer))
    width = outer.shape[1]
    w0, w1, w2 = w0.reshape(width, -1), w1.reshape(width, -1), w2.reshape(-1, width)
    vec = w0[:, 3 * width :]
    return (
        *(w0[:, i * width : (i + 1) * width] for i in range(3)),
        w1[:, :width],
        w1[:, width:],
        w2,
        *(vec[:, i] for i in range(8)),
        vec[:, 8:12].reshape(-1),
    )


def scatter_grads(qkv, rest, outer, vectors, inner_bias):
    width = outer.shape[1]
    columns = [v[:, None] for v in vectors] + [inner_bias.reshape(width, 4)]
    pad = jnp.zeros((width, 256 - len(vectors) - 4), jnp.float32)
    g0 = jnp.concatenate(list(qkv) + columns + [pad], axis=1)
    g1 = jnp.concatenate(list(rest), axis=1)
    devices = lax.axis_size("dp") * lax.axis_size("fsdp")
    if own_kernels(width // devices):
        low = jnp.bfloat16
        o2, o1, o0 = scatter_all(
            (
                outer.astype(low).reshape(CHIPS, 2, 96, width),
                g1.astype(low).reshape(CHIPS, 48, -1),
                g0.astype(low).reshape(CHIPS, 48, -1),
            ),
            1,
        )
    else:
        o2, o1, o0 = (
            lax.psum_scatter(g, ("dp", "fsdp"), scatter_dimension=0, tiled=True) for g in (outer, g1, g0)
        )
    vec = o0[:, 3 * width :]
    return (
        o0[:, :width],
        vec[:, 0],
        o0[:, width : 2 * width],
        o0[:, 2 * width : 3 * width],
        vec[:, 1],
        o1[:, :width],
        vec[:, 2],
        vec[:, 3],
        vec[:, 4],
        o1[:, width:],
        vec[:, 8:12].reshape(-1),
        o2,
        vec[:, 5],
        vec[:, 6],
        vec[:, 7],
    )


def shards(
    tokens,
    cotangent,
    seg_lengths,
    alignment,
    query_weight,
    query_bias,
    key_weight,
    value_weight,
    value_bias,
    out_weight,
    out_bias,
    first_gain,
    first_shift,
    inner_weight,
    inner_bias,
    outer_weight,
    outer_bias,
    second_gain,
    second_shift,
):
    w_all = gather_params(
        (query_weight, key_weight, value_weight), (out_weight, inner_weight), outer_weight,
        (query_bias, value_bias, out_bias, first_gain, first_shift, outer_bias, second_gain, second_shift),
        inner_bias,
    )
    (
        w_query,
        w_key,
        w_value,
        w_out,
        w_inner,
        w_outer,
        b_query,
        b_value,
        b_out,
        g_first,
        s_first,
        b_outer,
        g_second,
        s_second,
        b_inner,
    ) = w_all
    back_query, back_key, back_value, back_out = w_query, w_key, w_value, w_out
    back_first, back_inner, back_outer, back_second = g_first, w_inner, w_outer, g_second
    text_count = alignment.shape[1]
    slot_count = tokens.shape[1]
    seg_count = slot_count - text_count
    member = alignment[:, None, :] == jnp.arange(seg_count, dtype=jnp.int32)[None, :, None]
    member_float = member.astype(jnp.float32)
    counts = jnp.maximum(jnp.sum(member_float, axis=-1), 1.0)
    pooled = (
        jnp.einsum(
            "bst,btd->bsd",
            member.astype(jnp.bfloat16),
            tokens[:, :text_count],
            preferred_element_type=jnp.float32,
        )
        / counts[:, :, None]
    )
    text_zeros = jnp.zeros((tokens.shape[0], text_count, tokens.shape[2]), jnp.float32)
    base = tokens.astype(jnp.float32) + jnp.concatenate([text_zeros, pooled], axis=1)
    valid_keys = (
        jnp.arange(slot_count, dtype=jnp.int32)[None, :] < text_count + seg_lengths[:, None]
    )
    base_low = base.astype(jnp.bfloat16)
    query_rows = (apply_weight(base_low, w_query) + b_query).astype(jnp.bfloat16)
    key_rows = apply_weight(base_low, w_key).astype(jnp.bfloat16)
    value_rows = (apply_weight(base_low, w_value) + b_value).astype(jnp.bfloat16)
    attended, log_total = lax.map(attend_forward, (query_rows, key_rows, value_rows, valid_keys))
    attended_low = attended.astype(jnp.bfloat16)
    first_sum = base + apply_weight(attended_low, w_out) + b_out
    first_hat, first_inv = norm_parts(first_sum)
    normed = first_hat * g_first + s_first
    normed_low = normed.astype(jnp.bfloat16)
    pre_act = apply_weight(normed_low, w_inner) + b_inner
    act_low = jax.nn.gelu(pre_act, approximate=False).astype(jnp.bfloat16)
    second_sum = normed + apply_weight(act_low, w_outer) + b_outer
    second_hat, second_inv = norm_parts(second_sum)
    encoded = (second_hat * g_second + s_second).astype(jnp.bfloat16)
    grad_y = cotangent.astype(jnp.float32)
    grad_second_gain = jnp.sum(grad_y * second_hat, axis=(0, 1))
    grad_second_shift = jnp.sum(grad_y, axis=(0, 1))
    grad_second = norm_back(grad_y * back_second, second_hat, second_inv)
    grad_mlp_low = grad_second.astype(jnp.bfloat16)
    grad_outer_weight = weight_grad(act_low, grad_mlp_low)
    grad_outer_bias = column_sum(grad_mlp_low)
    grad_pre_low = (apply_transposed(grad_mlp_low, back_outer) * gelu_slope(pre_act)).astype(
        jnp.bfloat16
    )
    grad_inner_weight = weight_grad(normed_low, grad_pre_low)
    grad_inner_bias = column_sum(grad_pre_low)
    grad_normed = grad_second + apply_transposed(grad_pre_low, back_inner)
    grad_first_gain = jnp.sum(grad_normed * first_hat, axis=(0, 1))
    grad_first_shift = jnp.sum(grad_normed, axis=(0, 1))
    grad_first = norm_back(grad_normed * back_first, first_hat, first_inv)
    grad_branch_low = grad_first.astype(jnp.bfloat16)
    grad_out_weight = weight_grad(attended_low, grad_branch_low)
    grad_out_bias = column_sum(grad_branch_low)
    grad_attended_low = apply_transposed(grad_branch_low, back_out).astype(jnp.bfloat16)
    grad_query, grad_key, grad_value = lax.map(
        attend_backward,
        (query_rows, key_rows, value_rows, valid_keys, log_total, grad_attended_low),
    )
    grad_query_weight = weight_grad(base_low, grad_query)
    grad_query_bias = column_sum(grad_query)
    grad_key_weight = weight_grad(base_low, grad_key)
    grad_value_weight = weight_grad(base_low, grad_value)
    grad_value_bias = column_sum(grad_value)
    grad_base = (
        grad_first
        + apply_transposed(grad_query, back_query)
        + apply_transposed(grad_key, back_key)
        + apply_transposed(grad_value, back_value)
    )
    spread_back = jnp.einsum(
        "bst,bsd->btd",
        member_float,
        grad_base[:, text_count:] / counts[:, :, None],
        precision=lax.Precision.HIGHEST,
    )
    grad_tokens = jnp.concatenate(
        [grad_base[:, :text_count] + spread_back, grad_base[:, text_count:]], axis=1
    ).astype(jnp.bfloat16)
    owned = scatter_grads(
        (grad_query_weight, grad_key_weight, grad_value_weight),
        (grad_out_weight, grad_inner_weight),
        grad_outer_weight,
        (grad_query_bias, grad_value_bias, grad_out_bias, grad_first_gain, grad_first_shift, grad_outer_bias,
         grad_second_gain, grad_second_shift),
        grad_inner_bias,
    )
    return (
        encoded,
        grad_tokens,
        owned[0],
        owned[1],
        owned[2],
        owned[3],
        owned[4],
        owned[5],
        owned[6],
        owned[7],
        owned[8],
        owned[9],
        owned[10],
        owned[11],
        owned[12],
        owned[13],
        owned[14],
    )


def solution(mesh):
    in_specs = (
        P(("dp", "fsdp"), None, None),
        P(("dp", "fsdp"), None, None),
        P(("dp", "fsdp")),
        P(("dp", "fsdp"), None),
        P(("dp", "fsdp"), None),
        P(("dp", "fsdp")),
        P(("dp", "fsdp"), None),
        P(("dp", "fsdp"), None),
        P(("dp", "fsdp")),
        P(("dp", "fsdp"), None),
        P(("dp", "fsdp")),
        P(("dp", "fsdp")),
        P(("dp", "fsdp")),
        P(("dp", "fsdp"), None),
        P(("dp", "fsdp")),
        P(("dp", "fsdp"), None),
        P(("dp", "fsdp")),
        P(("dp", "fsdp")),
        P(("dp", "fsdp")),
    )
    out_specs = (
        P(("dp", "fsdp"), None, None),
        P(("dp", "fsdp"), None, None),
        P(("dp", "fsdp"), None),
        P(("dp", "fsdp")),
        P(("dp", "fsdp"), None),
        P(("dp", "fsdp"), None),
        P(("dp", "fsdp")),
        P(("dp", "fsdp"), None),
        P(("dp", "fsdp")),
        P(("dp", "fsdp")),
        P(("dp", "fsdp")),
        P(("dp", "fsdp"), None),
        P(("dp", "fsdp")),
        P(("dp", "fsdp"), None),
        P(("dp", "fsdp")),
        P(("dp", "fsdp")),
        P(("dp", "fsdp")),
    )
    return jax.shard_map(shards, mesh=mesh, in_specs=in_specs, out_specs=out_specs, check_vma=False)
```

```python
import functools
import jax
import jax.numpy as jnp
from jax import lax
from jax.experimental import pallas as pl
from jax.experimental.pallas import tpu as pltpu
from jax.sharding import PartitionSpec as P

MESH = pl.DeviceIdType.MESH
ANY = pl.BlockSpec(memory_space=pl.ANY)
VMEM = pl.BlockSpec(memory_space=pltpu.VMEM)
PLANES = 4
CHIPS = 16


class Place:
    def __init__(self):
        self.z = lax.axis_index("dp")
        self.f = lax.axis_index("fsdp")
        self.core = self.f % 2
        self.x = (self.f // 2) % 2
        self.y = self.f // 4
        self.sib = self.f + 1 - 2 * self.core
        self.xn = self.f + 2 - 4 * self.x
        self.yn = self.f + 4 - 8 * self.y
        self.spot = self.f // 2
        self.spot_x = self.xn // 2
        self.spot_y = self.yn // 2
        self.spot_d = 3 - self.spot

    def plane(self, back):
        return (self.z + PLANES - back) % PLANES

    def ahead(self, step):
        return (self.z + step) % PLANES

    def barrier(self):
        bar = pltpu.get_barrier_semaphore()
        for other in self.partners():
            pl.semaphore_signal(bar, inc=1, device_id=other, device_id_type=MESH)
        pl.semaphore_wait(bar, 3 + PLANES - 1)

    def partners(self):
        return [(self.z, self.sib), (self.z, self.xn), (self.z, self.yn)] + [
            (self.ahead(k), self.f) for k in range(1, PLANES)
        ]


def remote(src, dst, send, recv, dev):
    return pltpu.make_async_remote_copy(
        src_ref=src, dst_ref=dst, send_sem=send, recv_sem=recv, device_id=dev, device_id_type=MESH
    )


class Gather:
    SEMS = 3 + 4 + 4 + 4 + 4 + 4

    def __init__(self, place, full, own, send, recv, local, width=None):
        self.p, self.full, self.own = place, full, own
        self.send, self.recv, self.local = send, recv, local
        self.half = None if width is None else width // 2
        self.rows = own.shape[0]
        self.started = []

    def view(self, chip, r0=0, r1=None, core=None):
        core = self.p.core if core is None else core
        r1 = self.rows if r1 is None else r1
        if self.half is None:
            return self.full.at[chip, core, pl.ds(r0, r1 - r0), :]
        cols = pl.ds(pl.multiple_of(core * self.half, 128), self.half)
        return self.full.at[chip, pl.ds(r0, r1 - r0), cols]

    def block(self, plane, core):
        if self.half is None:
            return self.full.at[pl.ds(4 * plane, 4), core]
        cols = pl.ds(pl.multiple_of(core * self.half, 128), self.half)
        return self.full.at[pl.ds(4 * plane, 4), :, cols]

    def cut(self, back):
        if self.rows == 96:
            return 48
        return 32 if back % 2 == 0 else 16

    def copy(self, src, dst, index, dev):
        c = remote(src, dst, self.send.at[index], self.recv.at[index], dev)
        return c

    def start(self, src, dst, index, dev):
        c = self.copy(src, dst, index, dev)
        c.start()
        self.started.append(c)

    def chip(self, back, spot):
        return 4 * self.p.plane(back) + spot

    def along_z(self):
        p = self.p
        mine = self.view(self.chip(0, p.spot))
        c = pltpu.make_async_copy(self.own, mine, self.local)
        c.start()
        self.own_copy = c
        for k in range(1, PLANES):
            self.start(self.own, mine, k - 1, (p.ahead(k), p.f))

    def to_neighbours(self, back):
        p = self.p
        piece = self.view(self.chip(back, p.spot))
        if back:
            self.copy(piece, piece, back - 1, (p.z, p.f)).wait_recv()
        src = piece if back else self.own
        self.start(src, piece, 3 + back, (p.z, p.xn))
        self.start(src, piece, 7 + back, (p.z, p.yn))

    def to_diagonal(self, back):
        p, cut = self.p, self.cut(back)
        cx, cy = self.chip(back, p.spot_x), self.chip(back, p.spot_y)
        full_x, full_y = self.view(cx), self.view(cy)
        self.copy(full_x, full_x, 3 + back, (p.z, p.xn)).wait_recv()
        part = self.view(cx, 0, cut)
        self.start(part, part, 11 + back, (p.z, p.yn))
        self.copy(full_y, full_y, 7 + back, (p.z, p.yn)).wait_recv()
        part = self.view(cy, cut, self.rows)
        self.start(part, part, 15 + back, (p.z, p.xn))

    def to_core(self, back):
        p, cut = self.p, self.cut(back)
        cd = self.chip(back, p.spot_d)
        a, b = self.view(cd, 0, cut), self.view(cd, cut, self.rows)
        self.copy(a, a, 11 + back, (p.z, p.yn)).wait_recv()
        self.copy(b, b, 15 + back, (p.z, p.xn)).wait_recv()
        if back == 0:
            self.own_copy.wait()
        blk = self.block(p.plane(back), p.core)
        self.start(blk, blk, 19 + back, (p.z, p.sib))

    def finish(self):
        p = self.p
        for back in range(PLANES):
            blk = self.block(p.plane(back), 1 - p.core)
            self.copy(blk, blk, 19 + back, (p.z, p.sib)).wait_recv()

    def drain(self):
        for c in self.started:
            c.wait_send()


def build_own(place, shard, land, own):
    half = own.shape[1]
    first = place.core == 0
    for c0 in range(0, half, 128):
        mine = shard[:, pl.ds(pl.multiple_of(place.core * half + c0, 128), 128)]
        other = land[:, c0 : c0 + 128]
        top = jnp.where(first, mine, other)
        bottom = jnp.where(first, other, mine)
        own[:, c0 : c0 + 128] = jnp.concatenate([top, bottom], axis=0).astype(own.dtype)


class Pair:
    def __init__(self, place, shard, land, own, send, recv):
        half = own.shape[1]
        src = shard.at[:, pl.ds(pl.multiple_of((1 - place.core) * half, 128), half)]
        self.c = remote(src, land, send, recv, (place.z, place.sib))
        self.args = (place, shard, land, own)

    def start(self):
        self.c.start()

    def done(self):
        self.c.wait()
        build_own(*self.args)


def gather_steps(groups, pairs):
    g0, g1, g2 = groups
    steps = []

    def begin():
        for pr in pairs:
            pr.start()
        pairs[0].done()
        g0.along_z()
        g0.to_neighbours(0)
        pairs[1].done()
        g1.along_z()

    steps.append(begin)
    for k in (1, 2, 3):
        steps.append(functools.partial(g0.to_neighbours, k))
    steps.append(functools.partial(g1.to_neighbours, 0))
    steps.append(g2.along_z)
    for k in range(4):
        steps.append(functools.partial(g0.to_diagonal, k))
    for k in (1, 2, 3):
        steps.append(functools.partial(g1.to_neighbours, k))
    for k in range(4):
        steps.append(functools.partial(g0.to_core, k))
    steps.append(functools.partial(g2.to_neighbours, 0))
    steps.append(g0.finish)
    for k in range(4):
        steps.append(functools.partial(g1.to_diagonal, k))
    for k in (1, 2, 3):
        steps.append(functools.partial(g2.to_neighbours, k))
    for k in range(4):
        steps.append(functools.partial(g1.to_core, k))
    for k in range(4):
        steps.append(functools.partial(g2.to_diagonal, k))
    for k in range(4):
        steps.append(functools.partial(g2.to_core, k))
    steps.append(g1.finish)
    steps.append(g2.finish)
    for g in groups:
        steps.append(g.drain)
    return steps


def gather_kernel(s0, s1, s2, w0, w1, w2, land0, land1, own0, own1, pair_sem, local, send, recv):
    place = Place()
    place.barrier()
    pairs = [
        Pair(place, s0, land0, own0, pair_sem.at[0], pair_sem.at[1]),
        Pair(place, s1, land1, own1, pair_sem.at[2], pair_sem.at[3]),
    ]
    groups = [
        Gather(place, w0, own0, send.at[0], recv.at[0], local.at[0], w0.shape[2]),
        Gather(place, w1, own1, send.at[1], recv.at[1], local.at[1], w1.shape[2]),
        Gather(place, w2, s2, send.at[2], recv.at[2], local.at[2]),
    ]
    for step in gather_steps(groups, pairs):
        step()


def gather_all(s0, s1, s2):
    n0, n1 = s0.shape[1], s1.shape[1]
    bf = jnp.bfloat16
    return pl.pallas_call(
        gather_kernel,
        out_shape=(
            jax.ShapeDtypeStruct((CHIPS, 48, n0), bf),
            jax.ShapeDtypeStruct((CHIPS, 48, n1), bf),
            jax.ShapeDtypeStruct((CHIPS, 2, 96, s2.shape[1]), bf),
        ),
        in_specs=[VMEM] * 3,
        out_specs=[ANY] * 3,
        scratch_shapes=[
            pltpu.VMEM((24, n0 // 2), jnp.float32),
            pltpu.VMEM((24, n1 // 2), jnp.float32),
            pltpu.VMEM((48, n0 // 2), bf),
            pltpu.VMEM((48, n1 // 2), bf),
            pltpu.SemaphoreType.DMA((4,)),
            pltpu.SemaphoreType.DMA((3,)),
            pltpu.SemaphoreType.DMA((3, Gather.SEMS)),
            pltpu.SemaphoreType.DMA((3, Gather.SEMS)),
        ],
        compiler_params=pltpu.CompilerParams(
            collective_id=0, has_side_effects=True, vmem_limit_bytes=56 * 2**20
        ),
    )(s0, s1, s2)


class Scatter:
    SEMS = 4 + 4 + 4 + 4 + 4 + 3 + 1

    def __init__(self, place, full, bufs, out, send, recv, local, width=None):
        self.p, self.full, self.out = place, full, out
        self.sums, self.from_core, self.la, self.lb, self.lx, self.ly, self.lz = bufs[:7]
        if width is not None:
            self.total, self.last = bufs[7:]
        self.send, self.recv, self.local = send, recv, local
        self.half = None if width is None else width // 2
        self.rows = self.sums.shape[1]
        self.started = []

    @staticmethod
    def scratch(rows, cols, two_rows):
        bf = jnp.bfloat16
        shapes = [
            pltpu.VMEM((CHIPS, rows, cols), bf),
            pltpu.VMEM((CHIPS, rows, cols), bf),
            pltpu.VMEM((4, rows - 16, cols), bf),
            pltpu.VMEM((4, rows - 16, cols), bf),
            pltpu.VMEM((4, rows, cols), bf),
            pltpu.VMEM((4, rows, cols), bf),
            pltpu.VMEM((3, rows, cols), bf),
        ]
        if two_rows:
            shapes += [pltpu.VMEM((rows, cols), jnp.float32), pltpu.VMEM((rows // 2, cols), jnp.float32)]
        return shapes

    cut = Gather.cut
    chip = Gather.chip
    copy = Gather.copy
    start = Gather.start
    drain = Gather.drain
    block = Gather.block

    def from_sibling(self, back):
        p = self.p
        blk = pl.ds(4 * p.plane(back), 4)
        c = pltpu.make_async_copy(self.block(p.plane(back), p.core), self.sums.at[blk], self.local.at[back])
        c.start()
        self.start(self.block(p.plane(back), 1 - p.core), self.from_core.at[blk], back, (p.z, p.sib))

    def to_diagonal(self, back):
        p, cut, rows = self.p, self.cut(back), self.rows
        blk = pl.ds(4 * p.plane(back), 4)
        pltpu.make_async_copy(self.block(p.plane(back), p.core), self.sums.at[blk], self.local.at[back]).wait()
        self.copy(self.from_core.at[blk], self.from_core.at[blk], back, (p.z, p.sib)).wait_recv()
        for j in range(4):
            at = 4 * p.plane(back) + j
            self.sums[at] = self.sums[at] + self.from_core[at]
        cd = self.chip(back, p.spot_d)
        self.start(self.sums.at[cd, pl.ds(0, cut)], self.la.at[back, pl.ds(0, cut)], 4 + back, (p.z, p.xn))
        self.start(self.sums.at[cd, pl.ds(cut, rows - cut)], self.lb.at[back, pl.ds(0, rows - cut)], 8 + back, (p.z, p.yn))

    def to_neighbours(self, back):
        p, cut, rows = self.p, self.cut(back), self.rows
        cx, cy = self.chip(back, p.spot_x), self.chip(back, p.spot_y)
        a, b = self.la.at[back, pl.ds(0, cut)], self.lb.at[back, pl.ds(0, rows - cut)]
        self.copy(a, a, 4 + back, (p.z, p.xn)).wait_recv()
        self.sums[cy, 0:cut] = self.sums[cy, 0:cut] + a[...]
        self.start(self.sums.at[cy], self.ly.at[back], 16 + back, (p.z, p.yn))
        self.copy(b, b, 8 + back, (p.z, p.yn)).wait_recv()
        self.sums[cx, cut:rows] = self.sums[cx, cut:rows] + b[...]
        self.start(self.sums.at[cx], self.lx.at[back], 12 + back, (p.z, p.xn))

    def along_z(self, back):
        p = self.p
        c0 = self.chip(back, p.spot)
        lx, ly = self.lx.at[back], self.ly.at[back]
        self.copy(lx, lx, 12 + back, (p.z, p.xn)).wait_recv()
        self.copy(ly, ly, 16 + back, (p.z, p.yn)).wait_recv()
        f = jnp.float32
        got = self.sums[c0].astype(f) + lx[...].astype(f) + ly[...].astype(f)
        self.sums[c0] = got.astype(jnp.bfloat16)
        if back:
            self.start(self.sums.at[c0], self.lz.at[back - 1], 20 + back - 1, (p.plane(back), p.f))

    def owner(self):
        p = self.p
        f = jnp.float32
        for k in range(3):
            self.copy(self.lz.at[k], self.lz.at[k], 20 + k, (p.z, p.f)).wait_recv()
        c0 = self.chip(0, p.spot)
        total = self.sums[c0].astype(f)
        for k in range(3):
            total = total + self.lz[k].astype(f)
        if self.half is None:
            self.out[...] = total
            return
        self.total[...] = total
        rows = self.rows // 2
        theirs = pl.ds(pl.multiple_of((1 - p.core) * rows, 8), rows)
        self.start(self.total.at[theirs], self.last, 23, (p.z, p.sib))

    def finish(self):
        if self.half is None:
            return
        p, half = self.p, self.half
        rows = self.rows // 2
        self.copy(self.last, self.last, 23, (p.z, p.sib)).wait_recv()
        mine = pl.ds(pl.multiple_of(p.core * rows, 8), rows)
        self.out[:, pl.ds(pl.multiple_of(p.core * half, 128), half)] = self.total[mine]
        self.out[:, pl.ds(pl.multiple_of((1 - p.core) * half, 128), half)] = self.last[...]


def scatter_steps(groups):
    stages = [[], [], [], [], []]
    seq = []
    for i, g in enumerate(groups):
        for s, fn in enumerate((g.from_sibling, g.to_diagonal, g.to_neighbours, g.along_z)):
            for k in (3, 2, 1, 0):
                seq.append((i + s, i, s, functools.partial(fn, k)))
        seq.append((i + 4, i, 4, g.owner))
        seq.append((i + 5, i, 5, g.finish))
    seq.sort(key=lambda t: (t[0], -t[2] if t[2] < 1 else 0, t[1]))
    steps = [t[3] for t in seq]
    for g in groups:
        steps.append(g.drain)
    return steps


def scatter_kernel(kinds, *refs):
    n = len(kinds)
    fulls, outs, rest = refs[:n], refs[n : 2 * n], list(refs[2 * n :])
    local, send, recv = rest[-3:]
    place = Place()
    place.barrier()
    groups, at = [], 0
    for i, width in enumerate(kinds):
        count = 7 if width is None else 9
        groups.append(Scatter(place, fulls[i], rest[at : at + count], outs[i], send.at[i], recv.at[i], local.at[i], width))
        at += count
    for step in scatter_steps(groups):
        step()


def scatter_all(grads, cid):
    kinds, outs, scratch = [], [], []
    for g in grads:
        if g.ndim == 3:
            kinds.append(g.shape[2])
            outs.append(jax.ShapeDtypeStruct((24, g.shape[2]), jnp.float32))
            scratch += Scatter.scratch(48, g.shape[2] // 2, True)
        else:
            kinds.append(None)
            outs.append(jax.ShapeDtypeStruct((96, g.shape[3]), jnp.float32))
            scratch += Scatter.scratch(96, g.shape[3], False)
    n = len(kinds)
    return pl.pallas_call(
        functools.partial(scatter_kernel, tuple(kinds)),
        out_shape=tuple(outs),
        in_specs=[ANY] * n,
        out_specs=tuple([VMEM] * n),
        scratch_shapes=scratch
        + [pltpu.SemaphoreType.DMA((n, 4)), pltpu.SemaphoreType.DMA((n, Scatter.SEMS)), pltpu.SemaphoreType.DMA((n, Scatter.SEMS))],
        compiler_params=pltpu.CompilerParams(
            collective_id=cid, has_side_effects=True, vmem_limit_bytes=56 * 2**20
        ),
    )(*grads)


F = jnp.float32
BF = jnp.bfloat16
NN = (((1,), (0,)), ((), ()))
NT = (((1,), (1,)), ((), ()))
TN = (((0,), (0,)), ((), ()))
SMEM = pl.BlockSpec(memory_space=pltpu.SMEM)
HEADS = 12
HEAD_DIM = 64
QUAD = 4 * HEAD_DIM
scale = HEAD_DIM**-0.5
norm_eps = 1e-05
masked_score = -1000000000.0
LIMIT = 60 * 2**20


def dot(left, right, dims):
    return lax.dot_general(left, right, dims, preferred_element_type=F)


def once(shape, index):
    return pl.BlockSpec(shape, index, pipeline_mode=pl.Buffered(1))


def key_bias(count):
    row = lax.broadcasted_iota(jnp.int32, (128, 1), 0)
    return jnp.where(row < count, 0.0, masked_score).astype(F)


def masked(scores, text, bias):
    return jnp.concatenate([scores[:text], scores[text:] + bias], axis=0)


def head_lanes(h):
    lane = lax.broadcasted_iota(jnp.int32, (1, 128), 1)
    return (lane < HEAD_DIM) if h == 0 else (lane >= HEAD_DIM)


def pair_forward(q2, k2, v2, text, bias):
    vt = v2.T
    outs, logs = [], []
    for h in range(2):
        qh = jnp.where(head_lanes(h), q2, BF(0))
        scores = masked(dot(k2, qh, NT), text, bias)
        top = jnp.max(scores, axis=0, keepdims=True)
        expo = jnp.exp(scores - top)
        total = jnp.sum(expo, axis=0, keepdims=True)
        outs.append(dot(vt[HEAD_DIM * h : HEAD_DIM * (h + 1)], expo.astype(BF), NN) * (1.0 / total))
        logs.append(top + jnp.log(total))
    return jnp.concatenate(outs, axis=0).T.astype(BF), logs


def pair_backward(q2, k2, v2, o2, do2, logs, text, bias):
    prod = (do2.astype(F) * o2.astype(F)).T
    kt = (k2 * BF(scale)).T
    dq, dk, dv = [], [], []
    for h in range(2):
        rows = slice(HEAD_DIM * h, HEAD_DIM * (h + 1))
        qh = jnp.where(head_lanes(h), q2, BF(0))
        doh = jnp.where(head_lanes(h), do2, BF(0))
        delta = jnp.sum(prod[rows], axis=0, keepdims=True)
        probs = jnp.exp(masked(dot(k2, qh, NT), text, bias) - logs[h])
        grads = (probs * (dot(v2, doh, NT) - delta)).astype(BF)
        dv.append(dot(probs.astype(BF), do2, NN))
        dk.append(dot(grads, q2, NN))
        dq.append(dot(kt[rows], grads, NN))
    first = head_lanes(0)
    return (
        jnp.concatenate(dq, axis=0).T.astype(BF),
        jnp.where(first, dk[0], dk[1]).astype(BF),
        jnp.where(first, dv[0], dv[1]).astype(BF),
    )


def member_of(align, axis, segs):
    shape = (segs, align.shape[1]) if axis == 0 else (align.shape[0], segs)
    return (align == lax.broadcasted_iota(jnp.int32, shape, axis)).astype(F)


def forward_body(b, j, len_ref, tok_ref, al_ref, w_ref, bias_ref, outs, low_s):
    base_ref, low_ref, q_ref, k_ref, v_ref, att_ref, lse_ref = outs
    text, width = al_ref.shape[2], tok_ref.shape[2]
    segs = tok_ref.shape[1] - text

    @pl.when(j == 0)
    def _():
        member = member_of(al_ref[0], 0, segs)
        counts = jnp.maximum(jnp.sum(member, axis=1, keepdims=True), 1.0)
        tok = tok_ref[0]
        pooled = dot(member.astype(BF), tok[:text], NN) / counts
        seg_base = tok[text:].astype(F) + pooled
        base_ref[0, :text] = tok[:text].astype(F)
        base_ref[0, text:] = seg_base
        low_ref[0, :text] = tok[:text]
        low_ref[0, text:] = seg_base.astype(BF)
        low_s[:text] = tok[:text]
        low_s[text:] = seg_base.astype(BF)

    low = low_s[...]
    parts = []
    for i, ref in enumerate((q_ref, k_ref, v_ref)):
        at = i * width + j * QUAD
        rows = dot(low, w_ref[:, pl.ds(pl.multiple_of(at, QUAD), QUAD)], NN)
        if i != 1:
            rows = rows + bias_ref[i // 2 : i // 2 + 1, pl.ds(pl.multiple_of(j * QUAD, QUAD), QUAD)]
        rows = rows.astype(BF)
        if i == 0:
            rows = rows * BF(scale)
        ref[0] = rows
        parts.append(rows)
    bias = key_bias(len_ref[b])
    for pr in range(2):
        cols = slice(128 * pr, 128 * pr + 128)
        out, logs = pair_forward(parts[0][:, cols], parts[1][:, cols], parts[2][:, cols], text, bias)
        att_ref[0, :, cols] = out
        for h in range(2):
            lse_ref[0, 0, 2 * pr + h : 2 * pr + h + 1, :] = logs[h]


def forward_kernel(len_ref, tok_ref, al_ref, w_ref, bias_ref, *rest):
    forward_body(pl.program_id(0), pl.program_id(1), len_ref, tok_ref, al_ref, w_ref, bias_ref, rest[:7], rest[7])


def forward_attention(seg_lengths, tokens, alignment, w0, biases):
    docs, slots, width = tokens.shape
    text = alignment.shape[1]
    quads = width // QUAD
    doc = pl.BlockSpec((1, slots, width), lambda b, j: (b, 0, 0))
    quad = pl.BlockSpec((1, slots, QUAD), lambda b, j: (b, 0, j))
    wide = jax.ShapeDtypeStruct((docs, slots, width), BF)
    return pl.pallas_call(
        forward_kernel,
        grid=(docs, quads),
        in_specs=[
            SMEM,
            doc,
            pl.BlockSpec((1, 1, text), lambda b, j: (b, 0, 0)),
            once(w0.shape, lambda b, j: (0, 0)),
            once(biases.shape, lambda b, j: (0, 0)),
        ],
        out_specs=[doc, doc, quad, quad, quad, quad, pl.BlockSpec((1, 1, 8, slots), lambda b, j: (b, j, 0, 0))],
        out_shape=[
            jax.ShapeDtypeStruct((docs, slots, width), F),
            wide,
            wide,
            wide,
            wide,
            wide,
            jax.ShapeDtypeStruct((docs, quads, 8, slots), F),
        ],
        scratch_shapes=[pltpu.VMEM((slots, width), BF)],
        compiler_params=pltpu.CompilerParams(vmem_limit_bytes=LIMIT),
    )(seg_lengths, tokens, alignment[:, None, :], w0, biases)


def normal_parts(pre):
    size = jnp.abs(pre)
    dens = jnp.exp(pre * pre * -0.5)
    t = 1.0 / (1.0 + (0.3275911 * 0.7071067811865476) * size)
    poly = t * (
        0.5 * 0.254829592
        + t * (0.5 * -0.284496736 + t * (0.5 * 1.421413741 + t * (0.5 * -1.453152027 + t * (0.5 * 1.061405429))))
    )
    tail = poly * dens
    return jnp.where(pre >= 0, 1.0 - tail, tail), dens * 0.3989422804014327


def norm_parts(values_in):
    mean = jnp.mean(values_in, axis=-1, keepdims=True)
    centred = values_in - mean
    inverse = lax.rsqrt(jnp.mean(centred * centred, axis=-1, keepdims=True) + norm_eps)
    return centred * inverse, inverse


def norm_back(grad_hat, hat, inverse):
    return inverse * (
        grad_hat
        - jnp.mean(grad_hat, axis=-1, keepdims=True)
        - hat * jnp.mean(grad_hat * hat, axis=-1, keepdims=True)
    )


def col_sum(values):
    return jnp.sum(values, axis=0, keepdims=True)


def mlp_kernel(
    tiles, ff_cut, att_ref, base_ref, cot_ref, w1_ref, w2_ref, vec_ref, ib_ref,
    enc_ref, gf_ref, ga_ref, g1_ref, g2_ref, gv_ref, gib_ref,
    att_s, norm_s, act_s, slope_s, gmlp_s, gpre_s, gbr_s,
):
    i = pl.program_id(0)
    rows, width = att_ref.shape
    ff = ib_ref.shape[1]
    chunks = ff // ff_cut

    @pl.when(i == 0)
    def _():
        gv_ref[...] = jnp.zeros_like(gv_ref)
        gib_ref[...] = jnp.zeros_like(gib_ref)

    @pl.when(i < tiles)
    def _():
        at = pl.ds(pl.multiple_of(i * rows, rows), rows)
        vec = lambda k: vec_ref[k : k + 1, :]
        att = att_ref[...]
        att_s[at] = att
        first = base_ref[...] + dot(att, w1_ref[:, :width], NN) + vec(2)
        first_hat, first_inv = norm_parts(first)
        normed = first_hat * vec(3) + vec(4)
        norm_low = normed.astype(BF)
        norm_s[at] = norm_low
        second = normed + vec(5)
        for c in range(chunks):
            cols = slice(c * ff_cut, (c + 1) * ff_cut)
            pre = dot(norm_low, w1_ref[:, width + c * ff_cut : width + (c + 1) * ff_cut], NN) + ib_ref[:, cols]
            phi, dens = normal_parts(pre)
            act = (pre * phi).astype(BF)
            act_s[at, cols] = act
            slope_s[:, cols] = (phi + pre * dens).astype(BF)
            second = second + dot(act, w2_ref[cols, :], NN)
        hat, inv = norm_parts(second)
        enc_ref[...] = (hat * vec(6) + vec(7)).astype(BF)
        grad_y = cot_ref[...].astype(F)
        grad_second = norm_back(grad_y * vec(6), hat, inv)
        gmlp = grad_second.astype(BF)
        gmlp_s[at] = gmlp
        grad_normed = grad_second
        for c in range(chunks):
            cols = slice(c * ff_cut, (c + 1) * ff_cut)
            gact = dot(gmlp, w2_ref[cols, :], NT)
            gpre = (gact * slope_s[:, cols].astype(F)).astype(BF)
            gpre_s[at, cols] = gpre
            gib_ref[:, cols] += col_sum(gpre.astype(F))
            grad_normed = grad_normed + dot(gpre, w1_ref[:, width + c * ff_cut : width + (c + 1) * ff_cut], NT)
        grad_first = norm_back(grad_normed * vec(3), first_hat, first_inv)
        gf_ref[...] = grad_first
        gbr = grad_first.astype(BF)
        gbr_s[at] = gbr
        ga_ref[...] = dot(gbr, w1_ref[:, :width], NT).astype(BF)
        gv_ref[2:3] += col_sum(gbr.astype(F))
        gv_ref[3:4] += col_sum(grad_normed * first_hat)
        gv_ref[4:5] += col_sum(grad_normed)
        gv_ref[5:6] += col_sum(gmlp.astype(F))
        gv_ref[6:7] += col_sum(grad_y * hat)
        gv_ref[7:8] += col_sum(grad_y)

    @pl.when((i >= tiles) & (i < tiles + 4))
    def _():
        cols = pl.ds(pl.multiple_of((i - tiles) * width, width), width)
        g2_ref[...] = dot(act_s[:, cols], gmlp_s[...], TN).astype(BF)

    @pl.when((i >= tiles + 4) & (i < tiles + 8))
    def _():
        cols = pl.ds(pl.multiple_of((i - tiles - 4) * width, width), width)
        g1_ref[...] = dot(norm_s[...], gpre_s[:, cols], TN).astype(BF)

    @pl.when(i == tiles + 8)
    def _():
        g1_ref[...] = dot(att_s[...], gbr_s[...], TN).astype(BF)


def mlp_both(attended, base, cotangent, w1, w2, vec, inner_bias, rows=320, ff_cut=768):
    total, width = attended.shape
    ff = inner_bias.shape[1]
    tiles = total // rows
    tile = pl.BlockSpec((rows, width), lambda i: (jnp.minimum(i, tiles - 1), 0))
    whole = lambda shape: once(shape, lambda i: (0, 0))
    return pl.pallas_call(
        functools.partial(mlp_kernel, tiles, ff_cut),
        grid=(tiles + 9,),
        in_specs=[tile, tile, tile, whole(w1.shape), whole(w2.shape), whole(vec.shape), whole(inner_bias.shape)],
        out_specs=[
            tile,
            tile,
            tile,
            pl.BlockSpec((width, width), lambda i: (0, jnp.where(i == tiles + 8, 0, jnp.clip(i - tiles - 4, 0, 3) + 1))),
            pl.BlockSpec((width, width), lambda i: (jnp.clip(i - tiles, 0, 3), 0)),
            whole((8, width)),
            whole((1, ff)),
        ],
        out_shape=[
            jax.ShapeDtypeStruct((total, width), BF),
            jax.ShapeDtypeStruct((total, width), F),
            jax.ShapeDtypeStruct((total, width), BF),
            jax.ShapeDtypeStruct((width, width + ff), BF),
            jax.ShapeDtypeStruct((ff, width), BF),
            jax.ShapeDtypeStruct((8, width), F),
            jax.ShapeDtypeStruct((1, ff), F),
        ],
        scratch_shapes=[
            pltpu.VMEM((total, width), BF),
            pltpu.VMEM((total, width), BF),
            pltpu.VMEM((total, ff), BF),
            pltpu.VMEM((rows, ff), BF),
            pltpu.VMEM((total, width), BF),
            pltpu.VMEM((total, ff), BF),
            pltpu.VMEM((total, width), BF),
        ],
        compiler_params=pltpu.CompilerParams(vmem_limit_bytes=LIMIT),
    )(attended, base, cotangent, w1, w2, vec, inner_bias)


def backward_body(j, b, refs, outs, scratch):
    len_ref, al_ref, q_ref, k_ref, v_ref, o_ref, do_ref, lse_ref, low_ref, gf_ref, w_ref, vec_ref = refs
    gq_ref, gk_ref, gv_ref, gvec_ref, gt_ref = outs
    gbase_s, acc_s, vsum_s = scratch
    text, width = al_ref.shape[1], low_ref.shape[2]
    segs = low_ref.shape[1] - text
    quads = width // QUAD

    bias = key_bias(len_ref[b])
    parts = [[], [], []]
    for pr in range(2):
        cols = slice(128 * pr, 128 * pr + 128)
        logs = [lse_ref[0, 0, 2 * pr + h : 2 * pr + h + 1, :] for h in range(2)]
        got = pair_backward(
            q_ref[0, :, cols], k_ref[0, :, cols], v_ref[0, :, cols], o_ref[0, :, cols], do_ref[0, :, cols], logs, text, bias
        )
        for i in range(3):
            parts[i].append(got[i])
    quad_grads = [jnp.concatenate(p, axis=1) for p in parts]
    cols = pl.ds(pl.multiple_of(j * QUAD, QUAD), QUAD)

    @pl.when(j == 0)
    def _():
        gbase_s[b] = gf_ref[0]

    gbase = gbase_s[b]
    for i in range(3):
        at = pl.ds(pl.multiple_of(i * width + j * QUAD, QUAD), QUAD)
        gbase = gbase + dot(quad_grads[i], w_ref[:, at], NT)
    gbase_s[b] = gbase

    low = low_ref[0]
    weight = [dot(low, g, TN) for g in quad_grads]
    sums = [col_sum(quad_grads[0].astype(F)), col_sum(quad_grads[2].astype(F))]

    @pl.when(b == 0)
    def _():
        for i in range(3):
            acc_s[i] = weight[i]
        for i in range(2):
            vsum_s[i : i + 1, cols] = sums[i]

    @pl.when(b == 1)
    def _():
        for i, ref in enumerate((gq_ref, gk_ref, gv_ref)):
            ref[...] = (acc_s[i] + weight[i]).astype(BF)
        for i in range(2):
            vsum_s[i : i + 1, cols] += sums[i]

    @pl.when(j == quads - 1)
    def _():
        member = member_of(al_ref[0], 1, segs)
        counts = jnp.maximum(jnp.sum(member, axis=0, keepdims=True), 1.0)
        share = gbase[text:] / counts.T
        high = share.astype(BF)
        rest = (share - high.astype(F)).astype(BF)
        sel = member.astype(BF)
        spread = dot(sel, high, NN) + dot(sel, rest, NN)
        gt_ref[0, :text] = (gbase[:text] + spread).astype(BF)
        gt_ref[0, text:] = gbase[text:].astype(BF)

    @pl.when((j == quads - 1) & (b == 1))
    def _():
        lane = lax.broadcasted_iota(jnp.int32, (1, 128), 1)
        cols2 = jnp.where(lane < 2, jnp.concatenate([vsum_s[...], jnp.zeros((120, width), F)], axis=0).T, 0.0)
        gvec_ref[...] = (cols2 + vec_ref[...]).astype(BF)


def backward_kernel(*refs):
    backward_body(pl.program_id(0), pl.program_id(1), refs[:12], refs[12:17], refs[17:])


def backward_attention(seg_lengths, alignment, q, k, v, att, gatt, lse, low, gfirst, w0, vec):
    docs, slots, width = low.shape
    text = alignment.shape[1]
    quads = width // QUAD
    quad = pl.BlockSpec((1, slots, QUAD), lambda j, b: (b, 0, j))
    doc = pl.BlockSpec((1, slots, width), lambda j, b: (b, 0, 0))
    wide = jax.ShapeDtypeStruct((width, width), BF)
    col = pl.BlockSpec((width, QUAD), lambda j, b: (0, j))
    return pl.pallas_call(
        backward_kernel,
        grid=(quads, docs),
        in_specs=[
            SMEM,
            pl.BlockSpec((1, text, 1), lambda j, b: (b, 0, 0)),
            quad,
            quad,
            quad,
            quad,
            quad,
            pl.BlockSpec((1, 1, 8, slots), lambda j, b: (b, j, 0, 0)),
            doc,
            pl.BlockSpec((1, slots, width), lambda j, b: (jnp.where(j == 0, b, 1), 0, 0)),
            once(w0.shape, lambda j, b: (0, 0)),
            once(vec.shape, lambda j, b: (0, 0)),
        ],
        out_specs=[
            col,
            col,
            col,
            once((width, 128), lambda j, b: (0, 0)),
            pl.BlockSpec((1, slots, width), lambda j, b: (jnp.where(j == quads - 1, b, 0), 0, 0)),
        ],
        out_shape=[wide, wide, wide, jax.ShapeDtypeStruct((width, 128), BF), jax.ShapeDtypeStruct((docs, slots, width), BF)],
        scratch_shapes=[
            pltpu.VMEM((docs, slots, width), F),
            pltpu.VMEM((3, width, QUAD), F),
            pltpu.VMEM((8, width), F),
        ],
        compiler_params=pltpu.CompilerParams(vmem_limit_bytes=LIMIT),
    )(seg_lengths, alignment[:, :, None], q, k, v, att, gatt, lse, low, gfirst, w0, vec)


def own_kernels(shard_rows):
    return lax.axis_size("dp") == PLANES and lax.axis_size("fsdp") == 8 and shard_rows == 24


def shards(
    tokens, cotangent, seg_lengths, alignment, query_weight, query_bias, key_weight, value_weight, value_bias,
    out_weight, out_bias, first_gain, first_shift, inner_weight, inner_bias, outer_weight, outer_bias, second_gain,
    second_shift,
):
    docs, slots, width = tokens.shape
    rows = query_weight.shape[0]
    ff = inner_weight.shape[1]
    every = ("dp", "fsdp")
    own = own_kernels(rows)
    vectors = (query_bias, value_bias, out_bias, first_gain, first_shift, outer_bias, second_gain, second_shift)
    columns = [t[:, None] for t in vectors] + [inner_bias.reshape(rows, 4)]
    pad = jnp.zeros((rows, 256 - 12), BF)
    s0 = jnp.concatenate([query_weight, key_weight, value_weight] + columns + [pad], axis=1)
    s1 = jnp.concatenate([out_weight, inner_weight], axis=1)
    if own:
        w0, w1, w2 = gather_all(s0.astype(F), s1.astype(F), outer_weight)
    else:
        w0, w1, w2 = (lax.all_gather(s, every, axis=0, tiled=True) for s in (s0, s1, outer_weight))
    w0, w1, w2 = w0.reshape(width, -1), w1.reshape(width, -1), w2.reshape(-1, width)
    vec = w0[:, 3 * width : 3 * width + 12].astype(F)
    rows_vec = vec[:, :8].T
    inner_row = vec[:, 8:12].reshape(1, ff)

    base, low, q, k, v, att, lse = forward_attention(seg_lengths, tokens, alignment, w0, rows_vec)
    flat = lambda t: t.reshape(docs * slots, width)
    encoded, gfirst, gatt, g1, g2, gvec, ginner = mlp_both(
        flat(att), flat(base), flat(cotangent), w1, w2, rows_vec, inner_row
    )
    whole = lambda t: t.reshape(docs, slots, width)
    vec_cols = jnp.concatenate([gvec.T, ginner.reshape(width, 4), jnp.zeros((width, 116), F)], axis=1)
    gq, gk, gv, gcols, grad_tokens = backward_attention(
        seg_lengths, alignment, q, k, v, att, whole(gatt), lse, low, whole(gfirst), w0, vec_cols
    )
    g0 = jnp.concatenate([gq, gk, gv, gcols, jnp.zeros((width, 128), BF)], axis=1)
    if own:
        o2, o1, o0 = scatter_all(
            (g2.reshape(CHIPS, 2, 96, width), g1.reshape(CHIPS, 48, -1), g0.reshape(CHIPS, 48, -1)), 1
        )
    else:
        o2, o1, o0 = (lax.psum_scatter(g.astype(F), every, scatter_dimension=0, tiled=True) for g in (g2, g1, g0))
    sums = o0[:, 3 * width :]
    return (
        whole(encoded),
        grad_tokens,
        o0[:, :width],
        sums[:, 0],
        o0[:, width : 2 * width],
        o0[:, 2 * width : 3 * width],
        sums[:, 1],
        o1[:, :width],
        sums[:, 2],
        sums[:, 3],
        sums[:, 4],
        o1[:, width:],
        sums[:, 8:12].reshape(-1),
        o2,
        sums[:, 5],
        sums[:, 6],
        sums[:, 7],
    )


def solution(mesh):
    in_specs = (
        P(("dp", "fsdp"), None, None),
        P(("dp", "fsdp"), None, None),
        P(("dp", "fsdp")),
        P(("dp", "fsdp"), None),
        P(("dp", "fsdp"), None),
        P(("dp", "fsdp")),
        P(("dp", "fsdp"), None),
        P(("dp", "fsdp"), None),
        P(("dp", "fsdp")),
        P(("dp", "fsdp"), None),
        P(("dp", "fsdp")),
        P(("dp", "fsdp")),
        P(("dp", "fsdp")),
        P(("dp", "fsdp"), None),
        P(("dp", "fsdp")),
        P(("dp", "fsdp"), None),
        P(("dp", "fsdp")),
        P(("dp", "fsdp")),
        P(("dp", "fsdp")),
    )
    out_specs = (
        P(("dp", "fsdp"), None, None),
        P(("dp", "fsdp"), None, None),
        P(("dp", "fsdp"), None),
        P(("dp", "fsdp")),
        P(("dp", "fsdp"), None),
        P(("dp", "fsdp"), None),
        P(("dp", "fsdp")),
        P(("dp", "fsdp"), None),
        P(("dp", "fsdp")),
        P(("dp", "fsdp")),
        P(("dp", "fsdp")),
        P(("dp", "fsdp"), None),
        P(("dp", "fsdp")),
        P(("dp", "fsdp"), None),
        P(("dp", "fsdp")),
        P(("dp", "fsdp")),
        P(("dp", "fsdp")),
    )
    return jax.shard_map(shards, mesh=mesh, in_specs=in_specs, out_specs=out_specs, check_vma=False)
```

```python
import functools
import jax
import jax.numpy as jnp
from jax import lax
from jax.experimental import pallas as pl
from jax.experimental.pallas import tpu as pltpu
from jax.sharding import PartitionSpec as P

MESH = pl.DeviceIdType.MESH
ANY = pl.BlockSpec(memory_space=pl.ANY)
VMEM = pl.BlockSpec(memory_space=pltpu.VMEM)
PLANES = 4
CHIPS = 16


class Place:
    def __init__(self):
        self.z = lax.axis_index("dp")
        self.f = lax.axis_index("fsdp")
        self.core = self.f % 2
        self.x = (self.f // 2) % 2
        self.y = self.f // 4
        self.sib = self.f + 1 - 2 * self.core
        self.xn = self.f + 2 - 4 * self.x
        self.yn = self.f + 4 - 8 * self.y
        self.spot = self.f // 2
        self.spot_x = self.xn // 2
        self.spot_y = self.yn // 2
        self.spot_d = 3 - self.spot

    def plane(self, back):
        return (self.z + PLANES - back) % PLANES

    def ahead(self, step):
        return (self.z + step) % PLANES

    def barrier(self):
        bar = pltpu.get_barrier_semaphore()
        for other in self.partners():
            pl.semaphore_signal(bar, inc=1, device_id=other, device_id_type=MESH)
        pl.semaphore_wait(bar, 3 + PLANES - 1)

    def partners(self):
        return [(self.z, self.sib), (self.z, self.xn), (self.z, self.yn)] + [
            (self.ahead(k), self.f) for k in range(1, PLANES)
        ]


def remote(src, dst, send, recv, dev):
    return pltpu.make_async_remote_copy(
        src_ref=src, dst_ref=dst, send_sem=send, recv_sem=recv, device_id=dev, device_id_type=MESH
    )


class Gather:
    SEMS = 3 + 4 + 4 + 4 + 4 + 4

    def __init__(self, place, full, own, send, recv, local, width=None):
        self.p, self.full, self.own = place, full, own
        self.send, self.recv, self.local = send, recv, local
        self.half = None if width is None else width // 2
        self.rows = own.shape[0]
        self.started = []

    def view(self, chip, r0=0, r1=None, core=None):
        core = self.p.core if core is None else core
        r1 = self.rows if r1 is None else r1
        if self.half is None:
            return self.full.at[chip, core, pl.ds(r0, r1 - r0), :]
        cols = pl.ds(pl.multiple_of(core * self.half, 128), self.half)
        return self.full.at[chip, pl.ds(r0, r1 - r0), cols]

    def block(self, plane, core):
        if self.half is None:
            return self.full.at[pl.ds(4 * plane, 4), core]
        cols = pl.ds(pl.multiple_of(core * self.half, 128), self.half)
        return self.full.at[pl.ds(4 * plane, 4), :, cols]

    def cut(self, back):
        if self.rows == 96:
            return 48
        return 32 if back % 2 == 0 else 16

    def copy(self, src, dst, index, dev):
        c = remote(src, dst, self.send.at[index], self.recv.at[index], dev)
        return c

    def start(self, make):
        make().start()
        self.started.append(make)

    def chip(self, back, spot):
        return 4 * self.p.plane(back) + spot

    def along_z(self):
        p = self.p
        mine = lambda: self.view(self.chip(0, p.spot))
        self.own_copy().start()
        for k in range(1, PLANES):
            self.start(lambda k=k: self.copy(self.own, mine(), k - 1, (p.ahead(k), p.f)))

    def own_copy(self):
        return pltpu.make_async_copy(self.own, self.view(self.chip(0, self.p.spot)), self.local)

    def to_neighbours(self, back):
        p = self.p
        piece = lambda: self.view(self.chip(back, p.spot))
        if back:
            self.copy(piece(), piece(), back - 1, (p.z, p.f)).wait_recv()
        src = piece if back else lambda: self.own
        self.start(lambda: self.copy(src(), piece(), 3 + back, (p.z, p.xn)))
        self.start(lambda: self.copy(src(), piece(), 7 + back, (p.z, p.yn)))

    def to_diagonal(self, back):
        p, cut = self.p, self.cut(back)
        cx, cy = lambda: self.chip(back, p.spot_x), lambda: self.chip(back, p.spot_y)
        full_x, full_y = self.view(cx()), self.view(cy())
        self.copy(full_x, full_x, 3 + back, (p.z, p.xn)).wait_recv()
        part_x = lambda: self.view(cx(), 0, cut)
        self.start(lambda: self.copy(part_x(), part_x(), 11 + back, (p.z, p.yn)))
        self.copy(full_y, full_y, 7 + back, (p.z, p.yn)).wait_recv()
        part_y = lambda: self.view(cy(), cut, self.rows)
        self.start(lambda: self.copy(part_y(), part_y(), 15 + back, (p.z, p.xn)))

    def to_core(self, back):
        p, cut = self.p, self.cut(back)
        cd = self.chip(back, p.spot_d)
        a, b = self.view(cd, 0, cut), self.view(cd, cut, self.rows)
        self.copy(a, a, 11 + back, (p.z, p.yn)).wait_recv()
        self.copy(b, b, 15 + back, (p.z, p.xn)).wait_recv()
        if back == 0:
            self.own_copy().wait()
        blk = lambda: self.block(p.plane(back), p.core)
        self.start(lambda: self.copy(blk(), blk(), 19 + back, (p.z, p.sib)))

    def finish(self):
        p = self.p
        for back in range(PLANES):
            blk = self.block(p.plane(back), 1 - p.core)
            self.copy(blk, blk, 19 + back, (p.z, p.sib)).wait_recv()

    def drain(self):
        for make in self.started:
            make().wait_send()


def build_own(place, shard, land, own):
    half = own.shape[1]
    first = place.core == 0
    for c0 in range(0, half, 128):
        mine = shard[:, pl.ds(pl.multiple_of(place.core * half + c0, 128), 128)]
        other = land[:, c0 : c0 + 128]
        top = jnp.where(first, mine, other)
        bottom = jnp.where(first, other, mine)
        own[:, c0 : c0 + 128] = jnp.concatenate([top, bottom], axis=0).astype(own.dtype)


class Pair:
    def __init__(self, place, shard, land, own, send, recv):
        half = own.shape[1]
        src = lambda: shard.at[:, pl.ds(pl.multiple_of((1 - place.core) * half, 128), half)]
        self.c = lambda: remote(src(), land, send, recv, (place.z, place.sib))
        self.args = (place, shard, land, own)

    def start(self):
        self.c().start()

    def done(self):
        self.c().wait()
        build_own(*self.args)


class Scatter:
    SEMS = 4 + 4 + 4 + 4 + 4 + 3 + 1

    def __init__(self, place, full, bufs, out, send, recv, local, width=None):
        self.p, self.full, self.out = place, full, out
        self.sums, self.from_core, self.la, self.lb, self.lx, self.ly, self.lz = bufs[:7]
        if width is not None:
            self.total, self.last = bufs[7:]
        self.send, self.recv, self.local = send, recv, local
        self.half = None if width is None else width // 2
        self.rows = self.sums.shape[1]
        self.started = []

    @staticmethod
    def scratch(rows, cols, two_rows):
        bf = jnp.bfloat16
        shapes = [
            pltpu.VMEM((CHIPS, rows, cols), bf),
            pltpu.VMEM((CHIPS, rows, cols), bf),
            pltpu.VMEM((4, rows - 16, cols), bf),
            pltpu.VMEM((4, rows - 16, cols), bf),
            pltpu.VMEM((4, rows, cols), bf),
            pltpu.VMEM((4, rows, cols), bf),
            pltpu.VMEM((3, rows, cols), bf),
        ]
        if two_rows:
            shapes += [pltpu.VMEM((rows, cols), jnp.float32), pltpu.VMEM((rows // 2, cols), jnp.float32)]
        return shapes

    cut = Gather.cut
    chip = Gather.chip
    copy = Gather.copy
    start = Gather.start
    drain = Gather.drain
    block = Gather.block

    def from_sibling(self, back):
        p = self.p
        blk = lambda: pl.ds(4 * p.plane(back), 4)
        c = pltpu.make_async_copy(self.block(p.plane(back), p.core), self.sums.at[blk()], self.local.at[back])
        c.start()
        self.start(
            lambda: self.copy(
                self.block(p.plane(back), 1 - p.core), self.from_core.at[blk()], back, (p.z, p.sib)
            )
        )

    def to_diagonal(self, back):
        p, cut, rows = self.p, self.cut(back), self.rows
        blk = pl.ds(4 * p.plane(back), 4)
        pltpu.make_async_copy(self.block(p.plane(back), p.core), self.sums.at[blk], self.local.at[back]).wait()
        self.copy(self.from_core.at[blk], self.from_core.at[blk], back, (p.z, p.sib)).wait_recv()
        for j in range(4):
            at = 4 * p.plane(back) + j
            self.sums[at] = self.sums[at] + self.from_core[at]
        cd = lambda: self.chip(back, p.spot_d)
        self.start(
            lambda: self.copy(
                self.sums.at[cd(), pl.ds(0, cut)], self.la.at[back, pl.ds(0, cut)], 4 + back, (p.z, p.xn)
            )
        )
        self.start(
            lambda: self.copy(
                self.sums.at[cd(), pl.ds(cut, rows - cut)],
                self.lb.at[back, pl.ds(0, rows - cut)],
                8 + back,
                (p.z, p.yn),
            )
        )

    def to_neighbours(self, back):
        p, cut, rows = self.p, self.cut(back), self.rows
        cx, cy = self.chip(back, p.spot_x), self.chip(back, p.spot_y)
        a, b = self.la.at[back, pl.ds(0, cut)], self.lb.at[back, pl.ds(0, rows - cut)]
        self.copy(a, a, 4 + back, (p.z, p.xn)).wait_recv()
        self.sums[cy, 0:cut] = self.sums[cy, 0:cut] + a[...]
        to_y = lambda: self.sums.at[self.chip(back, p.spot_y)]
        self.start(lambda: self.copy(to_y(), self.ly.at[back], 16 + back, (p.z, p.yn)))
        self.copy(b, b, 8 + back, (p.z, p.yn)).wait_recv()
        self.sums[cx, cut:rows] = self.sums[cx, cut:rows] + b[...]
        to_x = lambda: self.sums.at[self.chip(back, p.spot_x)]
        self.start(lambda: self.copy(to_x(), self.lx.at[back], 12 + back, (p.z, p.xn)))

    def along_z(self, back):
        p = self.p
        c0 = self.chip(back, p.spot)
        lx, ly = self.lx.at[back], self.ly.at[back]
        self.copy(lx, lx, 12 + back, (p.z, p.xn)).wait_recv()
        self.copy(ly, ly, 16 + back, (p.z, p.yn)).wait_recv()
        f = jnp.float32
        got = self.sums[c0].astype(f) + lx[...].astype(f) + ly[...].astype(f)
        self.sums[c0] = got.astype(jnp.bfloat16)
        if back:
            mine = lambda: self.sums.at[self.chip(back, p.spot)]
            self.start(lambda: self.copy(mine(), self.lz.at[back - 1], 20 + back - 1, (p.plane(back), p.f)))

    def owner(self):
        p = self.p
        f = jnp.float32
        for k in range(3):
            self.copy(self.lz.at[k], self.lz.at[k], 20 + k, (p.z, p.f)).wait_recv()
        c0 = self.chip(0, p.spot)
        total = self.sums[c0].astype(f)
        for k in range(3):
            total = total + self.lz[k].astype(f)
        if self.half is None:
            self.out[...] = total
            return
        self.total[...] = total
        rows = self.rows // 2
        theirs = lambda: self.total.at[pl.ds(pl.multiple_of((1 - p.core) * rows, 8), rows)]
        self.start(lambda: self.copy(theirs(), self.last, 23, (p.z, p.sib)))

    def finish(self):
        if self.half is None:
            return
        p, half = self.p, self.half
        rows = self.rows // 2
        self.copy(self.last, self.last, 23, (p.z, p.sib)).wait_recv()
        mine = pl.ds(pl.multiple_of(p.core * rows, 8), rows)
        self.out[:, pl.ds(pl.multiple_of(p.core * half, 128), half)] = self.total[mine]
        self.out[:, pl.ds(pl.multiple_of((1 - p.core) * half, 128), half)] = self.last[...]


F = jnp.float32
BF = jnp.bfloat16
NN = (((1,), (0,)), ((), ()))
NT = (((1,), (1,)), ((), ()))
TN = (((0,), (0,)), ((), ()))
SMEM = pl.BlockSpec(memory_space=pltpu.SMEM)
HEADS = 12
HEAD_DIM = 64
QUAD = 4 * HEAD_DIM
scale = HEAD_DIM**-0.5
norm_eps = 1e-05
masked_score = -1000000000.0
LIMIT = 60 * 2**20


def dot(left, right, dims):
    return lax.dot_general(left, right, dims, preferred_element_type=F)


def once(shape, index):
    return pl.BlockSpec(shape, index, pipeline_mode=pl.Buffered(1))


def key_bias(count):
    row = lax.broadcasted_iota(jnp.int32, (128, 1), 0)
    return jnp.where(row < count, 0.0, masked_score).astype(F)


def masked(scores, text, bias):
    return jnp.concatenate([scores[:text], scores[text:] + bias], axis=0)


def head_lanes(h):
    lane = lax.broadcasted_iota(jnp.int32, (1, 128), 1)
    return (lane < HEAD_DIM) if h == 0 else (lane >= HEAD_DIM)


def pair_forward(q2, k2, v2, text, bias):
    vt = v2.T
    outs, logs = [], []
    for h in range(2):
        qh = jnp.where(head_lanes(h), q2, BF(0))
        scores = masked(dot(k2, qh, NT), text, bias)
        top = jnp.max(scores, axis=0, keepdims=True)
        expo = jnp.exp(scores - top)
        total = jnp.sum(expo, axis=0, keepdims=True)
        outs.append(dot(vt[HEAD_DIM * h : HEAD_DIM * (h + 1)], expo.astype(BF), NN) * (1.0 / total))
        logs.append(top + jnp.log(total))
    return jnp.concatenate(outs, axis=0).T.astype(BF), logs


def pair_backward(q2, k2, v2, o2, do2, logs, text, bias):
    prod = (do2.astype(F) * o2.astype(F)).T
    kt = (k2 * BF(scale)).T
    dq, dk, dv = [], [], []
    for h in range(2):
        rows = slice(HEAD_DIM * h, HEAD_DIM * (h + 1))
        qh = jnp.where(head_lanes(h), q2, BF(0))
        doh = jnp.where(head_lanes(h), do2, BF(0))
        delta = jnp.sum(prod[rows], axis=0, keepdims=True)
        probs = jnp.exp(masked(dot(k2, qh, NT), text, bias) - logs[h])
        grads = (probs * (dot(v2, doh, NT) - delta)).astype(BF)
        dv.append(dot(probs.astype(BF), do2, NN))
        dk.append(dot(grads, q2, NN))
        dq.append(dot(kt[rows], grads, NN))
    first = head_lanes(0)
    return (
        jnp.concatenate(dq, axis=0).T.astype(BF),
        jnp.where(first, dk[0], dk[1]).astype(BF),
        jnp.where(first, dv[0], dv[1]).astype(BF),
    )


def member_of(align, axis, segs):
    shape = (segs, align.shape[1]) if axis == 0 else (align.shape[0], segs)
    return (align == lax.broadcasted_iota(jnp.int32, shape, axis)).astype(F)


def forward_body(b, j, len_ref, tok_ref, al_ref, w_cols, bias_ref, outs, low_s, hook=lambda at: None):
    base_ref, low_ref, q_ref, k_ref, v_ref, att_ref, lse_ref = outs
    text, width = al_ref.shape[2], tok_ref.shape[2]
    segs = tok_ref.shape[1] - text

    @pl.when(j == 0)
    def _():
        member = member_of(al_ref[0], 0, segs)
        counts = jnp.maximum(jnp.sum(member, axis=1, keepdims=True), 1.0)
        tok = tok_ref[0]
        pooled = dot(member.astype(BF), tok[:text], NN) / counts
        seg_base = tok[text:].astype(F) + pooled
        base_ref[0, :text] = tok[:text].astype(F)
        base_ref[0, text:] = seg_base
        low_ref[0, :text] = tok[:text]
        low_ref[0, text:] = seg_base.astype(BF)
        low_s[:text] = tok[:text]
        low_s[text:] = seg_base.astype(BF)

    hook(0)
    low = low_s[...]
    parts = []
    for i, ref in enumerate((q_ref, k_ref, v_ref)):
        at = i * width + j * QUAD
        rows = dot(low, w_cols(pl.ds(pl.multiple_of(at, QUAD), QUAD)), NN)
        if i != 1:
            rows = rows + bias_ref[i // 2 : i // 2 + 1, pl.ds(pl.multiple_of(j * QUAD, QUAD), QUAD)]
        rows = rows.astype(BF)
        if i == 0:
            rows = rows * BF(scale)
        ref[0] = rows
        parts.append(rows)
    bias = key_bias(len_ref[b])
    for pr in range(2):
        cols = slice(128 * pr, 128 * pr + 128)
        out, logs = pair_forward(parts[0][:, cols], parts[1][:, cols], parts[2][:, cols], text, bias)
        att_ref[0, :, cols] = out
        for h in range(2):
            lse_ref[0, 0, 2 * pr + h : 2 * pr + h + 1, :] = logs[h]
        hook(1 + pr)


def forward_kernel(len_ref, tok_ref, al_ref, w_ref, bias_ref, *rest):
    w_cols = lambda cols: w_ref[:, cols]
    forward_body(pl.program_id(0), pl.program_id(1), len_ref, tok_ref, al_ref, w_cols, bias_ref, rest[:7], rest[7])


def forward_attention(seg_lengths, tokens, alignment, w0, biases):
    docs, slots, width = tokens.shape
    text = alignment.shape[1]
    quads = width // QUAD
    doc = pl.BlockSpec((1, slots, width), lambda b, j: (b, 0, 0))
    quad = pl.BlockSpec((1, slots, QUAD), lambda b, j: (b, 0, j))
    wide = jax.ShapeDtypeStruct((docs, slots, width), BF)
    return pl.pallas_call(
        forward_kernel,
        grid=(docs, quads),
        in_specs=[
            SMEM,
            doc,
            pl.BlockSpec((1, 1, text), lambda b, j: (b, 0, 0)),
            once(w0.shape, lambda b, j: (0, 0)),
            once(biases.shape, lambda b, j: (0, 0)),
        ],
        out_specs=[doc, doc, quad, quad, quad, quad, pl.BlockSpec((1, 1, 8, slots), lambda b, j: (b, j, 0, 0))],
        out_shape=[
            jax.ShapeDtypeStruct((docs, slots, width), F),
            wide,
            wide,
            wide,
            wide,
            wide,
            jax.ShapeDtypeStruct((docs, quads, 8, slots), F),
        ],
        scratch_shapes=[pltpu.VMEM((slots, width), BF)],
        compiler_params=pltpu.CompilerParams(vmem_limit_bytes=LIMIT),
    )(seg_lengths, tokens, alignment[:, None, :], w0, biases)


def normal_parts(pre):
    size = jnp.abs(pre)
    dens = jnp.exp(pre * pre * -0.5)
    t = 1.0 / (1.0 + (0.3275911 * 0.7071067811865476) * size)
    poly = t * (
        0.5 * 0.254829592
        + t * (0.5 * -0.284496736 + t * (0.5 * 1.421413741 + t * (0.5 * -1.453152027 + t * (0.5 * 1.061405429))))
    )
    tail = poly * dens
    return jnp.where(pre >= 0, 1.0 - tail, tail), dens * 0.3989422804014327


def norm_parts(values_in):
    mean = jnp.mean(values_in, axis=-1, keepdims=True)
    centred = values_in - mean
    inverse = lax.rsqrt(jnp.mean(centred * centred, axis=-1, keepdims=True) + norm_eps)
    return centred * inverse, inverse


def norm_back(grad_hat, hat, inverse):
    return inverse * (
        grad_hat
        - jnp.mean(grad_hat, axis=-1, keepdims=True)
        - hat * jnp.mean(grad_hat * hat, axis=-1, keepdims=True)
    )


def col_sum(values):
    return jnp.sum(values, axis=0, keepdims=True)


def mlp_kernel(
    tiles, ff_cut, att_ref, base_ref, cot_ref, w1_ref, w2_ref, vec_ref, ib_ref,
    enc_ref, gf_ref, ga_ref, g1_ref, g2_ref, gv_ref, gib_ref,
    att_s, norm_s, act_s, slope_s, gmlp_s, gpre_s, gbr_s,
):
    i = pl.program_id(0)
    rows, width = att_ref.shape
    ff = ib_ref.shape[1]
    chunks = ff // ff_cut

    @pl.when(i == 0)
    def _():
        gv_ref[...] = jnp.zeros_like(gv_ref)
        gib_ref[...] = jnp.zeros_like(gib_ref)

    @pl.when(i < tiles)
    def _():
        at = pl.ds(pl.multiple_of(i * rows, rows), rows)
        vec = lambda k: vec_ref[k : k + 1, :]
        att = att_ref[...]
        att_s[at] = att
        first = base_ref[...] + dot(att, w1_ref[:, :width], NN) + vec(2)
        first_hat, first_inv = norm_parts(first)
        normed = first_hat * vec(3) + vec(4)
        norm_low = normed.astype(BF)
        norm_s[at] = norm_low
        second = normed + vec(5)
        for c in range(chunks):
            cols = slice(c * ff_cut, (c + 1) * ff_cut)
            pre = dot(norm_low, w1_ref[:, width + c * ff_cut : width + (c + 1) * ff_cut], NN) + ib_ref[:, cols]
            phi, dens = normal_parts(pre)
            act = (pre * phi).astype(BF)
            act_s[at, cols] = act
            slope_s[:, cols] = (phi + pre * dens).astype(BF)
            second = second + dot(act, w2_ref[cols, :], NN)
        hat, inv = norm_parts(second)
        enc_ref[...] = (hat * vec(6) + vec(7)).astype(BF)
        grad_y = cot_ref[...].astype(F)
        grad_second = norm_back(grad_y * vec(6), hat, inv)
        gmlp = grad_second.astype(BF)
        gmlp_s[at] = gmlp
        grad_normed = grad_second
        for c in range(chunks):
            cols = slice(c * ff_cut, (c + 1) * ff_cut)
            gact = dot(gmlp, w2_ref[cols, :], NT)
            gpre = (gact * slope_s[:, cols].astype(F)).astype(BF)
            gpre_s[at, cols] = gpre
            gib_ref[:, cols] += col_sum(gpre.astype(F))
            grad_normed = grad_normed + dot(gpre, w1_ref[:, width + c * ff_cut : width + (c + 1) * ff_cut], NT)
        grad_first = norm_back(grad_normed * vec(3), first_hat, first_inv)
        gf_ref[...] = grad_first
        gbr = grad_first.astype(BF)
        gbr_s[at] = gbr
        ga_ref[...] = dot(gbr, w1_ref[:, :width], NT).astype(BF)
        gv_ref[2:3] += col_sum(gbr.astype(F))
        gv_ref[3:4] += col_sum(grad_normed * first_hat)
        gv_ref[4:5] += col_sum(grad_normed)
        gv_ref[5:6] += col_sum(gmlp.astype(F))
        gv_ref[6:7] += col_sum(grad_y * hat)
        gv_ref[7:8] += col_sum(grad_y)

    @pl.when((i >= tiles) & (i < tiles + 4))
    def _():
        cols = pl.ds(pl.multiple_of((i - tiles) * width, width), width)
        g2_ref[...] = dot(act_s[:, cols], gmlp_s[...], TN).astype(BF)

    @pl.when((i >= tiles + 4) & (i < tiles + 8))
    def _():
        cols = pl.ds(pl.multiple_of((i - tiles - 4) * width, width), width)
        g1_ref[...] = dot(norm_s[...], gpre_s[:, cols], TN).astype(BF)

    @pl.when(i == tiles + 8)
    def _():
        g1_ref[...] = dot(att_s[...], gbr_s[...], TN).astype(BF)


def mlp_both(attended, base, cotangent, w1, w2, vec, inner_bias, rows=320, ff_cut=768):
    total, width = attended.shape
    ff = inner_bias.shape[1]
    tiles = total // rows
    tile = pl.BlockSpec((rows, width), lambda i: (jnp.minimum(i, tiles - 1), 0))
    whole = lambda shape: once(shape, lambda i: (0, 0))
    return pl.pallas_call(
        functools.partial(mlp_kernel, tiles, ff_cut),
        grid=(tiles + 9,),
        in_specs=[tile, tile, tile, whole(w1.shape), whole(w2.shape), whole(vec.shape), whole(inner_bias.shape)],
        out_specs=[
            tile,
            tile,
            tile,
            pl.BlockSpec((width, width), lambda i: (0, jnp.where(i == tiles + 8, 0, jnp.clip(i - tiles - 4, 0, 3) + 1))),
            pl.BlockSpec((width, width), lambda i: (jnp.clip(i - tiles, 0, 3), 0)),
            whole((8, width)),
            whole((1, ff)),
        ],
        out_shape=[
            jax.ShapeDtypeStruct((total, width), BF),
            jax.ShapeDtypeStruct((total, width), F),
            jax.ShapeDtypeStruct((total, width), BF),
            jax.ShapeDtypeStruct((width, width + ff), BF),
            jax.ShapeDtypeStruct((ff, width), BF),
            jax.ShapeDtypeStruct((8, width), F),
            jax.ShapeDtypeStruct((1, ff), F),
        ],
        scratch_shapes=[
            pltpu.VMEM((total, width), BF),
            pltpu.VMEM((total, width), BF),
            pltpu.VMEM((total, ff), BF),
            pltpu.VMEM((rows, ff), BF),
            pltpu.VMEM((total, width), BF),
            pltpu.VMEM((total, ff), BF),
            pltpu.VMEM((total, width), BF),
        ],
        compiler_params=pltpu.CompilerParams(vmem_limit_bytes=LIMIT),
    )(attended, base, cotangent, w1, w2, vec, inner_bias)


def backward_body(j, b, refs, keep, gt_ref, scratch, hook=lambda at: None):
    len_ref, al_ref, q_ref, k_ref, v_ref, o_ref, do_ref, lse_ref, low_ref, gf_ref, w_ref, vec_ref = refs
    gbase_s, acc_s, vsum_s = scratch
    text, width = al_ref.shape[1], low_ref.shape[2]
    segs = low_ref.shape[1] - text
    quads = width // QUAD

    hook(0)
    bias = key_bias(len_ref[b])
    parts = [[], [], []]
    for pr in range(2):
        cols = slice(128 * pr, 128 * pr + 128)
        logs = [lse_ref[0, 0, 2 * pr + h : 2 * pr + h + 1, :] for h in range(2)]
        got = pair_backward(
            q_ref[0, :, cols], k_ref[0, :, cols], v_ref[0, :, cols], o_ref[0, :, cols], do_ref[0, :, cols], logs, text, bias
        )
        for i in range(3):
            parts[i].append(got[i])
        if pr == 0:
            hook(1)
    quad_grads = [jnp.concatenate(p, axis=1) for p in parts]
    cols = pl.ds(pl.multiple_of(j * QUAD, QUAD), QUAD)

    @pl.when(j == 0)
    def _():
        gbase_s[b] = gf_ref[0]

    gbase = gbase_s[b]
    for i in range(3):
        at = pl.ds(pl.multiple_of(i * width + j * QUAD, QUAD), QUAD)
        gbase = gbase + dot(quad_grads[i], w_ref[:, at], NT)
    gbase_s[b] = gbase

    low = low_ref[0]
    weight = [dot(low, g, TN) for g in quad_grads]
    sums = [col_sum(quad_grads[0].astype(F)), col_sum(quad_grads[2].astype(F))]

    @pl.when(b == 0)
    def _():
        for i in range(3):
            acc_s[i] = weight[i]
        for i in range(2):
            vsum_s[i : i + 1, cols] = sums[i]

    @pl.when(b == 1)
    def _():
        for i in range(2):
            vsum_s[i : i + 1, cols] += sums[i]
        keep(lambda i: (acc_s[i] + weight[i]).astype(BF))

    @pl.when(j == quads - 1)
    def _():
        member = member_of(al_ref[0], 1, segs)
        counts = jnp.maximum(jnp.sum(member, axis=0, keepdims=True), 1.0)
        share = gbase[text:] / counts.T
        high = share.astype(BF)
        rest = (share - high.astype(F)).astype(BF)
        sel = member.astype(BF)
        spread = dot(sel, high, NN) + dot(sel, rest, NN)
        gt_ref[0, :text] = (gbase[:text] + spread).astype(BF)
        gt_ref[0, text:] = gbase[text:].astype(BF)

    hook(2)


def vector_cols(vsum_s, vec_ref):
    lane = lax.broadcasted_iota(jnp.int32, (1, 128), 1)
    pad = jnp.zeros((120, vsum_s.shape[1]), F)
    return (jnp.where(lane < 2, jnp.concatenate([vsum_s[...], pad], axis=0).T, 0.0) + vec_ref[...]).astype(BF)


def backward_kernel(*refs):
    gvec_ref, gt_ref = refs[15:17]

    def keep(grad):
        for i in range(3):
            refs[12 + i][...] = grad(i)

        @pl.when(pl.program_id(0) == pl.num_programs(0) - 1)
        def _():
            gvec_ref[...] = vector_cols(refs[19], refs[11])

    backward_body(pl.program_id(0), pl.program_id(1), refs[:12], keep, gt_ref, refs[17:])


def backward_attention(seg_lengths, alignment, q, k, v, att, gatt, lse, low, gfirst, w0, vec):
    docs, slots, width = low.shape
    text = alignment.shape[1]
    quads = width // QUAD
    quad = pl.BlockSpec((1, slots, QUAD), lambda j, b: (b, 0, j))
    doc = pl.BlockSpec((1, slots, width), lambda j, b: (b, 0, 0))
    wide = jax.ShapeDtypeStruct((width, width), BF)
    col = pl.BlockSpec((width, QUAD), lambda j, b: (0, j))
    return pl.pallas_call(
        backward_kernel,
        grid=(quads, docs),
        in_specs=[
            SMEM,
            pl.BlockSpec((1, text, 1), lambda j, b: (b, 0, 0)),
            quad,
            quad,
            quad,
            quad,
            quad,
            pl.BlockSpec((1, 1, 8, slots), lambda j, b: (b, j, 0, 0)),
            doc,
            pl.BlockSpec((1, slots, width), lambda j, b: (jnp.where(j == 0, b, 1), 0, 0)),
            once(w0.shape, lambda j, b: (0, 0)),
            once(vec.shape, lambda j, b: (0, 0)),
        ],
        out_specs=[
            col,
            col,
            col,
            once((width, 128), lambda j, b: (0, 0)),
            pl.BlockSpec((1, slots, width), lambda j, b: (jnp.where(j == quads - 1, b, 0), 0, 0)),
        ],
        out_shape=[wide, wide, wide, jax.ShapeDtypeStruct((width, 128), BF), jax.ShapeDtypeStruct((docs, slots, width), BF)],
        scratch_shapes=[
            pltpu.VMEM((docs, slots, width), F),
            pltpu.VMEM((3, width, QUAD), F),
            pltpu.VMEM((8, width), F),
        ],
        compiler_params=pltpu.CompilerParams(vmem_limit_bytes=LIMIT),
    )(seg_lengths, alignment[:, :, None], q, k, v, att, gatt, lse, low, gfirst, w0, vec)


def at_slots(plan, step, slot):
    for (when, where), calls in plan.items():
        if where == slot:

            @pl.when(step == when)
            def _():
                for call in calls:
                    call()


def each(fn, *backs):
    return [functools.partial(fn, k) for k in backs]


def forward_fused_kernel(
    len_ref, tok_ref, al_ref, s0, s1, s2, *rest
):
    outs, (w0, w1, w2) = rest[:7], rest[7:10]
    low_s, w0_s, bias_s, land0, land1, own0, own1, pair_sem, local, send, recv = rest[10:]
    b, j = pl.program_id(0), pl.program_id(1)
    quads = pl.num_programs(1)
    step = b * quads + j
    place = Place()
    pairs = [
        Pair(place, s0, land0, own0, pair_sem.at[0], pair_sem.at[1]),
        Pair(place, s1, land1, own1, pair_sem.at[2], pair_sem.at[3]),
    ]
    g0 = Gather(place, w0_s, own0, send.at[0], recv.at[0], local.at[0], w0.shape[2])
    g1 = Gather(place, w1, own1, send.at[1], recv.at[1], local.at[1], w1.shape[2])
    g2 = Gather(place, w2, s2, send.at[2], recv.at[2], local.at[2])
    width = tok_ref.shape[2]
    save = lambda: pltpu.make_async_copy(w0_s, w0, local.at[3])

    def bias_rows():
        vec = w0_s[:, :, 3 * width : 3 * width + 128].reshape(width, 128).astype(F)
        bias_s[...] = vec.T[:8]

    plan = {
        (0, -1): [
            place.barrier, pairs[0].start, pairs[1].start, pairs[0].done, g0.along_z,
            functools.partial(g0.to_neighbours, 0), pairs[1].done, g1.along_z, g2.along_z,
        ],
        (0, 0): [
            *each(g0.to_neighbours, 1, 2, 3), *each(g0.to_diagonal, 0), *each(g1.to_neighbours, 0),
            *each(g0.to_diagonal, 1, 2, 3), *each(g1.to_neighbours, 1, 2, 3), *each(g0.to_core, 0, 1, 2, 3),
            *each(g2.to_neighbours, 0, 1), g0.finish, save().start, bias_rows,
        ],
        (0, 1): each(g1.to_diagonal, 0, 1),
        (0, 2): [*each(g1.to_diagonal, 2), *each(g2.to_neighbours, 2, 3)],
        (1, 1): [*each(g1.to_diagonal, 3), *each(g1.to_core, 0)],
        (1, 2): each(g1.to_core, 1),
        (2, 1): [*each(g2.to_diagonal, 0), *each(g1.to_core, 2)],
        (2, 2): [*each(g2.to_diagonal, 1), *each(g1.to_core, 3)],
        (3, 1): each(g2.to_diagonal, 2),
        (3, 2): each(g2.to_diagonal, 3),
        (4, 1): each(g2.to_core, 0),
        (4, 2): each(g2.to_core, 1),
        (5, 2): [
            *each(g2.to_core, 2, 3), g1.finish, g2.finish, lambda: save().wait(), g0.drain, g1.drain, g2.drain,
        ],
    }
    at_slots(plan, step, -1)
    w_cols = lambda cols: w0_s[:, :, cols].reshape(width, QUAD)
    forward_body(
        b, j, len_ref, tok_ref, al_ref, w_cols, bias_s, outs, low_s, functools.partial(at_slots, plan, step)
    )


def forward_fused(seg_lengths, tokens, alignment, s0, s1, s2):
    docs, slots, width = tokens.shape
    text = alignment.shape[1]
    quads = width // QUAD
    n0, n1 = s0.shape[1], s1.shape[1]
    doc = pl.BlockSpec((1, slots, width), lambda b, j: (b, 0, 0))
    quad = pl.BlockSpec((1, slots, QUAD), lambda b, j: (b, 0, j))
    wide = jax.ShapeDtypeStruct((docs, slots, width), BF)
    full = lambda a: once(a.shape, lambda b, j: (0, 0))
    return pl.pallas_call(
        forward_fused_kernel,
        grid=(docs, quads),
        in_specs=[SMEM, doc, pl.BlockSpec((1, 1, text), lambda b, j: (b, 0, 0)), full(s0), full(s1), full(s2)],
        out_specs=[doc, doc, quad, quad, quad, quad, pl.BlockSpec((1, 1, 8, slots), lambda b, j: (b, j, 0, 0))]
        + [ANY] * 3,
        out_shape=[
            jax.ShapeDtypeStruct((docs, slots, width), F),
            wide,
            wide,
            wide,
            wide,
            wide,
            jax.ShapeDtypeStruct((docs, quads, 8, slots), F),
            jax.ShapeDtypeStruct((CHIPS, 48, n0), BF),
            jax.ShapeDtypeStruct((CHIPS, 48, n1), BF),
            jax.ShapeDtypeStruct((CHIPS, 2, 96, width), BF),
        ],
        scratch_shapes=[
            pltpu.VMEM((slots, width), BF),
            pltpu.VMEM((CHIPS, 48, n0), BF),
            pltpu.VMEM((8, width), F),
            pltpu.VMEM((24, n0 // 2), F),
            pltpu.VMEM((24, n1 // 2), F),
            pltpu.VMEM((48, n0 // 2), BF),
            pltpu.VMEM((48, n1 // 2), BF),
            pltpu.SemaphoreType.DMA((4,)),
            pltpu.SemaphoreType.DMA((4,)),
            pltpu.SemaphoreType.DMA((3, Gather.SEMS)),
            pltpu.SemaphoreType.DMA((3, Gather.SEMS)),
        ],
        compiler_params=pltpu.CompilerParams(collective_id=0, has_side_effects=True, vmem_limit_bytes=LIMIT),
    )(seg_lengths, tokens, alignment[:, None, :], s0, s1, s2)


def backward_fused_kernel(widths, *refs):
    ins, (g2_ref, g1_ref) = refs[:12], refs[12:14]
    gt_ref, o_wide, o_inner, o_outer, o_vec = refs[14], refs[15:19], refs[19], refs[20], refs[21]
    scratch = refs[22:25]
    rest = list(refs[25:])
    local, send, recv = rest[-3:]
    j, b = pl.program_id(0), pl.program_id(1)
    step = 2 * j + b
    width = ins[8].shape[2]
    place = Place()
    take = lambda n: [rest.pop(0) for _ in range(n)]
    quad_s, stage = take(3), take(1)[0]
    sources = [g2_ref, g1_ref, *quad_s]
    groups = []
    for i, (src, wide) in enumerate(zip(sources, widths)):
        bufs = take(7 if wide is None else 9)
        out = o_outer if wide is None else stage.at[:, pl.ds(0, wide)]
        groups.append(Scatter(place, src, bufs, out, send.at[i], recv.at[i], local.at[i], wide))
    g2, g1, q0, q1, q2 = groups

    def give_rest():
        g1.finish()
        o_wide[3][...] = stage[:, :width]
        o_inner[...] = stage[:, width : widths[1]]

    def give_quad(k):
        groups[2 + k].finish()
        for i in range(3):
            o_wide[i][:, k * QUAD : (k + 1) * QUAD] = stage[:, i * QUAD : (i + 1) * QUAD]
        if k == 2:
            o_vec[...] = stage[:, 3 * QUAD : 3 * QUAD + 128]

    def keep(grad):
        for k in range(3):

            @pl.when(j == k)
            def _():
                for i in range(3):
                    quad_s[k][:, :, i * QUAD : (i + 1) * QUAD] = grad(i).reshape(CHIPS, 48, QUAD)
                if k == 2:
                    vec = vector_cols(scratch[2], ins[11])
                    both = jnp.concatenate([vec, jnp.zeros_like(vec)], axis=1)
                    quad_s[k][:, :, 3 * QUAD :] = both.reshape(CHIPS, 48, QUAD)

    late, soon = (3, 2), (1, 0)
    all4 = late + soon
    plan = {
        (0, 0): [place.barrier, *each(g2.from_sibling, *all4), *each(g1.from_sibling, *all4)],
        (0, 1): each(g2.to_diagonal, *late),
        (0, 2): [*each(g2.to_diagonal, *soon), *each(g1.to_diagonal, *late)],
        (1, 1): [*each(g2.to_neighbours, *late), *each(g1.to_diagonal, *soon)],
        (1, 2): [*each(g2.to_neighbours, *soon), *each(q0.from_sibling, *all4)],
        (2, 1): [*each(g1.to_neighbours, *late), *each(g2.along_z, *late)],
        (2, 2): [*each(g1.to_neighbours, *soon), *each(q0.to_diagonal, *all4), *each(g2.along_z, *soon)],
        (3, 1): [*each(g1.along_z, *late)],
        (3, 2): [*each(q0.to_neighbours, *all4), *each(q1.from_sibling, *all4), *each(g1.along_z, *soon), g2.owner],
        (4, 1): [g2.finish, *each(q1.to_diagonal, *all4)],
        (4, 2): [*each(q0.along_z, *all4), g1.owner],
        (5, 1): [*each(q1.to_neighbours, *all4), give_rest],
        (5, 2): [
            *each(q2.from_sibling, *all4), *each(q1.along_z, *all4), q0.owner, *each(q2.to_diagonal, *all4),
            functools.partial(give_quad, 0), *each(q2.to_neighbours, *all4), q1.owner, *each(q2.along_z, *all4),
            functools.partial(give_quad, 1), q2.owner, functools.partial(give_quad, 2),
            *[g.drain for g in groups],
        ],
    }
    backward_body(j, b, ins, keep, gt_ref, scratch, functools.partial(at_slots, plan, step))


def backward_fused(seg_lengths, alignment, q, k, v, att, gatt, lse, low, gfirst, w0, vec, g2, g1):
    docs, slots, width = low.shape
    text = alignment.shape[1]
    quads = width // QUAD
    quad = pl.BlockSpec((1, slots, QUAD), lambda j, b: (b, 0, j))
    doc = pl.BlockSpec((1, slots, width), lambda j, b: (b, 0, 0))
    whole = lambda *shape: once(shape, lambda j, b: (0,) * len(shape))
    n1 = g1.shape[2]
    widths = (None, n1, 3 * QUAD, 3 * QUAD, 4 * QUAD)
    bufs = []
    for wide in widths:
        bufs += Scatter.scratch(96, width, False) if wide is None else Scatter.scratch(48, wide // 2, True)
    n = len(widths)
    shard = jax.ShapeDtypeStruct((24, width), F)
    return pl.pallas_call(
        functools.partial(backward_fused_kernel, widths),
        grid=(quads, docs),
        in_specs=[
            SMEM,
            pl.BlockSpec((1, text, 1), lambda j, b: (b, 0, 0)),
            quad,
            quad,
            quad,
            quad,
            quad,
            pl.BlockSpec((1, 1, 8, slots), lambda j, b: (b, j, 0, 0)),
            doc,
            pl.BlockSpec((1, slots, width), lambda j, b: (jnp.where(j == 0, b, 1), 0, 0)),
            whole(*w0.shape),
            whole(*vec.shape),
            ANY,
            ANY,
        ],
        out_specs=[
            pl.BlockSpec((1, slots, width), lambda j, b: (jnp.where(j == quads - 1, b, 0), 0, 0)),
            *[whole(24, width)] * 4,
            whole(24, n1 - width),
            whole(96, width),
            whole(24, 128),
        ],
        out_shape=[
            jax.ShapeDtypeStruct((docs, slots, width), BF),
            shard,
            shard,
            shard,
            shard,
            jax.ShapeDtypeStruct((24, n1 - width), F),
            jax.ShapeDtypeStruct((96, width), F),
            jax.ShapeDtypeStruct((24, 128), F),
        ],
        scratch_shapes=[
            pltpu.VMEM((docs, slots, width), F),
            pltpu.VMEM((3, width, QUAD), F),
            pltpu.VMEM((8, width), F),
            *[pltpu.VMEM((CHIPS, 48, wide), BF) for wide in widths[2:]],
            pltpu.VMEM((24, n1), F),
            *bufs,
            pltpu.SemaphoreType.DMA((n, 4)),
            pltpu.SemaphoreType.DMA((n, Scatter.SEMS)),
            pltpu.SemaphoreType.DMA((n, Scatter.SEMS)),
        ],
        compiler_params=pltpu.CompilerParams(collective_id=1, has_side_effects=True, vmem_limit_bytes=LIMIT),
    )(seg_lengths, alignment[:, :, None], q, k, v, att, gatt, lse, low, gfirst, w0, vec, g2, g1)


def own_kernels(shard_rows, docs):
    return lax.axis_size("dp") == PLANES and lax.axis_size("fsdp") == 8 and shard_rows == 24 and docs == 2


def shards(
    tokens, cotangent, seg_lengths, alignment, query_weight, query_bias, key_weight, value_weight, value_bias,
    out_weight, out_bias, first_gain, first_shift, inner_weight, inner_bias, outer_weight, outer_bias, second_gain,
    second_shift,
):
    docs, slots, width = tokens.shape
    rows = query_weight.shape[0]
    ff = inner_weight.shape[1]
    every = ("dp", "fsdp")
    own = own_kernels(rows, docs)
    vectors = (query_bias, value_bias, out_bias, first_gain, first_shift, outer_bias, second_gain, second_shift)
    columns = [t[:, None] for t in vectors] + [inner_bias.reshape(rows, 4)]
    pad = jnp.zeros((rows, 256 - 12), BF)
    s0 = jnp.concatenate([query_weight, key_weight, value_weight] + columns + [pad], axis=1)
    s1 = jnp.concatenate([out_weight, inner_weight], axis=1)
    if own:
        *saved, w0, w1, w2 = forward_fused(seg_lengths, tokens, alignment, s0.astype(F), s1.astype(F), outer_weight)
    else:
        w0, w1, w2 = (lax.all_gather(s, every, axis=0, tiled=True) for s in (s0, s1, outer_weight))
    w0, w1, w2 = w0.reshape(width, -1), w1.reshape(width, -1), w2.reshape(-1, width)
    vec = w0[:, 3 * width : 3 * width + 12].astype(F)
    rows_vec = vec[:, :8].T
    inner_row = vec[:, 8:12].reshape(1, ff)
    if not own:
        saved = forward_attention(seg_lengths, tokens, alignment, w0, rows_vec)
    base, low, q, k, v, att, lse = saved

    flat = lambda t: t.reshape(docs * slots, width)
    encoded, gfirst, gatt, g1, g2, gvec, ginner = mlp_both(
        flat(att), flat(base), flat(cotangent), w1, w2, rows_vec, inner_row
    )
    whole = lambda t: t.reshape(docs, slots, width)
    vec_cols = jnp.concatenate([gvec.T, ginner.reshape(width, 4), jnp.zeros((width, 116), F)], axis=1)
    back = (seg_lengths, alignment, q, k, v, att, whole(gatt), lse, low, whole(gfirst), w0, vec_cols)
    if own:
        grad_tokens, gq, gk, gv, gout, ginn, gouter, sums = backward_fused(
            *back, g2.reshape(CHIPS, 2, 96, width), g1.reshape(CHIPS, 48, -1)
        )
    else:
        gq, gk, gv, gcols, grad_tokens = backward_attention(*back)
        owned = lambda g: lax.psum_scatter(g.astype(F), every, scatter_dimension=0, tiled=True)
        gq, gk, gv, sums, gouter = (owned(g) for g in (gq, gk, gv, gcols, g2))
        g1 = owned(g1)
        gout, ginn = g1[:, :width], g1[:, width:]
    return (
        whole(encoded), grad_tokens, gq, sums[:, 0], gk, gv, sums[:, 1], gout, sums[:, 2], sums[:, 3], sums[:, 4],
        ginn, sums[:, 8:12].reshape(-1), gouter, sums[:, 5], sums[:, 6], sums[:, 7],
    )


def solution(mesh):
    in_specs = (
        P(("dp", "fsdp"), None, None),
        P(("dp", "fsdp"), None, None),
        P(("dp", "fsdp")),
        P(("dp", "fsdp"), None),
        P(("dp", "fsdp"), None),
        P(("dp", "fsdp")),
        P(("dp", "fsdp"), None),
        P(("dp", "fsdp"), None),
        P(("dp", "fsdp")),
        P(("dp", "fsdp"), None),
        P(("dp", "fsdp")),
        P(("dp", "fsdp")),
        P(("dp", "fsdp")),
        P(("dp", "fsdp"), None),
        P(("dp", "fsdp")),
        P(("dp", "fsdp"), None),
        P(("dp", "fsdp")),
        P(("dp", "fsdp")),
        P(("dp", "fsdp")),
    )
    out_specs = (
        P(("dp", "fsdp"), None, None),
        P(("dp", "fsdp"), None, None),
        P(("dp", "fsdp"), None),
        P(("dp", "fsdp")),
        P(("dp", "fsdp"), None),
        P(("dp", "fsdp"), None),
        P(("dp", "fsdp")),
        P(("dp", "fsdp"), None),
        P(("dp", "fsdp")),
        P(("dp", "fsdp")),
        P(("dp", "fsdp")),
        P(("dp", "fsdp"), None),
        P(("dp", "fsdp")),
        P(("dp", "fsdp"), None),
        P(("dp", "fsdp")),
        P(("dp", "fsdp")),
        P(("dp", "fsdp")),
    )
    return jax.shard_map(shards, mesh=mesh, in_specs=in_specs, out_specs=out_specs, check_vma=False)
```

```python
import functools
import jax
import jax.numpy as jnp
from jax import lax
from jax.experimental import pallas as pl
from jax.experimental.pallas import tpu as pltpu
from jax.sharding import PartitionSpec as P

MESH = pl.DeviceIdType.MESH
ANY = pl.BlockSpec(memory_space=pl.ANY)
VMEM = pl.BlockSpec(memory_space=pltpu.VMEM)
PLANES = 4
CHIPS = 16


class Place:
    def __init__(self):
        self.z = lax.axis_index("dp")
        self.f = lax.axis_index("fsdp")
        self.core = self.f % 2
        self.x = (self.f // 2) % 2
        self.y = self.f // 4
        self.sib = self.f + 1 - 2 * self.core
        self.xn = self.f + 2 - 4 * self.x
        self.yn = self.f + 4 - 8 * self.y
        self.spot = self.f // 2
        self.spot_x = self.xn // 2
        self.spot_y = self.yn // 2
        self.spot_d = 3 - self.spot

    def plane(self, back):
        return (self.z + PLANES - back) % PLANES

    def coming(self, k):
        return (self.z, 1 + self.z % 2, (self.z + 2) % PLANES, 3 * ((self.z + 1) % 2))[k]

    def ahead(self, step):
        return (self.z + step) % PLANES

    def barrier(self):
        bar = pltpu.get_barrier_semaphore()
        for other in self.partners():
            pl.semaphore_signal(bar, inc=1, device_id=other, device_id_type=MESH)
        pl.semaphore_wait(bar, 3 + PLANES - 1)

    def partners(self):
        return [(self.z, self.sib), (self.z, self.xn), (self.z, self.yn)] + [
            (self.ahead(k), self.f) for k in range(1, PLANES)
        ]


def remote(src, dst, send, recv, dev):
    return pltpu.make_async_remote_copy(
        src_ref=src, dst_ref=dst, send_sem=send, recv_sem=recv, device_id=dev, device_id_type=MESH
    )


class Gather:
    SEMS = 29

    def __init__(self, place, full, own, send, recv, local, width=None):
        self.p, self.full, self.own = place, full, own
        self.send, self.recv, self.local = send, recv, local
        self.half = None if width is None else width // 2
        self.rows = own.shape[0]
        self.started = []

    def view(self, chip, r0=0, r1=None, core=None):
        core = self.p.core if core is None else core
        r1 = self.rows if r1 is None else r1
        if self.half is None:
            return self.full.at[chip, core, pl.ds(r0, r1 - r0), :]
        cols = pl.ds(pl.multiple_of(core * self.half, 128), self.half)
        return self.full.at[chip, pl.ds(r0, r1 - r0), cols]

    def block(self, plane, core):
        if self.half is None:
            return self.full.at[pl.ds(4 * plane, 4), core]
        cols = pl.ds(pl.multiple_of(core * self.half, 128), self.half)
        return self.full.at[pl.ds(4 * plane, 4), :, cols]

    def cut(self, k):
        if self.rows == 96:
            return 48
        return 32 if k % 2 == 0 else 16

    def copy(self, src, dst, index, dev, send=None):
        return remote(src, dst, self.send.at[index if send is None else send], self.recv.at[index], dev)

    def start(self, make, when=None):
        if when is None:
            make().start()
        else:
            pl.when(when())(lambda: make().start())
        self.started.append((make, when))

    def drain(self):
        for make, when in self.started:
            if when is None:
                make().wait_send()
            else:
                pl.when(when())(lambda: make().wait_send())

    def chip(self, k, spot):
        return 4 * self.p.coming(k) + spot

    def own_copy(self):
        return pltpu.make_async_copy(self.own, self.view(self.chip(0, self.p.spot)), self.local)

    def along_z(self):
        p = self.p
        mine = lambda: self.view(self.chip(0, p.spot))
        self.own_copy().start()
        self.start(lambda: self.copy(self.own, mine(), p.z, (p.z - 1, p.f), 24), lambda: p.z > 0)
        self.start(lambda: self.copy(self.own, mine(), p.z, (p.z + 1, p.f), 25), lambda: p.z < PLANES - 1)

    def onward(self, k, when=None):
        p = self.p
        piece = lambda: self.view(self.chip(k, p.spot))
        goal = lambda: p.z + jnp.where(p.coming(k) < p.z, 1, -1)
        goes = lambda: (goal() >= 0) & (goal() < PLANES)
        wait = lambda: self.copy(piece(), piece(), p.coming(k), (p.z, p.f)).wait_recv()
        both = goes if when is None else lambda: when() & goes()
        if when is None:
            wait()
        else:
            pl.when(when())(wait)
        self.start(lambda: self.copy(piece(), piece(), p.coming(k), (goal(), p.f), 25 + k), both)

    def to_neighbours(self, k):
        p = self.p
        piece = lambda: self.view(self.chip(k, p.spot))
        middle = lambda: p.z % 3 != 0
        if k == 1:
            self.onward(1)
            self.onward(3, middle)
        elif k == 2:
            self.onward(2)
        elif k == 3:
            self.onward(3, lambda: p.z % 3 == 0)
        src = piece if k else lambda: self.own
        self.start(lambda: self.copy(src(), piece(), 4 + k, (p.z, p.xn)))
        self.start(lambda: self.copy(src(), piece(), 8 + k, (p.z, p.yn)))

    def to_diagonal(self, k):
        p, cut = self.p, self.cut(k)
        cx, cy = lambda: self.chip(k, p.spot_x), lambda: self.chip(k, p.spot_y)
        full_x, full_y = self.view(cx()), self.view(cy())
        self.copy(full_x, full_x, 4 + k, (p.z, p.xn)).wait_recv()
        part_x = lambda: self.view(cx(), 0, cut)
        self.start(lambda: self.copy(part_x(), part_x(), 12 + k, (p.z, p.yn)))
        self.copy(full_y, full_y, 8 + k, (p.z, p.yn)).wait_recv()
        part_y = lambda: self.view(cy(), cut, self.rows)
        self.start(lambda: self.copy(part_y(), part_y(), 16 + k, (p.z, p.xn)))

    def to_core(self, k):
        p, cut = self.p, self.cut(k)
        cd = self.chip(k, p.spot_d)
        a, b = self.view(cd, 0, cut), self.view(cd, cut, self.rows)
        self.copy(a, a, 12 + k, (p.z, p.yn)).wait_recv()
        self.copy(b, b, 16 + k, (p.z, p.xn)).wait_recv()
        if k == 0:
            self.own_copy().wait()
        blk = lambda: self.block(p.coming(k), p.core)
        self.start(lambda: self.copy(blk(), blk(), 20 + k, (p.z, p.sib)))

    def finish(self):
        p = self.p
        for k in range(PLANES):
            blk = self.block(p.coming(k), 1 - p.core)
            self.copy(blk, blk, 20 + k, (p.z, p.sib)).wait_recv()


def build_own(place, shard, land, own):
    half = own.shape[1]
    first = place.core == 0
    for c0 in range(0, half, 128):
        mine = shard[:, pl.ds(pl.multiple_of(place.core * half + c0, 128), 128)]
        other = land[:, c0 : c0 + 128]
        top = jnp.where(first, mine, other)
        bottom = jnp.where(first, other, mine)
        own[:, c0 : c0 + 128] = jnp.concatenate([top, bottom], axis=0).astype(own.dtype)


class Pair:
    def __init__(self, place, shard, land, own, send, recv):
        half = own.shape[1]
        src = lambda: shard.at[:, pl.ds(pl.multiple_of((1 - place.core) * half, 128), half)]
        self.c = lambda: remote(src(), land, send, recv, (place.z, place.sib))
        self.args = (place, shard, land, own)

    def start(self):
        self.c().start()

    def done(self):
        self.c().wait()
        build_own(*self.args)


class Scatter:
    SEMS = 4 + 4 + 4 + 4 + 4 + 3 + 1

    def __init__(self, place, full, bufs, out, send, recv, local, width=None):
        self.p, self.full, self.out = place, full, out
        self.sums, self.from_core, self.la, self.lb, self.lx, self.ly, self.lz = bufs[:7]
        if width is not None:
            self.total, self.last = bufs[7:]
        self.send, self.recv, self.local = send, recv, local
        self.half = None if width is None else width // 2
        self.rows = self.sums.shape[1]
        self.started = []

    @staticmethod
    def scratch(rows, cols, two_rows):
        bf = jnp.bfloat16
        shapes = [
            pltpu.VMEM((CHIPS, rows, cols), bf),
            pltpu.VMEM((CHIPS, rows, cols), bf),
            pltpu.VMEM((4, rows - 16, cols), bf),
            pltpu.VMEM((4, rows - 16, cols), bf),
            pltpu.VMEM((4, rows, cols), bf),
            pltpu.VMEM((4, rows, cols), bf),
            pltpu.VMEM((3, rows, cols), bf),
        ]
        if two_rows:
            shapes += [pltpu.VMEM((rows, cols), jnp.float32), pltpu.VMEM((rows // 2, cols), jnp.float32)]
        return shapes

    def chip(self, back, spot):
        return 4 * self.p.plane(back) + spot

    cut = Gather.cut
    copy = Gather.copy
    start = Gather.start
    drain = Gather.drain
    block = Gather.block

    def from_sibling(self, back):
        p = self.p
        blk = lambda: pl.ds(4 * p.plane(back), 4)
        c = pltpu.make_async_copy(self.block(p.plane(back), p.core), self.sums.at[blk()], self.local.at[back])
        c.start()
        self.start(
            lambda: self.copy(
                self.block(p.plane(back), 1 - p.core), self.from_core.at[blk()], back, (p.z, p.sib)
            )
        )

    def to_diagonal(self, back):
        p, cut, rows = self.p, self.cut(back), self.rows
        blk = pl.ds(4 * p.plane(back), 4)
        pltpu.make_async_copy(self.block(p.plane(back), p.core), self.sums.at[blk], self.local.at[back]).wait()
        self.copy(self.from_core.at[blk], self.from_core.at[blk], back, (p.z, p.sib)).wait_recv()
        for j in range(4):
            at = 4 * p.plane(back) + j
            self.sums[at] = self.sums[at] + self.from_core[at]
        cd = lambda: self.chip(back, p.spot_d)
        self.start(
            lambda: self.copy(
                self.sums.at[cd(), pl.ds(0, cut)], self.la.at[back, pl.ds(0, cut)], 4 + back, (p.z, p.xn)
            )
        )
        self.start(
            lambda: self.copy(
                self.sums.at[cd(), pl.ds(cut, rows - cut)],
                self.lb.at[back, pl.ds(0, rows - cut)],
                8 + back,
                (p.z, p.yn),
            )
        )

    def to_neighbours(self, back):
        p, cut, rows = self.p, self.cut(back), self.rows
        cx, cy = self.chip(back, p.spot_x), self.chip(back, p.spot_y)
        a, b = self.la.at[back, pl.ds(0, cut)], self.lb.at[back, pl.ds(0, rows - cut)]
        self.copy(a, a, 4 + back, (p.z, p.xn)).wait_recv()
        self.sums[cy, 0:cut] = self.sums[cy, 0:cut] + a[...]
        to_y = lambda: self.sums.at[self.chip(back, p.spot_y)]
        self.start(lambda: self.copy(to_y(), self.ly.at[back], 16 + back, (p.z, p.yn)))
        self.copy(b, b, 8 + back, (p.z, p.yn)).wait_recv()
        self.sums[cx, cut:rows] = self.sums[cx, cut:rows] + b[...]
        to_x = lambda: self.sums.at[self.chip(back, p.spot_x)]
        self.start(lambda: self.copy(to_x(), self.lx.at[back], 12 + back, (p.z, p.xn)))

    def along_z(self, back):
        p = self.p
        c0 = self.chip(back, p.spot)
        lx, ly = self.lx.at[back], self.ly.at[back]
        self.copy(lx, lx, 12 + back, (p.z, p.xn)).wait_recv()
        self.copy(ly, ly, 16 + back, (p.z, p.yn)).wait_recv()
        f = jnp.float32
        got = self.sums[c0].astype(f) + lx[...].astype(f) + ly[...].astype(f)
        self.sums[c0] = got.astype(jnp.bfloat16)
        if back:
            mine = lambda: self.sums.at[self.chip(back, p.spot)]
            self.start(lambda: self.copy(mine(), self.lz.at[back - 1], 20 + back - 1, (p.plane(back), p.f)))

    def owner(self):
        p = self.p
        f = jnp.float32
        for k in range(3):
            self.copy(self.lz.at[k], self.lz.at[k], 20 + k, (p.z, p.f)).wait_recv()
        c0 = self.chip(0, p.spot)
        total = self.sums[c0].astype(f)
        for k in range(3):
            total = total + self.lz[k].astype(f)
        if self.half is None:
            self.out[...] = total
            return
        self.total[...] = total
        rows = self.rows // 2
        theirs = lambda: self.total.at[pl.ds(pl.multiple_of((1 - p.core) * rows, 8), rows)]
        self.start(lambda: self.copy(theirs(), self.last, 23, (p.z, p.sib)))

    def finish(self):
        if self.half is None:
            return
        p, half = self.p, self.half
        rows = self.rows // 2
        self.copy(self.last, self.last, 23, (p.z, p.sib)).wait_recv()
        mine = pl.ds(pl.multiple_of(p.core * rows, 8), rows)
        self.out[:, pl.ds(pl.multiple_of(p.core * half, 128), half)] = self.total[mine]
        self.out[:, pl.ds(pl.multiple_of((1 - p.core) * half, 128), half)] = self.last[...]


F = jnp.float32
BF = jnp.bfloat16
NN = (((1,), (0,)), ((), ()))
NT = (((1,), (1,)), ((), ()))
TN = (((0,), (0,)), ((), ()))
SMEM = pl.BlockSpec(memory_space=pltpu.SMEM)
HEADS = 12
HEAD_DIM = 64
QUAD = 4 * HEAD_DIM
scale = HEAD_DIM**-0.5
norm_eps = 1e-05
masked_score = -1000000000.0
LIMIT = 60 * 2**20


def dot(left, right, dims):
    return lax.dot_general(left, right, dims, preferred_element_type=F)


def once(shape, index):
    return pl.BlockSpec(shape, index, pipeline_mode=pl.Buffered(1))


def key_bias(count):
    row = lax.broadcasted_iota(jnp.int32, (128, 1), 0)
    return jnp.where(row < count, 0.0, masked_score).astype(F)


def masked(scores, text, bias):
    return jnp.concatenate([scores[:text], scores[text:] + bias], axis=0)


def head_lanes(h):
    lane = lax.broadcasted_iota(jnp.int32, (1, 128), 1)
    return (lane < HEAD_DIM) if h == 0 else (lane >= HEAD_DIM)


def pair_forward(q2, k2, v2, text, bias, between):
    vt = v2.T
    outs, logs = [], []
    for h in range(2):
        qh = jnp.where(head_lanes(h), q2, BF(0))
        scores = masked(dot(k2, qh, NT), text, bias)
        top = jnp.max(scores, axis=0, keepdims=True)
        expo = jnp.exp(scores - top)
        total = jnp.sum(expo, axis=0, keepdims=True)
        outs.append(dot(vt[HEAD_DIM * h : HEAD_DIM * (h + 1)], expo.astype(BF), NN) * (1.0 / total))
        logs.append(top + jnp.log(total))
        if h == 0:
            between()
    return jnp.concatenate(outs, axis=0).T.astype(BF), logs


def pair_backward(q2, k2, v2, o2, do2, logs, text, bias, between):
    prod = (do2.astype(F) * o2.astype(F)).T
    kt = (k2 * BF(scale)).T
    dq, dk, dv = [], [], []
    for h in range(2):
        rows = slice(HEAD_DIM * h, HEAD_DIM * (h + 1))
        qh = jnp.where(head_lanes(h), q2, BF(0))
        doh = jnp.where(head_lanes(h), do2, BF(0))
        delta = jnp.sum(prod[rows], axis=0, keepdims=True)
        probs = jnp.exp(masked(dot(k2, qh, NT), text, bias) - logs[h])
        grads = (probs * (dot(v2, doh, NT) - delta)).astype(BF)
        dv.append(dot(probs.astype(BF), do2, NN))
        dk.append(dot(grads, q2, NN))
        dq.append(dot(kt[rows], grads, NN))
        if h == 0:
            between()
    first = head_lanes(0)
    return (
        jnp.concatenate(dq, axis=0).T.astype(BF),
        jnp.where(first, dk[0], dk[1]).astype(BF),
        jnp.where(first, dv[0], dv[1]).astype(BF),
    )


def member_of(align, segs):
    return (align == lax.broadcasted_iota(jnp.int32, (segs, align.shape[1]), 0)).astype(F)


def forward_body(b, j, len_ref, tok_ref, al_ref, w_cols, bias_ref, outs, low_s, hook=lambda at: None):
    base_ref, low_ref, q_ref, k_ref, v_ref, att_ref, lse_ref = outs
    text, width = al_ref.shape[1], tok_ref.shape[2]
    segs = tok_ref.shape[1] - text

    @pl.when(j == 0)
    def _():
        member = member_of(al_ref[pl.ds(b, 1), :], segs)
        counts = jnp.maximum(jnp.sum(member, axis=1, keepdims=True), 1.0)
        tok = tok_ref[0]
        pooled = dot(member.astype(BF), tok[:text], NN) / counts
        seg_base = tok[text:].astype(F) + pooled
        base_ref[0, :text] = tok[:text].astype(F)
        base_ref[0, text:] = seg_base
        low_ref[0, :text] = tok[:text]
        low_ref[0, text:] = seg_base.astype(BF)
        low_s[:text] = tok[:text]
        low_s[text:] = seg_base.astype(BF)

    hook(0)
    low = low_s[...]
    parts = []
    for i, ref in enumerate((q_ref, k_ref, v_ref)):
        at = i * width + j * QUAD
        rows = dot(low, w_cols(pl.ds(pl.multiple_of(at, QUAD), QUAD)), NN)
        if i != 1:
            rows = rows + bias_ref[i // 2 : i // 2 + 1, pl.ds(pl.multiple_of(j * QUAD, QUAD), QUAD)]
        rows = rows.astype(BF)
        if i == 0:
            rows = rows * BF(scale)
        ref[0] = rows
        parts.append(rows)
    bias = key_bias(len_ref[b])
    for pr in range(2):
        cols = slice(128 * pr, 128 * pr + 128)
        out, logs = pair_forward(parts[0][:, cols], parts[1][:, cols], parts[2][:, cols], text, bias, lambda: hook(1 + 2 * pr))
        att_ref[0, :, cols] = out
        for h in range(2):
            lse_ref[0, 0, 2 * pr + h : 2 * pr + h + 1, :] = logs[h]
        hook(2 + 2 * pr)


def forward_kernel(len_ref, tok_ref, al_ref, w_ref, bias_ref, *rest):
    w_cols = lambda cols: w_ref[:, cols]
    forward_body(pl.program_id(0), pl.program_id(1), len_ref, tok_ref, al_ref, w_cols, bias_ref, rest[:7], rest[7])


def forward_attention(seg_lengths, tokens, alignment, w0, biases):
    docs, slots, width = tokens.shape
    quads = width // QUAD
    doc = pl.BlockSpec((1, slots, width), lambda b, j: (b, 0, 0))
    quad = pl.BlockSpec((1, slots, QUAD), lambda b, j: (b, 0, j))
    wide = jax.ShapeDtypeStruct((docs, slots, width), BF)
    return pl.pallas_call(
        forward_kernel,
        grid=(docs, quads),
        in_specs=[
            SMEM,
            doc,
            once(alignment.shape, lambda b, j: (0, 0)),
            once(w0.shape, lambda b, j: (0, 0)),
            once(biases.shape, lambda b, j: (0, 0)),
        ],
        out_specs=[doc, doc, quad, quad, quad, quad, pl.BlockSpec((1, 1, 8, slots), lambda b, j: (b, j, 0, 0))],
        out_shape=[
            jax.ShapeDtypeStruct((docs, slots, width), F),
            wide,
            wide,
            wide,
            wide,
            wide,
            jax.ShapeDtypeStruct((docs, quads, 8, slots), F),
        ],
        scratch_shapes=[pltpu.VMEM((slots, width), BF)],
        compiler_params=pltpu.CompilerParams(vmem_limit_bytes=LIMIT),
    )(seg_lengths, tokens, alignment, w0, biases)


def normal_parts(pre):
    size = jnp.abs(pre)
    dens = jnp.exp(pre * pre * -0.5)
    t = 1.0 / (1.0 + (0.3275911 * 0.7071067811865476) * size)
    poly = t * (
        0.5 * 0.254829592
        + t * (0.5 * -0.284496736 + t * (0.5 * 1.421413741 + t * (0.5 * -1.453152027 + t * (0.5 * 1.061405429))))
    )
    tail = poly * dens
    return jnp.where(pre >= 0, 1.0 - tail, tail), dens * 0.3989422804014327


def norm_parts(values_in):
    mean = jnp.mean(values_in, axis=-1, keepdims=True)
    centred = values_in - mean
    inverse = lax.rsqrt(jnp.mean(centred * centred, axis=-1, keepdims=True) + norm_eps)
    return centred * inverse, inverse


def norm_back(grad_hat, hat, inverse):
    return inverse * (
        grad_hat
        - jnp.mean(grad_hat, axis=-1, keepdims=True)
        - hat * jnp.mean(grad_hat * hat, axis=-1, keepdims=True)
    )


def col_sum(values):
    return jnp.sum(values, axis=0, keepdims=True)


def mlp_first(att, base, w_out, w_in, vec, inner_bias, put, ff_cut=768, hook=lambda at: None):
    first = base + dot(att, w_out(), NN) + vec(2)
    hat, inv = norm_parts(first)
    low = (hat * vec(3) + vec(4)).astype(BF)
    put("norm", hat, inv, low)
    chunks = inner_bias.shape[1] // ff_cut
    pre_of = lambda c: dot(low, w_in(c * ff_cut, ff_cut), NN) + inner_bias[:, c * ff_cut : (c + 1) * ff_cut]
    pre = pre_of(0)
    for c in range(chunks):
        later = pre_of(c + 1) if c + 1 < chunks else None
        phi, dens = normal_parts(pre)
        put("act", slice(c * ff_cut, (c + 1) * ff_cut), (pre * phi).astype(BF), (phi + pre * dens).astype(BF))
        pre = later
        hook(1 + c)


def mlp_second(hat1, act, w_outer, cot, vec, ff_cut=768):
    second = hat1 * vec(3) + vec(4) + vec(5)
    for c in range(act.shape[1] // ff_cut):
        second = second + dot(act[:, c * ff_cut : (c + 1) * ff_cut], w_outer(c * ff_cut, ff_cut), NN)
    hat, inv = norm_parts(second)
    grad_y = cot.astype(F)
    sums = (col_sum(grad_y * hat), col_sum(grad_y))
    return (hat * vec(6) + vec(7)).astype(BF), norm_back(grad_y * vec(6), hat, inv), sums


def mlp_back(grad_second, gmlp, hat1, inv1, slope, w_outer, w_out, w_in, vec, put, ff_cut=768, hook=lambda at: None):
    grad_normed = grad_second
    chunks = slope.shape[1] // ff_cut
    act_of = lambda c: dot(gmlp, w_outer(c * ff_cut, ff_cut), NT)
    gact = act_of(0)
    for c in range(chunks):
        later = act_of(c + 1) if c + 1 < chunks else None
        cols = slice(c * ff_cut, (c + 1) * ff_cut)
        gpre = (gact * slope[:, cols].astype(F)).astype(BF)
        put("pre", cols, gpre)
        grad_normed = grad_normed + dot(gpre, w_in(c * ff_cut, ff_cut), NT)
        gact = later
        if c == 1:
            hook(1)
    grad_first = norm_back(grad_normed * vec(3), hat1, inv1)
    low = grad_first.astype(BF)
    put("first", grad_first, low, col_sum(grad_normed * hat1), col_sum(grad_normed))
    return dot(low, w_out(), NT).astype(BF)


def mlp_kernel(
    tiles, att_ref, base_ref, cot_ref, w1_ref, w2_ref, vec_ref, ib_ref,
    enc_ref, gf_ref, ga_ref, g1_ref, g2_ref, gv_ref, gib_ref,
    att_s, norm_s, act_s, slope_s, gmlp_s, gpre_s, gbr_s,
):
    i = pl.program_id(0)
    rows, width = att_ref.shape

    @pl.when(i == 0)
    def _():
        gv_ref[...] = jnp.zeros_like(gv_ref)
        gib_ref[...] = jnp.zeros_like(gib_ref)

    @pl.when(i < tiles)
    def _():
        at = pl.ds(pl.multiple_of(i * rows, rows), rows)
        vec = lambda k: vec_ref[k : k + 1, :]
        w_out = lambda: w1_ref[:, :width]
        w_in = lambda c, n: w1_ref[:, width + c : width + c + n]
        w_outer = lambda c, n: w2_ref[c : c + n, :]
        kept = {}

        def put(kind, *got):
            if kind == "norm":
                kept["hat"], kept["inv"], norm_s[at] = got
            elif kind == "act":
                act_s[at, got[0]], slope_s[:, got[0]] = got[1:]
            elif kind == "pre":
                gpre_s[at, got[0]] = got[1]
                gib_ref[:, got[0]] += col_sum(got[1].astype(F))
            else:
                gf_ref[...], gbr_s[at] = got[:2]
                gv_ref[2:3] += col_sum(got[1].astype(F))
                gv_ref[3:4] += got[2]
                gv_ref[4:5] += got[3]

        att_s[at] = att_ref[...]
        mlp_first(att_ref[...], base_ref[...], w_out, w_in, vec, ib_ref[...], put)
        enc_ref[...], grad_second, sums = mlp_second(kept["hat"], act_s[at], w_outer, cot_ref[...], vec)
        gmlp = grad_second.astype(BF)
        gmlp_s[at] = gmlp
        gv_ref[5:6] += col_sum(gmlp.astype(F))
        gv_ref[6:7] += sums[0]
        gv_ref[7:8] += sums[1]
        ga_ref[...] = mlp_back(
            grad_second, gmlp, kept["hat"], kept["inv"], slope_s[...], w_outer, w_out, w_in, vec, put
        )

    @pl.when((i >= tiles) & (i < tiles + 4))
    def _():
        cols = pl.ds(pl.multiple_of((i - tiles) * width, width), width)
        g2_ref[...] = dot(act_s[:, cols], gmlp_s[...], TN).astype(BF)

    @pl.when((i >= tiles + 4) & (i < tiles + 8))
    def _():
        cols = pl.ds(pl.multiple_of((i - tiles - 4) * width, width), width)
        g1_ref[...] = dot(norm_s[...], gpre_s[:, cols], TN).astype(BF)

    @pl.when(i == tiles + 8)
    def _():
        g1_ref[...] = dot(att_s[...], gbr_s[...], TN).astype(BF)


def mlp_both(attended, base, cotangent, w1, w2, vec, inner_bias, rows=320):
    total, width = attended.shape
    ff = inner_bias.shape[1]
    tiles = total // rows
    tile = pl.BlockSpec((rows, width), lambda i: (jnp.minimum(i, tiles - 1), 0))
    whole = lambda shape: once(shape, lambda i: (0, 0))
    return pl.pallas_call(
        functools.partial(mlp_kernel, tiles),
        grid=(tiles + 9,),
        in_specs=[tile, tile, tile, whole(w1.shape), whole(w2.shape), whole(vec.shape), whole(inner_bias.shape)],
        out_specs=[
            tile,
            tile,
            tile,
            pl.BlockSpec((width, width), lambda i: (0, jnp.where(i == tiles + 8, 0, jnp.clip(i - tiles - 4, 0, 3) + 1))),
            pl.BlockSpec((width, width), lambda i: (jnp.clip(i - tiles, 0, 3), 0)),
            whole((8, width)),
            whole((1, ff)),
        ],
        out_shape=[
            jax.ShapeDtypeStruct((total, width), BF),
            jax.ShapeDtypeStruct((total, width), F),
            jax.ShapeDtypeStruct((total, width), BF),
            jax.ShapeDtypeStruct((width, width + ff), BF),
            jax.ShapeDtypeStruct((ff, width), BF),
            jax.ShapeDtypeStruct((8, width), F),
            jax.ShapeDtypeStruct((1, ff), F),
        ],
        scratch_shapes=[
            pltpu.VMEM((total, width), BF),
            pltpu.VMEM((total, width), BF),
            pltpu.VMEM((total, ff), BF),
            pltpu.VMEM((rows, ff), BF),
            pltpu.VMEM((total, width), BF),
            pltpu.VMEM((total, ff), BF),
            pltpu.VMEM((total, width), BF),
        ],
        compiler_params=pltpu.CompilerParams(vmem_limit_bytes=LIMIT),
    )(attended, base, cotangent, w1, w2, vec, inner_bias)


def backward_body(j, b, refs, keep, gt_ref, scratch, hook=lambda at: None):
    len_ref, al_ref, q_ref, k_ref, v_ref, o_ref, do_ref, lse_ref, low_ref, gf_ref, w_ref = refs
    gbase_s, acc_s, vsum_s = scratch
    text, width = al_ref.shape[1], low_ref.shape[2]
    segs = low_ref.shape[1] - text
    quads = width // QUAD
    align = al_ref[pl.ds(b, 1), :]

    hook(0)
    bias = key_bias(len_ref[b])
    parts = [[], [], []]
    for pr in range(2):
        cols = slice(128 * pr, 128 * pr + 128)
        logs = [lse_ref[0, 0, 2 * pr + h : 2 * pr + h + 1, :] for h in range(2)]
        got = pair_backward(
            q_ref[0, :, cols], k_ref[0, :, cols], v_ref[0, :, cols], o_ref[0, :, cols], do_ref[0, :, cols], logs, text, bias,
            lambda: hook(1 + 2 * pr),
        )
        for i in range(3):
            parts[i].append(got[i])
        if pr == 0:
            hook(2)
    quad_grads = [jnp.concatenate(p, axis=1) for p in parts]
    cols = pl.ds(pl.multiple_of(j * QUAD, QUAD), QUAD)

    @pl.when(j == 0)
    def _():
        gbase_s[b] = gf_ref[0]

    gbase = gbase_s[b]
    for i in range(3):
        at = pl.ds(pl.multiple_of(i * width + j * QUAD, QUAD), QUAD)
        gbase = gbase + dot(quad_grads[i], w_ref[:, at], NT)
    gbase_s[b] = gbase

    low = low_ref[0]
    weight = [dot(low, g, TN) for g in quad_grads]
    sums = [col_sum(quad_grads[0].astype(F)), col_sum(quad_grads[2].astype(F))]

    @pl.when(b == 0)
    def _():
        for i in range(3):
            acc_s[i] = weight[i]
        for i in range(2):
            vsum_s[i : i + 1, cols] = sums[i]

    @pl.when(b == 1)
    def _():
        for i in range(2):
            vsum_s[i : i + 1, cols] += sums[i]
        keep(lambda i: (acc_s[i] + weight[i]).astype(BF))

    @pl.when(j == quads - 1)
    def _():
        member = member_of(align, segs)
        counts = jnp.maximum(jnp.sum(member, axis=1, keepdims=True), 1.0)
        share = gbase[text:] / counts
        high = share.astype(BF)
        rest = (share - high.astype(F)).astype(BF)
        sel = member.astype(BF)
        spread = dot(sel, high, TN) + dot(sel, rest, TN)
        gt_ref[0, :text] = (gbase[:text] + spread).astype(BF)
        gt_ref[0, text:] = gbase[text:].astype(BF)

    hook(4)


def vector_cols(vsum_s, gv_ref, gib_ref, cols_s):
    width = gv_ref.shape[1]
    rows = jnp.concatenate([vsum_s[:2], gv_ref[2:], jnp.zeros((120, width), F)], axis=0)
    cols_s[...] = jnp.zeros_like(cols_s)
    share = gib_ref.shape[1] * 24 // width
    for d in range(width // 24):
        cols_s[24 * d : 24 * d + 1, :share] = gib_ref[:, d * share : (d + 1) * share]
    return jnp.concatenate([rows.T, cols_s[...]], axis=1).astype(BF)


def backward_kernel(*refs):
    vsum_ref, gt_ref = refs[14:16]

    def keep(grad):
        for i in range(3):
            refs[11 + i][...] = grad(i)

    backward_body(pl.program_id(0), pl.program_id(1), refs[:11], keep, gt_ref, [refs[16], refs[17], vsum_ref])


def backward_attention(seg_lengths, alignment, q, k, v, att, gatt, lse, low, gfirst, w0):
    docs, slots, width = low.shape
    quads = width // QUAD
    quad = pl.BlockSpec((1, slots, QUAD), lambda j, b: (b, 0, j))
    doc = pl.BlockSpec((1, slots, width), lambda j, b: (b, 0, 0))
    wide = jax.ShapeDtypeStruct((width, width), BF)
    col = pl.BlockSpec((width, QUAD), lambda j, b: (0, j))
    return pl.pallas_call(
        backward_kernel,
        grid=(quads, docs),
        in_specs=[
            SMEM,
            once(alignment.shape, lambda j, b: (0, 0)),
            quad,
            quad,
            quad,
            quad,
            quad,
            pl.BlockSpec((1, 1, 8, slots), lambda j, b: (b, j, 0, 0)),
            doc,
            pl.BlockSpec((1, slots, width), lambda j, b: (jnp.where(j == 0, b, 1), 0, 0)),
            once(w0.shape, lambda j, b: (0, 0)),
        ],
        out_specs=[
            col,
            col,
            col,
            once((8, width), lambda j, b: (0, 0)),
            pl.BlockSpec((1, slots, width), lambda j, b: (jnp.where(j == quads - 1, b, 0), 0, 0)),
        ],
        out_shape=[wide, wide, wide, jax.ShapeDtypeStruct((8, width), F), jax.ShapeDtypeStruct((docs, slots, width), BF)],
        scratch_shapes=[
            pltpu.VMEM((docs, slots, width), F),
            pltpu.VMEM((3, width, QUAD), F),
        ],
        compiler_params=pltpu.CompilerParams(vmem_limit_bytes=LIMIT),
    )(seg_lengths, alignment, q, k, v, att, gatt, lse, low, gfirst, w0)


def at_slots(plan, step, slot):
    for (when, where), calls in plan.items():
        if where == slot:

            @pl.when(step == when)
            def _():
                for call in calls:
                    call()


def each(fn, *backs):
    return [functools.partial(fn, k) for k in backs]


TILE = 320
ATTEND = 6


def forward_fused_kernel(
    len_ref, tok_ref, al_ref, wq, wk, wv, wo, wi, s2, vp, *rest
):
    low_ref, q_ref, k_ref, v_ref, att_ref, lse_ref = rest[:6]
    hat_ref, inv_ref, norm_ref, act_ref, slope_ref, vec_ref, w0, w1, w2 = rest[6:15]
    (
        low_s, base_s, att_s, w0_s, w1_s, ib_s, cols_s, s0, s1, land0, land1, own0, own1, pair_sem, local, send, recv,
    ) = rest[15:]
    step = pl.program_id(0)
    width, ff = tok_ref.shape[2], wi.shape[1]
    place = Place()
    pairs = [
        Pair(place, s0, land0, own0, pair_sem.at[0], pair_sem.at[1]),
        Pair(place, s1, land1, own1, pair_sem.at[2], pair_sem.at[3]),
    ]
    g0 = Gather(place, w0_s, own0, send.at[0], recv.at[0], local.at[0], w0.shape[2])
    g1 = Gather(place, w1_s, own1, send.at[1], recv.at[1], local.at[1], w1.shape[2])
    g2 = Gather(place, w2, s2, send.at[2], recv.at[2], local.at[2])
    saves = [
        lambda: pltpu.make_async_copy(w0_s, w0, local.at[3]),
        lambda: pltpu.make_async_copy(w1_s, w1, local.at[4]),
    ]
    start_of = lambda k: lambda: saves[k]().start()
    wait_of = lambda k: lambda: saves[k]().wait()

    def pack():
        for i, ref in enumerate((wq, wk, wv)):
            s0[:, i * width : (i + 1) * width] = ref[...].astype(F)
        rows = jnp.concatenate([vp[:8], jnp.zeros((120, 128), F)], axis=0)
        s0[:, 3 * width : 3 * width + 128] = rows.T[:24]
        top = lax.broadcasted_iota(jnp.int32, (24, 1), 0) == 0
        s0[:, 3 * width + 128 :] = jnp.where(top, vp[8:9], 0.0)

    def pack_rest():
        s1[:, :width] = wo[...].astype(F)
        s1[:, width:] = wi[...].astype(F)

    def vectors():
        cols = w0_s[:, :, 3 * width : 3 * width + 128].reshape(width, 128).astype(F)
        vec_ref[...] = cols.T[:8]
        cols_s[...] = w0_s[:, :, 3 * width + 128 :].reshape(width, 128).astype(F)
        share = ff * 24 // width
        for d in range(width // 24):
            ib_s[:, d * share : (d + 1) * share] = cols_s[24 * d : 24 * d + 1, :share]

    attend_plan = {
        (0, -1): [
            pack, place.barrier, pairs[0].start, pack_rest, pairs[1].start, pairs[0].done, g0.along_z,
            functools.partial(g0.to_neighbours, 0), pairs[1].done,
        ],
        (0, 0): [
            *each(g0.to_neighbours, 1), *each(g0.to_diagonal, 0), *each(g0.to_neighbours, 2), *each(g0.to_diagonal, 1),
            *each(g0.to_neighbours, 3), g1.along_z, *each(g0.to_core, 0), *each(g0.to_diagonal, 2),
            *each(g1.to_neighbours, 0), *each(g0.to_core, 1), *each(g0.to_diagonal, 3), *each(g0.to_core, 2, 3),
            *each(g1.to_neighbours, 1), g0.finish, start_of(0), vectors,
        ],
        (0, 1): [*each(g1.to_diagonal, 0), *each(g1.to_neighbours, 2)],
        (0, 2): each(g1.to_diagonal, 1),
        (0, 4): each(g1.to_neighbours, 3),
        (1, 1): each(g1.to_diagonal, 2),
        (1, 2): each(g1.to_core, 0),
        (1, 4): [*each(g1.to_diagonal, 3), *each(g1.to_core, 1)],
        (2, 2): each(g1.to_core, 2),
        (2, 4): [g2.along_z, *each(g1.to_core, 3)],
        (3, 1): each(g2.to_neighbours, 0),
        (3, 3): each(g2.to_neighbours, 1),
        (4, 1): [*each(g2.to_neighbours, 2), *each(g2.to_diagonal, 0)],
        (4, 3): each(g2.to_diagonal, 1),
        (5, 1): each(g2.to_neighbours, 3),
        (5, 3): each(g2.to_diagonal, 2),
    }
    mlp_plan = {
        (6, 0): [g1.finish, start_of(1)],
        (6, 1): each(g2.to_core, 0),
        (6, 3): each(g2.to_core, 1),
        (7, 1): each(g2.to_diagonal, 3),
        (7, 3): each(g2.to_core, 2),
        (8, 1): each(g2.to_core, 3),
        (9, 5): [g2.finish, wait_of(0), wait_of(1), g0.drain, g1.drain, g2.drain],
    }

    @pl.when(step < ATTEND)
    def _():
        at_slots(attend_plan, step, -1)
        b, j = step // 3, step % 3
        outs = (base_s.at[pl.ds(b, 1)], low_ref, q_ref, k_ref, v_ref, att_ref, lse_ref)
        w_cols = lambda cols: w0_s[:, :, cols].reshape(width, QUAD)
        hook = functools.partial(at_slots, attend_plan, step)
        forward_body(b, j, len_ref, tok_ref, al_ref, w_cols, vec_ref, outs, low_s, hook)
        att_s[b, :, pl.ds(pl.multiple_of(j * QUAD, QUAD), QUAD)] = att_ref[0]

    @pl.when(step >= ATTEND)
    def _():
        hook = functools.partial(at_slots, mlp_plan, step)
        hook(0)
        t = step - ATTEND
        rows = pl.ds(pl.multiple_of((t % 2) * TILE, TILE), TILE)

        def put(kind, *got):
            if kind == "norm":
                hat_ref[...] = got[0]
                inv_ref[...] = jnp.broadcast_to(got[1], inv_ref.shape)
                norm_ref[...] = got[2]
            else:
                act_ref[:, got[0]], slope_ref[:, got[0]] = got[1:]

        w_out = lambda: w1_s[:, :, :width].reshape(width, width)
        w_in = lambda c, n: w1_s[:, :, width + c : width + c + n].reshape(width, n)
        vec = lambda k: vec_ref[k : k + 1, :]
        mlp_first(att_s[t // 2, rows], base_s[t // 2, rows], w_out, w_in, vec, ib_s[...], put, hook=hook)
        hook(5)


def forward_fused(seg_lengths, tokens, alignment, wq, wk, wv, wo, wi, s2, vp):
    docs, slots, width = tokens.shape
    ff = wi.shape[1]
    quads = width // QUAD
    n0, n1 = 3 * width + 256, width + ff
    total = docs * slots
    last = ATTEND - 1
    doc_of = lambda s: jnp.minimum(s, last) // quads
    doc = pl.BlockSpec((1, slots, width), lambda s: (doc_of(s), 0, 0))
    quad = pl.BlockSpec((1, slots, QUAD), lambda s: (doc_of(s), 0, jnp.minimum(s, last) % quads))
    wide = jax.ShapeDtypeStruct((docs, slots, width), BF)
    full = lambda *shape: once(shape, lambda s: (0,) * len(shape))
    tile = lambda n: pl.BlockSpec((TILE, n), lambda s: (jnp.maximum(s - ATTEND, 0), 0))
    ins = (alignment, wq, wk, wv, wo, wi, s2, vp)
    return pl.pallas_call(
        forward_fused_kernel,
        grid=(ATTEND + total // TILE,),
        in_specs=[SMEM, doc] + [full(*a.shape) for a in ins],
        out_specs=[
            doc, quad, quad, quad, quad,
            pl.BlockSpec((1, 1, 8, slots), lambda s: (doc_of(s), jnp.minimum(s, last) % quads, 0, 0)),
            tile(width), tile(128), tile(width), tile(ff), tile(ff), full(8, width),
        ]
        + [ANY] * 3,
        out_shape=[
            wide,
            wide,
            wide,
            wide,
            wide,
            jax.ShapeDtypeStruct((docs, quads, 8, slots), F),
            jax.ShapeDtypeStruct((total, width), F),
            jax.ShapeDtypeStruct((total, 128), F),
            jax.ShapeDtypeStruct((total, width), BF),
            jax.ShapeDtypeStruct((total, ff), BF),
            jax.ShapeDtypeStruct((total, ff), BF),
            jax.ShapeDtypeStruct((8, width), F),
            jax.ShapeDtypeStruct((CHIPS, 48, n0), BF),
            jax.ShapeDtypeStruct((CHIPS, 48, n1), BF),
            jax.ShapeDtypeStruct((CHIPS, 2, 96, width), BF),
        ],
        scratch_shapes=[
            pltpu.VMEM((slots, width), BF),
            pltpu.VMEM((docs, slots, width), F),
            pltpu.VMEM((docs, slots, width), BF),
            pltpu.VMEM((CHIPS, 48, n0), BF),
            pltpu.VMEM((CHIPS, 48, n1), BF),
            pltpu.VMEM((1, ff), F),
            pltpu.VMEM((width, 128), F),
            pltpu.VMEM((24, n0), F),
            pltpu.VMEM((24, n1), F),
            pltpu.VMEM((24, n0 // 2), F),
            pltpu.VMEM((24, n1 // 2), F),
            pltpu.VMEM((48, n0 // 2), BF),
            pltpu.VMEM((48, n1 // 2), BF),
            pltpu.SemaphoreType.DMA((4,)),
            pltpu.SemaphoreType.DMA((5,)),
            pltpu.SemaphoreType.DMA((3, Gather.SEMS)),
            pltpu.SemaphoreType.DMA((3, Gather.SEMS)),
        ],
        compiler_params=pltpu.CompilerParams(collective_id=0, has_side_effects=True, vmem_limit_bytes=LIMIT),
    )(seg_lengths, tokens, *ins)


def middle_kernel(hat_ref, inv_ref, cot_ref, vec_ref, *rest):
    act_h, slope_h, norm_h, att_h, w1_h, w2_h = rest[:6]
    enc_ref, gf_ref, ga_ref, g1_ref, gv_ref, gib_ref, o_outer = rest[6:13]
    act_s, slope_s, w1_s, w2_s, gsec_s, gmlp_s, g2_s = rest[13:20]
    bufs = rest[20:27]
    load_sem, local, send, recv = rest[27:]
    i = pl.program_id(0)
    rows, width = hat_ref.shape
    norm_s, att_s, gbr_s = (act_s.at[:, pl.ds(k * width, width)] for k in range(3))
    tiles = act_s.shape[0] // rows
    place = Place()
    g2 = Scatter(place, g2_s, bufs, o_outer, send.at[0], recv.at[0], local.at[0])

    cut = lambda t: pl.ds(t * rows, rows)
    loads = [lambda: pltpu.make_async_copy(w2_h, w2_s, load_sem.at[0])]
    for t in range(tiles):
        loads.append(lambda t=t: pltpu.make_async_copy(act_h.at[cut(t)], act_s.at[cut(t)], load_sem.at[1 + t]))
    for t in range(tiles):
        loads.append(lambda t=t: pltpu.make_async_copy(slope_h.at[cut(t)], slope_s.at[cut(t)], load_sem.at[5 + t]))
    loads += [
        lambda: pltpu.make_async_copy(w1_h, w1_s, load_sem.at[9]),
        lambda: pltpu.make_async_copy(norm_h, norm_s, load_sem.at[10]),
        lambda: pltpu.make_async_copy(att_h, att_s, load_sem.at[11]),
    ]
    wait = lambda k: lambda: loads[k]().wait()
    loads_start = lambda k: lambda: loads[k]().start()

    def begin():
        for load in loads[:2]:
            load().start()
        gv_ref[...] = jnp.zeros_like(gv_ref)
        gib_ref[...] = jnp.zeros_like(gib_ref)
        place.barrier()

    plan = {
        (0, 0): [begin, wait(0), wait(1), *map(loads_start, (2, 3, 4))],
        (1, 0): [wait(2), *map(loads_start, (9, 5))],
        (2, 0): [wait(3), *map(loads_start, (6, 7, 8))],
        (3, 0): [wait(4)],
        (4, 2): each(g2.from_sibling, 3),
        (5, 2): each(g2.from_sibling, 2),
        (6, 2): each(g2.from_sibling, 1),
        (7, 2): each(g2.from_sibling, 0),
        (6, 0): each(g2.to_diagonal, 3),
        (7, 0): each(g2.to_diagonal, 2),
        (8, 0): [loads_start(10), loads_start(11), wait(9), wait(5), *each(g2.to_diagonal, 1)],
        (8, 1): [*each(g2.to_diagonal, 0), *each(g2.to_neighbours, 3)],
        (8, 2): each(g2.to_neighbours, 2),
        (9, 0): [wait(6)],
        (9, 1): each(g2.to_neighbours, 1),
        (9, 2): each(g2.to_neighbours, 0),
        (10, 0): [wait(7)],
        (10, 1): each(g2.along_z, 3),
        (10, 2): each(g2.along_z, 2),
        (11, 0): [wait(8)],
        (11, 2): each(g2.along_z, 1),
        (12, 0): [wait(10)],
        (12, 2): each(g2.along_z, 0),
        (16, 0): [wait(11)],
        (16, 2): [g2.owner, g2.drain],
    }
    hook = functools.partial(at_slots, plan, i)
    hook(0)
    vec = lambda k: vec_ref[k : k + 1, :]
    w_outer = lambda c, n: w2_s[c * CHIPS // act_s.shape[1] : (c + n) * CHIPS // act_s.shape[1]].reshape(n, width)

    @pl.when(i < tiles)
    def _():
        at = pl.ds(pl.multiple_of(i * rows, rows), rows)
        enc_ref[...], grad_second, sums = mlp_second(hat_ref[...], act_s[at], w_outer, cot_ref[...], vec)
        gsec_s[at] = grad_second
        gmlp = grad_second.astype(BF)
        gmlp_s[at] = gmlp
        gv_ref[5:6] += col_sum(gmlp.astype(F))
        gv_ref[6:7] += sums[0]
        gv_ref[7:8] += sums[1]

    @pl.when((i >= tiles) & (i < 2 * tiles))
    def _():
        plane = place.plane(2 * tiles - 1 - i)
        cols = pl.ds(pl.multiple_of(plane * width, width), width)
        g2_s[pl.ds(4 * plane, 4)] = dot(act_s[:, cols], gmlp_s[...], TN).astype(BF).reshape(4, 2, 96, width)

    @pl.when((i >= 2 * tiles) & (i < 3 * tiles))
    def _():
        at = pl.ds(pl.multiple_of((i - 2 * tiles) * rows, rows), rows)

        def put(kind, *got):
            if kind == "pre":
                slope_s[at, got[0]] = got[1]
                gib_ref[:, got[0]] += col_sum(got[1].astype(F))
            else:
                gf_ref[...], gbr_s[at] = got[:2]
                gv_ref[2:3] += col_sum(got[1].astype(F))
                gv_ref[3:4] += got[2]
                gv_ref[4:5] += got[3]

        w_out = lambda: w1_s[:, :, :width].reshape(width, width)
        w_in = lambda c, n: w1_s[:, :, width + c : width + c + n].reshape(width, n)
        ga_ref[...] = mlp_back(
            gsec_s[at], gmlp_s[at], hat_ref[...], inv_ref[:, 0:1], slope_s[at], w_outer, w_out, w_in, vec, put, hook=hook
        )

    @pl.when((i >= 3 * tiles) & (i < 4 * tiles))
    def _():
        cols = pl.ds(pl.multiple_of((i - 3 * tiles) * width, width), width)
        g1_ref[...] = dot(norm_s[...], slope_s[:, cols], TN).astype(BF)

    @pl.when(i == 4 * tiles)
    def _():
        g1_ref[...] = dot(att_s[...], gbr_s[...], TN).astype(BF)

    hook(2)


def middle(hat, inv, cotangent, vec, act, slope, norm, att, w1, w2):
    total, width = hat.shape
    ff = act.shape[1]
    tiles = total // TILE
    early = lambda n: pl.BlockSpec((TILE, n), lambda i: (jnp.minimum(i, tiles - 1), 0))
    late = lambda n: pl.BlockSpec((TILE, n), lambda i: (jnp.clip(i - 2 * tiles, 0, tiles - 1), 0))
    full = lambda *shape: once(shape, lambda i: (0,) * len(shape))
    return pl.pallas_call(
        middle_kernel,
        grid=(4 * tiles + 1,),
        in_specs=[
            pl.BlockSpec(
                (TILE, width),
                lambda i: (jnp.where(i < 2 * tiles, jnp.minimum(i, tiles - 1), jnp.minimum(i - 2 * tiles, tiles - 1)), 0),
            ),
            late(128),
            early(width),
            full(8, width),
        ]
        + [ANY] * 6,
        out_specs=[
            early(width),
            late(width),
            late(width),
            pl.BlockSpec((width, width), lambda i: (0, jnp.where(i == 4 * tiles, 0, jnp.clip(i - 3 * tiles, 0, 3) + 1))),
            full(8, width),
            full(1, ff),
            full(96, width),
        ],
        out_shape=[
            jax.ShapeDtypeStruct((total, width), BF),
            jax.ShapeDtypeStruct((total, width), F),
            jax.ShapeDtypeStruct((total, width), BF),
            jax.ShapeDtypeStruct((width, width + ff), BF),
            jax.ShapeDtypeStruct((8, width), F),
            jax.ShapeDtypeStruct((1, ff), F),
            jax.ShapeDtypeStruct((96, width), F),
        ],
        scratch_shapes=[
            pltpu.VMEM((total, ff), BF),
            pltpu.VMEM((total, ff), BF),
            pltpu.VMEM(w1.shape, BF),
            pltpu.VMEM(w2.shape, BF),
            pltpu.VMEM((total, width), F),
            pltpu.VMEM((total, width), BF),
            pltpu.VMEM(w2.shape, BF),
            *Scatter.scratch(96, width, False),
            pltpu.SemaphoreType.DMA((12,)),
            pltpu.SemaphoreType.DMA((1, 4)),
            pltpu.SemaphoreType.DMA((1, Scatter.SEMS)),
            pltpu.SemaphoreType.DMA((1, Scatter.SEMS)),
        ],
        compiler_params=pltpu.CompilerParams(collective_id=2, has_side_effects=True, vmem_limit_bytes=LIMIT),
    )(hat, inv, cotangent, vec, act, slope, norm, att, w1, w2)


def backward_fused_kernel(widths, *refs):
    ins, (gv_ref, gib_ref, g1_ref) = refs[:11], refs[11:14]
    gt_ref, o_wide, o_inner, o_vec, o_ib = refs[14], refs[15:19], refs[19], refs[20], refs[21]
    scratch, cols_s = refs[22:25], refs[25]
    rest = list(refs[26:])
    local, send, recv = rest[-3:]
    j, b = pl.program_id(0), pl.program_id(1)
    step = 2 * j + b
    width = ins[8].shape[2]
    place = Place()
    take = lambda n: [rest.pop(0) for _ in range(n)]
    quad_s, stage = take(3), take(1)[0]
    sources = [g1_ref, *quad_s]
    groups = []
    for i, (src, wide) in enumerate(zip(sources, widths)):
        out = stage.at[:, pl.ds(0, wide)]
        groups.append(Scatter(place, src, take(9), out, send.at[i], recv.at[i], local.at[i], wide))
    g1, q0, q1, q2 = groups

    def give_rest():
        g1.finish()
        o_wide[3][...] = stage[:, :width]
        o_inner[...] = stage[:, width : widths[0]]

    def give_quad(k):
        groups[1 + k].finish()
        for i in range(3):
            o_wide[i][:, k * QUAD : (k + 1) * QUAD] = stage[:, i * QUAD : (i + 1) * QUAD]
        if k == 2:
            o_vec[...] = stage[:, 3 * QUAD : 3 * QUAD + 128].T[:8]
            o_ib[...] = stage[0:1, 3 * QUAD + 128 : 4 * QUAD]

    def keep(grad):
        for k in range(3):

            @pl.when(j == k)
            def _():
                for i in range(3):
                    quad_s[k][:, :, i * QUAD : (i + 1) * QUAD] = grad(i).reshape(CHIPS, 48, QUAD)
                if k == 2:
                    both = vector_cols(scratch[2], gv_ref, gib_ref, cols_s)
                    quad_s[k][:, :, 3 * QUAD :] = both.reshape(CHIPS, 48, QUAD)

    late, soon = (3, 2), (1, 0)
    all4 = late + soon
    plan = {
        (0, 0): [place.barrier, *each(g1.from_sibling, *all4)],
        (0, 2): each(g1.to_diagonal, 3),
        (0, 4): each(g1.to_diagonal, 2, 1, 0),
        (1, 2): each(g1.to_neighbours, 3),
        (1, 4): [*each(g1.to_neighbours, 2, 1, 0), *each(q0.from_sibling, *all4)],
        (2, 2): each(g1.along_z, 3),
        (2, 4): [*each(g1.along_z, 2), *each(q0.to_diagonal, *all4)],
        (3, 2): each(g1.along_z, 1),
        (3, 4): [*each(g1.along_z, 0), *each(q0.to_neighbours, *all4), *each(q1.from_sibling, *all4)],
        (4, 2): each(q1.to_diagonal, *all4),
        (4, 4): [*each(q0.along_z, *all4), *each(q1.to_neighbours, *all4)],
        (5, 2): [g1.owner],
        (5, 4): [
            *each(q2.from_sibling, *all4), *each(q1.along_z, *all4), q0.owner, *each(q2.to_diagonal, *all4),
            give_rest, functools.partial(give_quad, 0), *each(q2.to_neighbours, *all4), q1.owner,
            *each(q2.along_z, *all4), functools.partial(give_quad, 1), q2.owner, functools.partial(give_quad, 2),
            *[g.drain for g in groups],
        ],
    }
    backward_body(j, b, ins, keep, gt_ref, scratch, functools.partial(at_slots, plan, step))


def backward_fused(seg_lengths, alignment, q, k, v, att, gatt, lse, low, gfirst, w0, gv, gib, g1):
    docs, slots, width = low.shape
    quads = width // QUAD
    quad = pl.BlockSpec((1, slots, QUAD), lambda j, b: (b, 0, j))
    doc = pl.BlockSpec((1, slots, width), lambda j, b: (b, 0, 0))
    whole = lambda *shape: once(shape, lambda j, b: (0,) * len(shape))
    n1 = g1.shape[2]
    widths = (n1, 3 * QUAD, 3 * QUAD, 4 * QUAD)
    bufs = []
    for wide in widths:
        bufs += Scatter.scratch(48, wide // 2, True)
    n = len(widths)
    shard = jax.ShapeDtypeStruct((24, width), F)
    return pl.pallas_call(
        functools.partial(backward_fused_kernel, widths),
        grid=(quads, docs),
        in_specs=[
            SMEM,
            whole(*alignment.shape),
            quad,
            quad,
            quad,
            quad,
            quad,
            pl.BlockSpec((1, 1, 8, slots), lambda j, b: (b, j, 0, 0)),
            doc,
            pl.BlockSpec((1, slots, width), lambda j, b: (jnp.where(j == 0, b, 1), 0, 0)),
            whole(*w0.shape),
            whole(*gv.shape),
            whole(*gib.shape),
            ANY,
        ],
        out_specs=[
            pl.BlockSpec((1, slots, width), lambda j, b: (jnp.where(j == quads - 1, b, 0), 0, 0)),
            *[whole(24, width)] * 4,
            whole(24, n1 - width),
            whole(8, 24),
            whole(1, 128),
        ],
        out_shape=[
            jax.ShapeDtypeStruct((docs, slots, width), BF),
            shard,
            shard,
            shard,
            shard,
            jax.ShapeDtypeStruct((24, n1 - width), F),
            jax.ShapeDtypeStruct((8, 24), F),
            jax.ShapeDtypeStruct((1, 128), F),
        ],
        scratch_shapes=[
            pltpu.VMEM((docs, slots, width), F),
            pltpu.VMEM((3, width, QUAD), F),
            pltpu.VMEM((8, width), F),
            pltpu.VMEM((width, 128), F),
            *[pltpu.VMEM((CHIPS, 48, wide), BF) for wide in widths[1:]],
            pltpu.VMEM((24, n1), F),
            *bufs,
            pltpu.SemaphoreType.DMA((n, 4)),
            pltpu.SemaphoreType.DMA((n, Scatter.SEMS)),
            pltpu.SemaphoreType.DMA((n, Scatter.SEMS)),
        ],
        compiler_params=pltpu.CompilerParams(collective_id=1, has_side_effects=True, vmem_limit_bytes=LIMIT),
    )(seg_lengths, alignment, q, k, v, att, gatt, lse, low, gfirst, w0, gv, gib, g1)


def own_kernels(shard_rows, docs):
    return lax.axis_size("dp") == PLANES and lax.axis_size("fsdp") == 8 and shard_rows == 24 and docs == 2


def shards(
    tokens, cotangent, seg_lengths, alignment, query_weight, query_bias, key_weight, value_weight, value_bias,
    out_weight, out_bias, first_gain, first_shift, inner_weight, inner_bias, outer_weight, outer_bias, second_gain,
    second_shift,
):
    docs, slots, width = tokens.shape
    rows = query_weight.shape[0]
    every = ("dp", "fsdp")
    vectors = (query_bias, value_bias, out_bias, first_gain, first_shift, outer_bias, second_gain, second_shift)
    weights = (query_weight, key_weight, value_weight, out_weight, inner_weight, outer_weight)
    flat = lambda t: t.reshape(docs * slots, width)
    whole = lambda t: t.reshape(docs, slots, width)
    if own_kernels(rows, docs):
        wide = lambda t: jnp.pad(t.astype(F), ((0, 128 - t.shape[0]),))
        packed = jnp.stack([wide(t) for t in (*vectors, inner_bias)] + [jnp.zeros((128,), F)] * 7)
        low, q, k, v, att, lse, hat, inv, norm, act, slope, vec, w0, w1, w2 = forward_fused(
            seg_lengths, tokens, alignment, *weights, packed
        )
        encoded, gfirst, gatt, g1, gvec, ginner, gouter = middle(
            hat, inv, flat(cotangent), vec, act, slope, norm, flat(att), w1, w2
        )
        grad_tokens, gq, gk, gv, gout, ginn, sums, gib = backward_fused(
            seg_lengths, alignment, q, k, v, att, whole(gatt), lse, low, whole(gfirst), w0.reshape(width, -1), gvec,
            ginner, g1.reshape(CHIPS, 48, -1),
        )
        sums, gib = tuple(sums[i] for i in range(8)), gib[0, : inner_bias.shape[0]]
    else:
        gather = lambda s: lax.all_gather(s, every, axis=0, tiled=True)
        owned = lambda g: lax.psum_scatter(g.astype(F), every, scatter_dimension=0, tiled=True)
        wq, wk, wv, wo, wi, w2 = (gather(w) for w in weights)
        w0, w1 = jnp.concatenate([wq, wk, wv], axis=1), jnp.concatenate([wo, wi], axis=1)
        vec = jnp.stack([gather(t).astype(F) for t in vectors])
        inner_row = gather(inner_bias).astype(F)[None]
        base, low, q, k, v, att, lse = forward_attention(seg_lengths, tokens, alignment, w0, vec)
        encoded, gfirst, gatt, g1, g2, gvec, ginner = mlp_both(
            flat(att), flat(base), flat(cotangent), w1, w2, vec, inner_row
        )
        gq, gk, gv, two, grad_tokens = backward_attention(
            seg_lengths, alignment, q, k, v, att, whole(gatt), lse, low, whole(gfirst), w0
        )
        gq, gk, gv, g1, gouter = (owned(g) for g in (gq, gk, gv, g1, g2))
        gout, ginn = g1[:, :width], g1[:, width:]
        sums = tuple(owned(two[i] if i < 2 else gvec[i]) for i in range(8))
        gib = owned(ginner[0])
    return (
        whole(encoded), grad_tokens, gq, sums[0], gk, gv, sums[1], gout, sums[2], sums[3], sums[4], ginn, gib, gouter,
        sums[5], sums[6], sums[7],
    )


def solution(mesh):
    in_specs = (
        P(("dp", "fsdp"), None, None),
        P(("dp", "fsdp"), None, None),
        P(("dp", "fsdp")),
        P(("dp", "fsdp"), None),
        P(("dp", "fsdp"), None),
        P(("dp", "fsdp")),
        P(("dp", "fsdp"), None),
        P(("dp", "fsdp"), None),
        P(("dp", "fsdp")),
        P(("dp", "fsdp"), None),
        P(("dp", "fsdp")),
        P(("dp", "fsdp")),
        P(("dp", "fsdp")),
        P(("dp", "fsdp"), None),
        P(("dp", "fsdp")),
        P(("dp", "fsdp"), None),
        P(("dp", "fsdp")),
        P(("dp", "fsdp")),
        P(("dp", "fsdp")),
    )
    out_specs = (
        P(("dp", "fsdp"), None, None),
        P(("dp", "fsdp"), None, None),
        P(("dp", "fsdp"), None),
        P(("dp", "fsdp")),
        P(("dp", "fsdp"), None),
        P(("dp", "fsdp"), None),
        P(("dp", "fsdp")),
        P(("dp", "fsdp"), None),
        P(("dp", "fsdp")),
        P(("dp", "fsdp")),
        P(("dp", "fsdp")),
        P(("dp", "fsdp"), None),
        P(("dp", "fsdp")),
        P(("dp", "fsdp"), None),
        P(("dp", "fsdp")),
        P(("dp", "fsdp")),
        P(("dp", "fsdp")),
    )
    return jax.shard_map(shards, mesh=mesh, in_specs=in_specs, out_specs=out_specs, check_vma=False)
```

```python
import functools
import jax
import jax.numpy as jnp
from jax import lax
from jax.experimental import pallas as pl
from jax.experimental.pallas import tpu as pltpu
from jax.sharding import PartitionSpec as P

MESH = pl.DeviceIdType.MESH
ANY = pl.BlockSpec(memory_space=pl.ANY)
VMEM = pl.BlockSpec(memory_space=pltpu.VMEM)
PLANES = 4
CHIPS = 16


class Place:
    def __init__(self):
        self.z = lax.axis_index("dp")
        self.f = lax.axis_index("fsdp")
        self.core = self.f % 2
        self.x = (self.f // 2) % 2
        self.y = self.f // 4
        self.sib = self.f + 1 - 2 * self.core
        self.xn = self.f + 2 - 4 * self.x
        self.yn = self.f + 4 - 8 * self.y
        self.spot = self.f // 2
        self.spot_x = self.xn // 2
        self.spot_y = self.yn // 2
        self.spot_d = 3 - self.spot

    def plane(self, back):
        return (self.z + PLANES - back) % PLANES

    def coming(self, k):
        return (self.z, 1 + self.z % 2, (self.z + 2) % PLANES, 3 * ((self.z + 1) % 2))[k]

    def ahead(self, step):
        return (self.z + step) % PLANES

    def barrier(self):
        bar = pltpu.get_barrier_semaphore()
        for other in self.partners():
            pl.semaphore_signal(bar, inc=1, device_id=other, device_id_type=MESH)
        pl.semaphore_wait(bar, 3 + PLANES - 1)

    def partners(self):
        return [(self.z, self.sib), (self.z, self.xn), (self.z, self.yn)] + [
            (self.ahead(k), self.f) for k in range(1, PLANES)
        ]


def remote(src, dst, send, recv, dev):
    return pltpu.make_async_remote_copy(
        src_ref=src, dst_ref=dst, send_sem=send, recv_sem=recv, device_id=dev, device_id_type=MESH
    )


class Gather:
    SEMS = 29

    def __init__(self, place, full, own, send, recv, local, width=None):
        self.p, self.full, self.own = place, full, own
        self.send, self.recv, self.local = send, recv, local
        self.half = None if width is None else width // 2
        self.rows = own.shape[0]
        self.started = []

    def view(self, chip, r0=0, r1=None, core=None):
        core = self.p.core if core is None else core
        r1 = self.rows if r1 is None else r1
        if self.half is None:
            return self.full.at[chip, core, pl.ds(r0, r1 - r0), :]
        cols = pl.ds(pl.multiple_of(core * self.half, 128), self.half)
        return self.full.at[chip, pl.ds(r0, r1 - r0), cols]

    def block(self, plane, core):
        if self.half is None:
            return self.full.at[pl.ds(4 * plane, 4), core]
        cols = pl.ds(pl.multiple_of(core * self.half, 128), self.half)
        return self.full.at[pl.ds(4 * plane, 4), :, cols]

    def cut(self, k):
        if self.rows == 96:
            return 48
        return 32 if k % 2 == 0 else 16

    def copy(self, src, dst, index, dev, send=None):
        return remote(src, dst, self.send.at[index if send is None else send], self.recv.at[index], dev)

    def start(self, make, when=None):
        if when is None:
            make().start()
        else:
            pl.when(when())(lambda: make().start())
        self.started.append((make, when))

    def drain(self):
        for make, when in self.started:
            if when is None:
                make().wait_send()
            else:
                pl.when(when())(lambda: make().wait_send())

    def chip(self, k, spot):
        return 4 * self.p.coming(k) + spot

    def own_copy(self):
        return pltpu.make_async_copy(self.own, self.view(self.chip(0, self.p.spot)), self.local)

    def along_z(self):
        p = self.p
        mine = lambda: self.view(self.chip(0, p.spot))
        self.own_copy().start()
        self.start(lambda: self.copy(self.own, mine(), p.z, (p.z - 1, p.f), 24), lambda: p.z > 0)
        self.start(lambda: self.copy(self.own, mine(), p.z, (p.z + 1, p.f), 25), lambda: p.z < PLANES - 1)

    def onward(self, k, when=None):
        p = self.p
        piece = lambda: self.view(self.chip(k, p.spot))
        goal = lambda: p.z + jnp.where(p.coming(k) < p.z, 1, -1)
        goes = lambda: (goal() >= 0) & (goal() < PLANES)
        wait = lambda: self.copy(piece(), piece(), p.coming(k), (p.z, p.f)).wait_recv()
        both = goes if when is None else lambda: when() & goes()
        if when is None:
            wait()
        else:
            pl.when(when())(wait)
        self.start(lambda: self.copy(piece(), piece(), p.coming(k), (goal(), p.f), 25 + k), both)

    def to_neighbours(self, k):
        p = self.p
        piece = lambda: self.view(self.chip(k, p.spot))
        middle = lambda: p.z % 3 != 0
        if k == 1:
            self.onward(1)
            self.onward(3, middle)
        elif k == 2:
            self.onward(2)
        elif k == 3:
            self.onward(3, lambda: p.z % 3 == 0)
        src = piece if k else lambda: self.own
        self.start(lambda: self.copy(src(), piece(), 4 + k, (p.z, p.xn)))
        self.start(lambda: self.copy(src(), piece(), 8 + k, (p.z, p.yn)))

    def to_diagonal(self, k):
        p, cut = self.p, self.cut(k)
        cx, cy = lambda: self.chip(k, p.spot_x), lambda: self.chip(k, p.spot_y)
        full_x, full_y = self.view(cx()), self.view(cy())
        self.copy(full_x, full_x, 4 + k, (p.z, p.xn)).wait_recv()
        part_x = lambda: self.view(cx(), 0, cut)
        self.start(lambda: self.copy(part_x(), part_x(), 12 + k, (p.z, p.yn)))
        self.copy(full_y, full_y, 8 + k, (p.z, p.yn)).wait_recv()
        part_y = lambda: self.view(cy(), cut, self.rows)
        self.start(lambda: self.copy(part_y(), part_y(), 16 + k, (p.z, p.xn)))

    def to_core(self, k):
        p, cut = self.p, self.cut(k)
        cd = self.chip(k, p.spot_d)
        a, b = self.view(cd, 0, cut), self.view(cd, cut, self.rows)
        self.copy(a, a, 12 + k, (p.z, p.yn)).wait_recv()
        self.copy(b, b, 16 + k, (p.z, p.xn)).wait_recv()
        if k == 0:
            self.own_copy().wait()
        blk = lambda: self.block(p.coming(k), p.core)
        self.start(lambda: self.copy(blk(), blk(), 20 + k, (p.z, p.sib)))

    def finish(self):
        p = self.p
        for k in range(PLANES):
            blk = self.block(p.coming(k), 1 - p.core)
            self.copy(blk, blk, 20 + k, (p.z, p.sib)).wait_recv()


def build_own(place, shard, land, own):
    half = own.shape[1]
    first = place.core == 0
    for c0 in range(0, half, 128):
        mine = shard[:, pl.ds(pl.multiple_of(place.core * half + c0, 128), 128)]
        other = land[:, c0 : c0 + 128]
        top = jnp.where(first, mine, other)
        bottom = jnp.where(first, other, mine)
        own[:, c0 : c0 + 128] = jnp.concatenate([top, bottom], axis=0).astype(own.dtype)


class Pair:
    def __init__(self, place, shard, land, own, send, recv):
        half = own.shape[1]
        src = lambda: shard.at[:, pl.ds(pl.multiple_of((1 - place.core) * half, 128), half)]
        self.c = lambda: remote(src(), land, send, recv, (place.z, place.sib))
        self.args = (place, shard, land, own)

    def start(self):
        self.c().start()

    def done(self):
        self.c().wait()
        build_own(*self.args)


class Scatter:
    SEMS = 4 + 4 + 4 + 4 + 4 + 3 + 1

    def __init__(self, place, full, bufs, out, send, recv, local, width=None):
        self.p, self.full, self.out = place, full, out
        self.sums, self.from_core, self.la, self.lb, self.lx, self.ly, self.lz = bufs[:7]
        if width is not None:
            self.total, self.last = bufs[7:]
        self.send, self.recv, self.local = send, recv, local
        self.half = None if width is None else width // 2
        self.rows = self.sums.shape[1]
        self.started = []

    @staticmethod
    def scratch(rows, cols, two_rows):
        bf = jnp.bfloat16
        shapes = [
            pltpu.VMEM((CHIPS, rows, cols), bf),
            pltpu.VMEM((CHIPS, rows, cols), bf),
            pltpu.VMEM((4, rows - 16, cols), bf),
            pltpu.VMEM((4, rows - 16, cols), bf),
            pltpu.VMEM((4, rows, cols), bf),
            pltpu.VMEM((4, rows, cols), bf),
            pltpu.VMEM((3, rows, cols), bf),
        ]
        if two_rows:
            shapes += [pltpu.VMEM((rows, cols), jnp.float32), pltpu.VMEM((rows // 2, cols), jnp.float32)]
        return shapes

    def chip(self, back, spot):
        return 4 * self.p.plane(back) + spot

    cut = Gather.cut
    copy = Gather.copy
    start = Gather.start
    drain = Gather.drain
    block = Gather.block

    def from_sibling(self, back):
        p = self.p
        blk = lambda: pl.ds(4 * p.plane(back), 4)
        c = pltpu.make_async_copy(self.block(p.plane(back), p.core), self.sums.at[blk()], self.local.at[back])
        c.start()
        self.start(
            lambda: self.copy(
                self.block(p.plane(back), 1 - p.core), self.from_core.at[blk()], back, (p.z, p.sib)
            )
        )

    def to_diagonal(self, back):
        p, cut, rows = self.p, self.cut(back), self.rows
        blk = pl.ds(4 * p.plane(back), 4)
        pltpu.make_async_copy(self.block(p.plane(back), p.core), self.sums.at[blk], self.local.at[back]).wait()
        self.copy(self.from_core.at[blk], self.from_core.at[blk], back, (p.z, p.sib)).wait_recv()
        for j in range(4):
            at = 4 * p.plane(back) + j
            self.sums[at] = self.sums[at] + self.from_core[at]
        cd = lambda: self.chip(back, p.spot_d)
        self.start(
            lambda: self.copy(
                self.sums.at[cd(), pl.ds(0, cut)], self.la.at[back, pl.ds(0, cut)], 4 + back, (p.z, p.xn)
            )
        )
        self.start(
            lambda: self.copy(
                self.sums.at[cd(), pl.ds(cut, rows - cut)],
                self.lb.at[back, pl.ds(0, rows - cut)],
                8 + back,
                (p.z, p.yn),
            )
        )

    def to_neighbours(self, back):
        p, cut, rows = self.p, self.cut(back), self.rows
        cx, cy = self.chip(back, p.spot_x), self.chip(back, p.spot_y)
        a, b = self.la.at[back, pl.ds(0, cut)], self.lb.at[back, pl.ds(0, rows - cut)]
        self.copy(a, a, 4 + back, (p.z, p.xn)).wait_recv()
        self.sums[cy, 0:cut] = self.sums[cy, 0:cut] + a[...]
        to_y = lambda: self.sums.at[self.chip(back, p.spot_y)]
        self.start(lambda: self.copy(to_y(), self.ly.at[back], 16 + back, (p.z, p.yn)))
        self.copy(b, b, 8 + back, (p.z, p.yn)).wait_recv()
        self.sums[cx, cut:rows] = self.sums[cx, cut:rows] + b[...]
        to_x = lambda: self.sums.at[self.chip(back, p.spot_x)]
        self.start(lambda: self.copy(to_x(), self.lx.at[back], 12 + back, (p.z, p.xn)))

    def along_z(self, back):
        p = self.p
        c0 = self.chip(back, p.spot)
        lx, ly = self.lx.at[back], self.ly.at[back]
        self.copy(lx, lx, 12 + back, (p.z, p.xn)).wait_recv()
        self.copy(ly, ly, 16 + back, (p.z, p.yn)).wait_recv()
        f = jnp.float32
        got = self.sums[c0].astype(f) + lx[...].astype(f) + ly[...].astype(f)
        self.sums[c0] = got.astype(jnp.bfloat16)
        if back:
            mine = lambda: self.sums.at[self.chip(back, p.spot)]
            self.start(lambda: self.copy(mine(), self.lz.at[back - 1], 20 + back - 1, (p.plane(back), p.f)))

    def owner(self):
        p = self.p
        f = jnp.float32
        for k in range(3):
            self.copy(self.lz.at[k], self.lz.at[k], 20 + k, (p.z, p.f)).wait_recv()
        c0 = self.chip(0, p.spot)
        total = self.sums[c0].astype(f)
        for k in range(3):
            total = total + self.lz[k].astype(f)
        if self.half is None:
            self.out[...] = total
            return
        self.total[...] = total
        rows = self.rows // 2
        theirs = lambda: self.total.at[pl.ds(pl.multiple_of((1 - p.core) * rows, 8), rows)]
        self.start(lambda: self.copy(theirs(), self.last, 23, (p.z, p.sib)))

    def finish(self):
        if self.half is None:
            return
        p, half = self.p, self.half
        rows = self.rows // 2
        self.copy(self.last, self.last, 23, (p.z, p.sib)).wait_recv()
        mine = pl.ds(pl.multiple_of(p.core * rows, 8), rows)
        self.out[:, pl.ds(pl.multiple_of(p.core * half, 128), half)] = self.total[mine]
        self.out[:, pl.ds(pl.multiple_of((1 - p.core) * half, 128), half)] = self.last[...]


F = jnp.float32
BF = jnp.bfloat16
NN = (((1,), (0,)), ((), ()))
NT = (((1,), (1,)), ((), ()))
TN = (((0,), (0,)), ((), ()))
SMEM = pl.BlockSpec(memory_space=pltpu.SMEM)
HEADS = 12
HEAD_DIM = 64
QUAD = 4 * HEAD_DIM
scale = HEAD_DIM**-0.5
norm_eps = 1e-05
masked_score = -1000000000.0
LIMIT = 60 * 2**20


def dot(left, right, dims):
    return lax.dot_general(left, right, dims, preferred_element_type=F)


def once(shape, index):
    return pl.BlockSpec(shape, index, pipeline_mode=pl.Buffered(1))


def key_bias(count):
    row = lax.broadcasted_iota(jnp.int32, (128, 1), 0)
    return jnp.where(row < count, 0.0, masked_score).astype(F)


def masked(scores, text, bias):
    return jnp.concatenate([scores[:text], scores[text:] + bias], axis=0)


def head_lanes(h):
    lane = lax.broadcasted_iota(jnp.int32, (1, 128), 1)
    return (lane < HEAD_DIM) if h == 0 else (lane >= HEAD_DIM)


def pair_forward(q2, k2, v2, text, bias, between):
    vt = v2.T
    outs, logs = [], []
    for h in range(2):
        qh = jnp.where(head_lanes(h), q2, BF(0))
        scores = masked(dot(k2, qh, NT), text, bias)
        top = jnp.max(scores, axis=0, keepdims=True)
        expo = jnp.exp(scores - top)
        total = jnp.sum(expo, axis=0, keepdims=True)
        outs.append(dot(vt[HEAD_DIM * h : HEAD_DIM * (h + 1)], expo.astype(BF), NN) * (1.0 / total))
        logs.append(top + jnp.log(total))
        if h == 0:
            between()
    return jnp.concatenate(outs, axis=0).T.astype(BF), logs


def pair_backward(q2, k2, v2, o2, do2, logs, text, bias, between):
    prod = (do2.astype(F) * o2.astype(F)).T
    kt = (k2 * BF(scale)).T
    dq, dk, dv = [], [], []
    for h in range(2):
        rows = slice(HEAD_DIM * h, HEAD_DIM * (h + 1))
        qh = jnp.where(head_lanes(h), q2, BF(0))
        doh = jnp.where(head_lanes(h), do2, BF(0))
        delta = jnp.sum(prod[rows], axis=0, keepdims=True)
        probs = jnp.exp(masked(dot(k2, qh, NT), text, bias) - logs[h])
        grads = (probs * (dot(v2, doh, NT) - delta)).astype(BF)
        dv.append(dot(probs.astype(BF), do2, NN))
        dk.append(dot(grads, q2, NN))
        dq.append(dot(kt[rows], grads, NN))
        if h == 0:
            between()
    first = head_lanes(0)
    return (
        jnp.concatenate(dq, axis=0).T.astype(BF),
        jnp.where(first, dk[0], dk[1]).astype(BF),
        jnp.where(first, dv[0], dv[1]).astype(BF),
    )


def member_of(align, segs):
    return (align == lax.broadcasted_iota(jnp.int32, (segs, align.shape[1]), 0)).astype(F)


def forward_body(b, j, len_ref, tok_ref, al_ref, w_cols, bias_ref, outs, low_s, hook=lambda at: None):
    base_ref, low_ref, q_ref, k_ref, v_ref, att_ref, lse_ref = outs
    text, width = al_ref.shape[1], tok_ref.shape[2]
    segs = tok_ref.shape[1] - text

    @pl.when(j == 0)
    def _():
        member = member_of(al_ref[pl.ds(b, 1), :], segs)
        counts = jnp.maximum(jnp.sum(member, axis=1, keepdims=True), 1.0)
        tok = tok_ref[0]
        pooled = dot(member.astype(BF), tok[:text], NN) / counts
        seg_base = tok[text:].astype(F) + pooled
        base_ref[0, :text] = tok[:text].astype(F)
        base_ref[0, text:] = seg_base
        low_ref[0, :text] = tok[:text]
        low_ref[0, text:] = seg_base.astype(BF)
        low_s[:text] = tok[:text]
        low_s[text:] = seg_base.astype(BF)

    hook(0)
    low = low_s[...]
    parts = []
    for i, ref in enumerate((q_ref, k_ref, v_ref)):
        at = i * width + j * QUAD
        rows = dot(low, w_cols(pl.ds(pl.multiple_of(at, QUAD), QUAD)), NN)
        if i != 1:
            rows = rows + bias_ref[i // 2 : i // 2 + 1, pl.ds(pl.multiple_of(j * QUAD, QUAD), QUAD)]
        rows = rows.astype(BF)
        if i == 0:
            rows = rows * BF(scale)
        ref[0] = rows
        parts.append(rows)
    bias = key_bias(len_ref[b])
    for pr in range(2):
        cols = slice(128 * pr, 128 * pr + 128)
        out, logs = pair_forward(parts[0][:, cols], parts[1][:, cols], parts[2][:, cols], text, bias, lambda: hook(1 + 2 * pr))
        att_ref[0, :, cols] = out
        for h in range(2):
            lse_ref[0, 0, 2 * pr + h : 2 * pr + h + 1, :] = logs[h]
        hook(2 + 2 * pr)


def forward_kernel(len_ref, tok_ref, al_ref, w_ref, bias_ref, *rest):
    w_cols = lambda cols: w_ref[:, cols]
    forward_body(pl.program_id(0), pl.program_id(1), len_ref, tok_ref, al_ref, w_cols, bias_ref, rest[:7], rest[7])


def forward_attention(seg_lengths, tokens, alignment, w0, biases):
    docs, slots, width = tokens.shape
    quads = width // QUAD
    doc = pl.BlockSpec((1, slots, width), lambda b, j: (b, 0, 0))
    quad = pl.BlockSpec((1, slots, QUAD), lambda b, j: (b, 0, j))
    wide = jax.ShapeDtypeStruct((docs, slots, width), BF)
    return pl.pallas_call(
        forward_kernel,
        grid=(docs, quads),
        in_specs=[
            SMEM,
            doc,
            once(alignment.shape, lambda b, j: (0, 0)),
            once(w0.shape, lambda b, j: (0, 0)),
            once(biases.shape, lambda b, j: (0, 0)),
        ],
        out_specs=[doc, doc, quad, quad, quad, quad, pl.BlockSpec((1, 1, 8, slots), lambda b, j: (b, j, 0, 0))],
        out_shape=[
            jax.ShapeDtypeStruct((docs, slots, width), F),
            wide,
            wide,
            wide,
            wide,
            wide,
            jax.ShapeDtypeStruct((docs, quads, 8, slots), F),
        ],
        scratch_shapes=[pltpu.VMEM((slots, width), BF)],
        compiler_params=pltpu.CompilerParams(vmem_limit_bytes=LIMIT),
    )(seg_lengths, tokens, alignment, w0, biases)


def normal_parts(pre):
    size = jnp.abs(pre)
    dens = jnp.exp(pre * pre * -0.5)
    t = 1.0 / (1.0 + (0.3275911 * 0.7071067811865476) * size)
    poly = t * (
        0.5 * 0.254829592
        + t * (0.5 * -0.284496736 + t * (0.5 * 1.421413741 + t * (0.5 * -1.453152027 + t * (0.5 * 1.061405429))))
    )
    tail = poly * dens
    return jnp.where(pre >= 0, 1.0 - tail, tail), dens * 0.3989422804014327


def norm_parts(values_in):
    mean = jnp.mean(values_in, axis=-1, keepdims=True)
    centred = values_in - mean
    inverse = lax.rsqrt(jnp.mean(centred * centred, axis=-1, keepdims=True) + norm_eps)
    return centred * inverse, inverse


def norm_back(grad_hat, hat, inverse):
    return inverse * (
        grad_hat
        - jnp.mean(grad_hat, axis=-1, keepdims=True)
        - hat * jnp.mean(grad_hat * hat, axis=-1, keepdims=True)
    )


def col_sum(values):
    return jnp.sum(values, axis=0, keepdims=True)


def mlp_norm(att, base, w_out, vec):
    first = base + dot(att, w_out(), NN) + vec(2)
    hat, inv = norm_parts(first)
    return hat, inv, (hat * vec(3) + vec(4)).astype(BF)


def mlp_units(low, w_in, inner_bias, put, first, ff_cut=768, hook=lambda at: None):
    chunks = inner_bias.shape[1] // ff_cut
    pre_of = lambda c: dot(low, w_in(first + c * ff_cut, ff_cut), NN) + inner_bias[:, c * ff_cut : (c + 1) * ff_cut]
    pre = pre_of(0)
    for c in range(chunks):
        later = pre_of(c + 1) if c + 1 < chunks else None
        phi, dens = normal_parts(pre)
        put(slice(c * ff_cut, (c + 1) * ff_cut), (pre * phi).astype(BF), (phi + pre * dens).astype(BF))
        pre = later
        hook(1 + c)


def mlp_second(hat1, act, w_outer, cot, vec, ff_cut=768):
    second = hat1 * vec(3) + vec(4) + vec(5)
    for c in range(act.shape[1] // ff_cut):
        second = second + dot(act[:, c * ff_cut : (c + 1) * ff_cut], w_outer(c * ff_cut, ff_cut), NN)
    hat, inv = norm_parts(second)
    grad_y = cot.astype(F)
    sums = (col_sum(grad_y * hat), col_sum(grad_y))
    return (hat * vec(6) + vec(7)).astype(BF), norm_back(grad_y * vec(6), hat, inv), sums


def mlp_back(grad_second, gmlp, hat1, inv1, slope, w_outer, w_out, w_in, vec, put, ff_cut=768, hook=lambda at: None):
    grad_normed = grad_second
    chunks = slope.shape[1] // ff_cut
    act_of = lambda c: dot(gmlp, w_outer(c * ff_cut, ff_cut), NT)
    gact = act_of(0)
    for c in range(chunks):
        later = act_of(c + 1) if c + 1 < chunks else None
        cols = slice(c * ff_cut, (c + 1) * ff_cut)
        gpre = (gact * slope[:, cols].astype(F)).astype(BF)
        put("pre", cols, gpre)
        grad_normed = grad_normed + dot(gpre, w_in(c * ff_cut, ff_cut), NT)
        gact = later
        if c == 1:
            hook(1)
    grad_first = norm_back(grad_normed * vec(3), hat1, inv1)
    low = grad_first.astype(BF)
    put("first", grad_first, low, col_sum(grad_normed * hat1), col_sum(grad_normed))
    return dot(low, w_out(), NT).astype(BF)


def mlp_kernel(
    tiles, att_ref, base_ref, cot_ref, w1_ref, w2_ref, vec_ref, ib_ref,
    enc_ref, gf_ref, ga_ref, g1_ref, g2_ref, gv_ref, gib_ref,
    att_s, norm_s, act_s, slope_s, gmlp_s, gpre_s, gbr_s,
):
    i = pl.program_id(0)
    rows, width = att_ref.shape

    @pl.when(i == 0)
    def _():
        gv_ref[...] = jnp.zeros_like(gv_ref)
        gib_ref[...] = jnp.zeros_like(gib_ref)

    @pl.when(i < tiles)
    def _():
        at = pl.ds(pl.multiple_of(i * rows, rows), rows)
        vec = lambda k: vec_ref[k : k + 1, :]
        w_out = lambda: w1_ref[:, :width]
        w_in = lambda c, n: w1_ref[:, width + c : width + c + n]
        w_outer = lambda c, n: w2_ref[c : c + n, :]

        def put_units(cols, act, slope):
            act_s[at, cols], slope_s[:, cols] = act, slope

        def put(kind, *got):
            if kind == "pre":
                gpre_s[at, got[0]] = got[1]
                gib_ref[:, got[0]] += col_sum(got[1].astype(F))
            else:
                gf_ref[...], gbr_s[at] = got[:2]
                gv_ref[2:3] += col_sum(got[1].astype(F))
                gv_ref[3:4] += got[2]
                gv_ref[4:5] += got[3]

        att_s[at] = att_ref[...]
        hat1, inv1, low = mlp_norm(att_ref[...], base_ref[...], w_out, vec)
        norm_s[at] = low
        mlp_units(low, w_in, ib_ref[...], put_units, 0)
        enc_ref[...], grad_second, sums = mlp_second(hat1, act_s[at], w_outer, cot_ref[...], vec)
        gmlp = grad_second.astype(BF)
        gmlp_s[at] = gmlp
        gv_ref[5:6] += col_sum(gmlp.astype(F))
        gv_ref[6:7] += sums[0]
        gv_ref[7:8] += sums[1]
        ga_ref[...] = mlp_back(
            grad_second, gmlp, hat1, inv1, slope_s[...], w_outer, w_out, w_in, vec, put
        )

    @pl.when((i >= tiles) & (i < tiles + 4))
    def _():
        cols = pl.ds(pl.multiple_of((i - tiles) * width, width), width)
        g2_ref[...] = dot(act_s[:, cols], gmlp_s[...], TN).astype(BF)

    @pl.when((i >= tiles + 4) & (i < tiles + 8))
    def _():
        cols = pl.ds(pl.multiple_of((i - tiles - 4) * width, width), width)
        g1_ref[...] = dot(norm_s[...], gpre_s[:, cols], TN).astype(BF)

    @pl.when(i == tiles + 8)
    def _():
        g1_ref[...] = dot(att_s[...], gbr_s[...], TN).astype(BF)


def mlp_both(attended, base, cotangent, w1, w2, vec, inner_bias, rows=320):
    total, width = attended.shape
    ff = inner_bias.shape[1]
    tiles = total // rows
    tile = pl.BlockSpec((rows, width), lambda i: (jnp.minimum(i, tiles - 1), 0))
    whole = lambda shape: once(shape, lambda i: (0, 0))
    return pl.pallas_call(
        functools.partial(mlp_kernel, tiles),
        grid=(tiles + 9,),
        in_specs=[tile, tile, tile, whole(w1.shape), whole(w2.shape), whole(vec.shape), whole(inner_bias.shape)],
        out_specs=[
            tile,
            tile,
            tile,
            pl.BlockSpec((width, width), lambda i: (0, jnp.where(i == tiles + 8, 0, jnp.clip(i - tiles - 4, 0, 3) + 1))),
            pl.BlockSpec((width, width), lambda i: (jnp.clip(i - tiles, 0, 3), 0)),
            whole((8, width)),
            whole((1, ff)),
        ],
        out_shape=[
            jax.ShapeDtypeStruct((total, width), BF),
            jax.ShapeDtypeStruct((total, width), F),
            jax.ShapeDtypeStruct((total, width), BF),
            jax.ShapeDtypeStruct((width, width + ff), BF),
            jax.ShapeDtypeStruct((ff, width), BF),
            jax.ShapeDtypeStruct((8, width), F),
            jax.ShapeDtypeStruct((1, ff), F),
        ],
        scratch_shapes=[
            pltpu.VMEM((total, width), BF),
            pltpu.VMEM((total, width), BF),
            pltpu.VMEM((total, ff), BF),
            pltpu.VMEM((rows, ff), BF),
            pltpu.VMEM((total, width), BF),
            pltpu.VMEM((total, ff), BF),
            pltpu.VMEM((total, width), BF),
        ],
        compiler_params=pltpu.CompilerParams(vmem_limit_bytes=LIMIT),
    )(attended, base, cotangent, w1, w2, vec, inner_bias)


def backward_body(j, b, refs, keep, gt_ref, scratch, hook=lambda at: None):
    len_ref, al_ref, q_ref, k_ref, v_ref, o_ref, do_ref, lse_ref, low_ref, gf_ref, w_ref = refs
    gbase_s, acc_s, vsum_s = scratch
    text, width = al_ref.shape[1], low_ref.shape[2]
    segs = low_ref.shape[1] - text
    quads = width // QUAD
    align = al_ref[pl.ds(b, 1), :]

    hook(0)
    bias = key_bias(len_ref[b])
    parts = [[], [], []]
    for pr in range(2):
        cols = slice(128 * pr, 128 * pr + 128)
        logs = [lse_ref[0, 0, 2 * pr + h : 2 * pr + h + 1, :] for h in range(2)]
        got = pair_backward(
            q_ref[0, :, cols], k_ref[0, :, cols], v_ref[0, :, cols], o_ref[0, :, cols], do_ref[0, :, cols], logs, text, bias,
            lambda: hook(1 + 2 * pr),
        )
        for i in range(3):
            parts[i].append(got[i])
        if pr == 0:
            hook(2)
    quad_grads = [jnp.concatenate(p, axis=1) for p in parts]
    cols = pl.ds(pl.multiple_of(j * QUAD, QUAD), QUAD)

    @pl.when(j == 0)
    def _():
        gbase_s[b] = gf_ref[0]

    gbase = gbase_s[b]
    for i in range(3):
        at = pl.ds(pl.multiple_of(i * width + j * QUAD, QUAD), QUAD)
        gbase = gbase + dot(quad_grads[i], w_ref[:, at], NT)
    gbase_s[b] = gbase

    low = low_ref[0]
    weight = [dot(low, g, TN) for g in quad_grads]
    sums = [col_sum(quad_grads[0].astype(F)), col_sum(quad_grads[2].astype(F))]

    @pl.when(b == 0)
    def _():
        for i in range(3):
            acc_s[i] = weight[i]
        for i in range(2):
            vsum_s[i : i + 1, cols] = sums[i]

    @pl.when(b == 1)
    def _():
        for i in range(2):
            vsum_s[i : i + 1, cols] += sums[i]
        keep(lambda i: (acc_s[i] + weight[i]).astype(BF))

    @pl.when(j == quads - 1)
    def _():
        member = member_of(align, segs)
        counts = jnp.maximum(jnp.sum(member, axis=1, keepdims=True), 1.0)
        share = gbase[text:] / counts
        high = share.astype(BF)
        rest = (share - high.astype(F)).astype(BF)
        sel = member.astype(BF)
        spread = dot(sel, high, TN) + dot(sel, rest, TN)
        gt_ref[0, :text] = (gbase[:text] + spread).astype(BF)
        gt_ref[0, text:] = gbase[text:].astype(BF)

    hook(4)


def vector_cols(vsum_s, gv_ref, gib_ref, cols_s):
    width = gv_ref.shape[1]
    rows = jnp.concatenate([vsum_s[:2], gv_ref[2:], jnp.zeros((120, width), F)], axis=0)
    cols_s[...] = jnp.zeros_like(cols_s)
    share = gib_ref.shape[1] * 24 // width
    for d in range(width // 24):
        cols_s[24 * d : 24 * d + 1, :share] = gib_ref[:, d * share : (d + 1) * share]
    return jnp.concatenate([rows.T, cols_s[...]], axis=1).astype(BF)


def backward_kernel(*refs):
    vsum_ref, gt_ref = refs[14:16]

    def keep(grad):
        for i in range(3):
            refs[11 + i][...] = grad(i)

    backward_body(pl.program_id(0), pl.program_id(1), refs[:11], keep, gt_ref, [refs[16], refs[17], vsum_ref])


def backward_attention(seg_lengths, alignment, q, k, v, att, gatt, lse, low, gfirst, w0):
    docs, slots, width = low.shape
    quads = width // QUAD
    quad = pl.BlockSpec((1, slots, QUAD), lambda j, b: (b, 0, j))
    doc = pl.BlockSpec((1, slots, width), lambda j, b: (b, 0, 0))
    wide = jax.ShapeDtypeStruct((width, width), BF)
    col = pl.BlockSpec((width, QUAD), lambda j, b: (0, j))
    return pl.pallas_call(
        backward_kernel,
        grid=(quads, docs),
        in_specs=[
            SMEM,
            once(alignment.shape, lambda j, b: (0, 0)),
            quad,
            quad,
            quad,
            quad,
            quad,
            pl.BlockSpec((1, 1, 8, slots), lambda j, b: (b, j, 0, 0)),
            doc,
            pl.BlockSpec((1, slots, width), lambda j, b: (jnp.where(j == 0, b, 1), 0, 0)),
            once(w0.shape, lambda j, b: (0, 0)),
        ],
        out_specs=[
            col,
            col,
            col,
            once((8, width), lambda j, b: (0, 0)),
            pl.BlockSpec((1, slots, width), lambda j, b: (jnp.where(j == quads - 1, b, 0), 0, 0)),
        ],
        out_shape=[wide, wide, wide, jax.ShapeDtypeStruct((8, width), F), jax.ShapeDtypeStruct((docs, slots, width), BF)],
        scratch_shapes=[
            pltpu.VMEM((docs, slots, width), F),
            pltpu.VMEM((3, width, QUAD), F),
        ],
        compiler_params=pltpu.CompilerParams(vmem_limit_bytes=LIMIT),
    )(seg_lengths, alignment, q, k, v, att, gatt, lse, low, gfirst, w0)


def at_slots(plan, step, slot):
    for (when, where), calls in plan.items():
        if where == slot:

            @pl.when(step == when)
            def _():
                for call in calls:
                    call()


def each(fn, *backs):
    return [functools.partial(fn, k) for k in backs]


TILE = 320
TILES = 4
ATTEND = 6


def forward_fused_kernel(
    len_ref, tok_ref, al_ref, wq, wk, wv, wo, wi, s2, vp, *rest
):
    low_ref, q_ref, k_ref, v_ref, att_ref, lse_ref = rest[:6]
    hat_ref, inv_ref, norm_ref, act_ref, slope_ref, vec_ref, w0, wa, wb, w2 = rest[6:16]
    (
        low_s, base_s, att_s, norm_s, w0_s, wa_s, wb_s, ib_s, cols_s, s0, sa, sb, land0, landa, landb, own0, owna, ownb,
        pair_sem, local, send, recv,
    ) = rest[16:]
    step = pl.program_id(0)
    width, ff = tok_ref.shape[2], wi.shape[1]
    place = Place()
    pairs = [
        Pair(place, s0, land0, own0, pair_sem.at[0], pair_sem.at[1]),
        Pair(place, sa, landa, owna, pair_sem.at[2], pair_sem.at[3]),
        Pair(place, sb, landb, ownb, pair_sem.at[4], pair_sem.at[5]),
    ]
    g0 = Gather(place, w0_s, own0, send.at[0], recv.at[0], local.at[0], w0.shape[2])
    ga = Gather(place, wa_s, owna, send.at[1], recv.at[1], local.at[1], wa.shape[2])
    gb = Gather(place, wb_s, ownb, send.at[2], recv.at[2], local.at[2], wb.shape[2])
    g2 = Gather(place, w2, s2, send.at[3], recv.at[3], local.at[3])
    saves = [
        lambda: pltpu.make_async_copy(w0_s, w0, local.at[4]),
        lambda: pltpu.make_async_copy(wa_s, wa, local.at[5]),
        lambda: pltpu.make_async_copy(wb_s, wb, local.at[6]),
    ]
    half = ff // 2
    start_of = lambda k: lambda: saves[k]().start()
    wait_of = lambda k: lambda: saves[k]().wait()

    def pack():
        for i, ref in enumerate((wq, wk, wv)):
            s0[:, i * width : (i + 1) * width] = ref[...].astype(F)
        cols_s[:128] = jnp.zeros((128, 128), F)
        for k in range(8):
            cols_s[k : k + 1, :24] = vp[:, 24 * k : 24 * k + 24]
        s0[:, 3 * width : 3 * width + 128] = cols_s[:128].T[:24]
        s0[:, 3 * width + 128 :] = jnp.zeros((24, 128), F)
        share = ff * 24 // width
        s0[0:1, 3 * width + 128 : 3 * width + 128 + share] = vp[:, 192 : 192 + share]

    def pack_rest():
        sa[:, :width] = wo[...].astype(F)
        sa[:, width:] = wi[:, :half].astype(F)
        sb[...] = wi[:, half:].astype(F)

    def vectors():
        cols = w0_s[:, :, 3 * width : 3 * width + 128].reshape(width, 128).astype(F)
        vec_ref[...] = cols.T[:8]
        cols_s[...] = w0_s[:, :, 3 * width + 128 :].reshape(width, 128).astype(F)
        share = ff * 24 // width
        for d in range(width // 24):
            ib_s[:, d * share : (d + 1) * share] = cols_s[24 * d : 24 * d + 1, :share]

    attend_plan = {
        (0, -1): [
            pack, place.barrier, pairs[0].start, pack_rest, pairs[1].start, pairs[2].start, pairs[0].done, g0.along_z,
            functools.partial(g0.to_neighbours, 0), pairs[1].done, pairs[2].done,
        ],
        (0, 0): [
            *each(g0.to_neighbours, 1), *each(g0.to_diagonal, 0), *each(g0.to_neighbours, 2), *each(g0.to_diagonal, 1),
            *each(g0.to_neighbours, 3), ga.along_z, *each(g0.to_core, 0), *each(g0.to_diagonal, 2),
            *each(ga.to_neighbours, 0), *each(g0.to_core, 1), *each(g0.to_diagonal, 3), *each(g0.to_core, 2, 3),
            *each(ga.to_neighbours, 1), g0.finish, start_of(0), vectors,
        ],
        (0, 1): [*each(ga.to_diagonal, 0), *each(ga.to_neighbours, 2)],
        (0, 2): [gb.along_z],
        (0, 3): each(ga.to_diagonal, 1),
        (0, 4): [*each(ga.to_neighbours, 3), *each(gb.to_neighbours, 0)],
        (1, 1): each(ga.to_core, 0),
        (1, 2): [*each(ga.to_diagonal, 2), *each(gb.to_neighbours, 1)],
        (1, 4): each(ga.to_core, 1),
        (2, 1): [*each(ga.to_diagonal, 3), *each(gb.to_neighbours, 2)],
        (2, 2): each(gb.to_diagonal, 0),
        (2, 3): [g2.along_z, *each(ga.to_core, 2)],
        (2, 4): [*each(gb.to_neighbours, 3), *each(gb.to_diagonal, 1)],
        (3, 1): [*each(ga.to_core, 3), *each(g2.to_neighbours, 0)],
        (3, 3): [*each(gb.to_diagonal, 2), *each(gb.to_core, 0)],
        (3, 4): each(g2.to_neighbours, 1),
        (4, 1): [*each(gb.to_diagonal, 3), *each(gb.to_core, 1)],
        (4, 3): [*each(g2.to_diagonal, 0), *each(gb.to_core, 2)],
        (4, 4): each(g2.to_neighbours, 2),
        (5, 1): [*each(gb.to_core, 3), *each(g2.to_diagonal, 1)],
        (5, 3): each(g2.to_neighbours, 3),
    }
    mlp_plan = {
        (6, 0): [ga.finish, start_of(1)],
        (6, 1): each(g2.to_core, 0),
        (6, 5): each(g2.to_diagonal, 2),
        (7, 2): each(g2.to_core, 1),
        (8, 1): each(g2.to_diagonal, 3),
        (9, 1): each(g2.to_core, 2),
        (10, 0): [gb.finish, start_of(2)],
        (10, 2): each(g2.to_core, 3),
        (13, 5): [
            g2.finish, wait_of(0), wait_of(1), wait_of(2), g0.drain, ga.drain, gb.drain, g2.drain,
        ],
    }

    @pl.when(step < ATTEND)
    def _():
        at_slots(attend_plan, step, -1)
        b, j = step // 3, step % 3
        outs = (base_s.at[pl.ds(b, 1)], low_ref, q_ref, k_ref, v_ref, att_ref, lse_ref)
        w_cols = lambda cols: w0_s[:, :, cols].reshape(width, QUAD)
        hook = functools.partial(at_slots, attend_plan, step)
        forward_body(b, j, len_ref, tok_ref, al_ref, w_cols, vec_ref, outs, low_s, hook)
        att_s[b, :, pl.ds(pl.multiple_of(j * QUAD, QUAD), QUAD)] = att_ref[0]

    @pl.when(step >= ATTEND)
    def _():
        hook = functools.partial(at_slots, mlp_plan, step)
        hook(0)
        first_plan = {at: calls for at, calls in mlp_plan.items() if at[0] < ATTEND + TILES}
        second_plan = {at: calls for at, calls in mlp_plan.items() if at[0] >= ATTEND + TILES}
        t = (step - ATTEND) % TILES
        here = pl.ds(pl.multiple_of(t * TILE, TILE), TILE)
        vec = lambda k: vec_ref[k : k + 1, :]

        def put(cols, act, slope):
            act_ref[:, cols], slope_ref[:, cols] = act, slope

        @pl.when(step < ATTEND + TILES)
        def _():
            rows = pl.ds(pl.multiple_of((t % 2) * TILE, TILE), TILE)
            w_out = lambda: wa_s[:, :, :width].reshape(width, width)
            w_in = lambda c, n: wa_s[:, :, width + c : width + c + n].reshape(width, n)
            hat, inv, low = mlp_norm(att_s[t // 2, rows], base_s[t // 2, rows], w_out, vec)
            hat_ref[...] = hat
            inv_ref[...] = jnp.broadcast_to(inv, inv_ref.shape)
            norm_ref[...] = low
            norm_s[here] = low
            mlp_units(low, w_in, ib_s[:, :half], put, 0, hook=functools.partial(at_slots, first_plan, step))

        @pl.when(step >= ATTEND + TILES)
        def _():
            w_in = lambda c, n: wb_s[:, :, c : c + n].reshape(width, n)
            mlp_units(norm_s[here], w_in, ib_s[:, half:], put, 0, hook=functools.partial(at_slots, second_plan, step))

        hook(5)


def forward_fused(seg_lengths, tokens, alignment, wq, wk, wv, wo, wi, s2, vp):
    docs, slots, width = tokens.shape
    ff = wi.shape[1]
    quads = width // QUAD
    n0, na, nb = 3 * width + 256, width + ff // 2, ff // 2
    total = docs * slots
    last = ATTEND - 1
    doc_of = lambda s: jnp.minimum(s, last) // quads
    doc = pl.BlockSpec((1, slots, width), lambda s: (doc_of(s), 0, 0))
    quad = pl.BlockSpec((1, slots, QUAD), lambda s: (doc_of(s), 0, jnp.minimum(s, last) % quads))
    wide = jax.ShapeDtypeStruct((docs, slots, width), BF)
    full = lambda *shape: once(shape, lambda s: (0,) * len(shape))
    tile = lambda n: pl.BlockSpec((TILE, n), lambda s: (jnp.clip(s - ATTEND, 0, TILES - 1), 0))
    past = lambda s: jnp.maximum(s - ATTEND, 0)
    units = pl.BlockSpec((TILE, ff // 2), lambda s: (past(s) % TILES, past(s) // TILES))
    ins = (alignment, wq, wk, wv, wo, wi, s2, vp)
    return pl.pallas_call(
        forward_fused_kernel,
        grid=(ATTEND + 2 * TILES,),
        in_specs=[SMEM, doc] + [full(*a.shape) for a in ins],
        out_specs=[
            doc, quad, quad, quad, quad,
            pl.BlockSpec((1, 1, 8, slots), lambda s: (doc_of(s), jnp.minimum(s, last) % quads, 0, 0)),
            tile(width), tile(128), tile(width), units, units, full(8, width),
        ]
        + [ANY] * 4,
        out_shape=[
            wide,
            wide,
            wide,
            wide,
            wide,
            jax.ShapeDtypeStruct((docs, quads, 8, slots), F),
            jax.ShapeDtypeStruct((total, width), F),
            jax.ShapeDtypeStruct((total, 128), F),
            jax.ShapeDtypeStruct((total, width), BF),
            jax.ShapeDtypeStruct((total, ff), BF),
            jax.ShapeDtypeStruct((total, ff), BF),
            jax.ShapeDtypeStruct((8, width), F),
            *[jax.ShapeDtypeStruct((CHIPS, 48, n), BF) for n in (n0, na, nb)],
            jax.ShapeDtypeStruct((CHIPS, 2, 96, width), BF),
        ],
        scratch_shapes=[
            pltpu.VMEM((slots, width), BF),
            pltpu.VMEM((docs, slots, width), F),
            pltpu.VMEM((docs, slots, width), BF),
            pltpu.VMEM((total, width), BF),
            *[pltpu.VMEM((CHIPS, 48, n), BF) for n in (n0, na, nb)],
            pltpu.VMEM((1, ff), F),
            pltpu.VMEM((width, 128), F),
            *[pltpu.VMEM((24, n), F) for n in (n0, na, nb)],
            *[pltpu.VMEM((24, n // 2), F) for n in (n0, na, nb)],
            *[pltpu.VMEM((48, n // 2), BF) for n in (n0, na, nb)],
            pltpu.SemaphoreType.DMA((6,)),
            pltpu.SemaphoreType.DMA((7,)),
            pltpu.SemaphoreType.DMA((4, Gather.SEMS)),
            pltpu.SemaphoreType.DMA((4, Gather.SEMS)),
        ],
        compiler_params=pltpu.CompilerParams(collective_id=0, has_side_effects=True, vmem_limit_bytes=LIMIT),
    )(seg_lengths, tokens, *ins)


def middle_kernel(hat_ref, inv_ref, cot_ref, vec_ref, *rest):
    act_h, slope_h, norm_h, att_h, wa_h, wb_h, w2_h = rest[:7]
    enc_ref, gf_ref, ga_ref, g1_ref, gv_ref, gib_ref, o_outer = rest[7:14]
    act_s, slope_s, wa_s, wb_s, w2_s, gsec_s, gmlp_s, g2_s = rest[14:22]
    bufs = rest[22:29]
    load_sem, local, send, recv = rest[29:]
    i = pl.program_id(0)
    rows, width = hat_ref.shape
    norm_s, att_s, gbr_s = (act_s.at[:, pl.ds(k * width, width)] for k in range(3))
    tiles = act_s.shape[0] // rows
    place = Place()
    g2 = Scatter(place, g2_s, bufs, o_outer, send.at[0], recv.at[0], local.at[0])

    cut = lambda t: pl.ds(t * rows, rows)
    loads = [lambda: pltpu.make_async_copy(w2_h, w2_s, load_sem.at[0])]
    for t in range(tiles):
        loads.append(lambda t=t: pltpu.make_async_copy(act_h.at[cut(t)], act_s.at[cut(t)], load_sem.at[1 + t]))
    for t in range(tiles):
        loads.append(lambda t=t: pltpu.make_async_copy(slope_h.at[cut(t)], slope_s.at[cut(t)], load_sem.at[5 + t]))
    loads += [
        lambda: pltpu.make_async_copy(wa_h, wa_s, load_sem.at[9]),
        lambda: pltpu.make_async_copy(norm_h, norm_s, load_sem.at[10]),
        lambda: pltpu.make_async_copy(att_h, att_s, load_sem.at[11]),
        lambda: pltpu.make_async_copy(wb_h, wb_s, load_sem.at[12]),
    ]
    wait = lambda k: lambda: loads[k]().wait()
    loads_start = lambda k: lambda: loads[k]().start()

    def begin():
        for load in loads[:2]:
            load().start()
        gv_ref[...] = jnp.zeros_like(gv_ref)
        gib_ref[...] = jnp.zeros_like(gib_ref)
        place.barrier()

    plan = {
        (0, 0): [begin, wait(0), wait(1), *map(loads_start, (2, 3, 4))],
        (1, 0): [wait(2), *map(loads_start, (9, 12, 5))],
        (2, 0): [wait(3), *map(loads_start, (6, 7, 8))],
        (3, 0): [wait(4)],
        (4, 2): each(g2.from_sibling, 3),
        (5, 2): each(g2.from_sibling, 2),
        (6, 2): each(g2.from_sibling, 1),
        (7, 2): each(g2.from_sibling, 0),
        (6, 0): each(g2.to_diagonal, 3),
        (7, 0): each(g2.to_diagonal, 2),
        (8, 0): [loads_start(10), loads_start(11), wait(9), wait(12), wait(5), *each(g2.to_diagonal, 1)],
        (8, 1): [*each(g2.to_diagonal, 0), *each(g2.to_neighbours, 3)],
        (8, 2): each(g2.to_neighbours, 2),
        (9, 0): [wait(6)],
        (9, 1): each(g2.to_neighbours, 1),
        (9, 2): each(g2.to_neighbours, 0),
        (10, 0): [wait(7)],
        (10, 1): each(g2.along_z, 3),
        (10, 2): each(g2.along_z, 2),
        (11, 0): [wait(8)],
        (11, 2): each(g2.along_z, 1),
        (12, 0): [wait(10)],
        (12, 2): each(g2.along_z, 0),
        (16, 0): [wait(11)],
        (16, 2): [g2.owner, g2.drain],
    }
    hook = functools.partial(at_slots, plan, i)
    hook(0)
    vec = lambda k: vec_ref[k : k + 1, :]
    w_outer = lambda c, n: w2_s[c * CHIPS // act_s.shape[1] : (c + n) * CHIPS // act_s.shape[1]].reshape(n, width)

    @pl.when(i < tiles)
    def _():
        at = pl.ds(pl.multiple_of(i * rows, rows), rows)
        enc_ref[...], grad_second, sums = mlp_second(hat_ref[...], act_s[at], w_outer, cot_ref[...], vec)
        gsec_s[at] = grad_second
        gmlp = grad_second.astype(BF)
        gmlp_s[at] = gmlp
        gv_ref[5:6] += col_sum(gmlp.astype(F))
        gv_ref[6:7] += sums[0]
        gv_ref[7:8] += sums[1]

    @pl.when((i >= tiles) & (i < 2 * tiles))
    def _():
        plane = place.plane(2 * tiles - 1 - i)
        cols = pl.ds(pl.multiple_of(plane * width, width), width)
        g2_s[pl.ds(4 * plane, 4)] = dot(act_s[:, cols], gmlp_s[...], TN).astype(BF).reshape(4, 2, 96, width)

    @pl.when((i >= 2 * tiles) & (i < 3 * tiles))
    def _():
        at = pl.ds(pl.multiple_of((i - 2 * tiles) * rows, rows), rows)

        def put(kind, *got):
            if kind == "pre":
                slope_s[at, got[0]] = got[1]
                gib_ref[:, got[0]] += col_sum(got[1].astype(F))
            else:
                gf_ref[...], gbr_s[at] = got[:2]
                gv_ref[2:3] += col_sum(got[1].astype(F))
                gv_ref[3:4] += got[2]
                gv_ref[4:5] += got[3]

        half = wb_s.shape[2]
        w_out = lambda: wa_s[:, :, :width].reshape(width, width)

        def w_in(c, n):
            part = wa_s[:, :, width + c : width + c + n] if c < half else wb_s[:, :, c - half : c - half + n]
            return part.reshape(width, n)

        ga_ref[...] = mlp_back(
            gsec_s[at], gmlp_s[at], hat_ref[...], inv_ref[:, 0:1], slope_s[at], w_outer, w_out, w_in, vec, put, hook=hook
        )

    @pl.when((i >= 3 * tiles) & (i < 4 * tiles))
    def _():
        cols = pl.ds(pl.multiple_of((i - 3 * tiles) * width, width), width)
        g1_ref[...] = dot(norm_s[...], slope_s[:, cols], TN).astype(BF)

    @pl.when(i == 4 * tiles)
    def _():
        g1_ref[...] = dot(att_s[...], gbr_s[...], TN).astype(BF)

    hook(2)


def middle(hat, inv, cotangent, vec, act, slope, norm, att, wa, wb, w2):
    total, width = hat.shape
    ff = act.shape[1]
    tiles = total // TILE
    early = lambda n: pl.BlockSpec((TILE, n), lambda i: (jnp.minimum(i, tiles - 1), 0))
    late = lambda n: pl.BlockSpec((TILE, n), lambda i: (jnp.clip(i - 2 * tiles, 0, tiles - 1), 0))
    full = lambda *shape: once(shape, lambda i: (0,) * len(shape))
    return pl.pallas_call(
        middle_kernel,
        grid=(4 * tiles + 1,),
        in_specs=[
            pl.BlockSpec(
                (TILE, width),
                lambda i: (jnp.where(i < 2 * tiles, jnp.minimum(i, tiles - 1), jnp.minimum(i - 2 * tiles, tiles - 1)), 0),
            ),
            late(128),
            early(width),
            full(8, width),
        ]
        + [ANY] * 7,
        out_specs=[
            early(width),
            late(width),
            late(width),
            pl.BlockSpec((width, width), lambda i: (0, jnp.where(i == 4 * tiles, 0, jnp.clip(i - 3 * tiles, 0, 3) + 1))),
            full(8, width),
            full(1, ff),
            full(96, width),
        ],
        out_shape=[
            jax.ShapeDtypeStruct((total, width), BF),
            jax.ShapeDtypeStruct((total, width), F),
            jax.ShapeDtypeStruct((total, width), BF),
            jax.ShapeDtypeStruct((width, width + ff), BF),
            jax.ShapeDtypeStruct((8, width), F),
            jax.ShapeDtypeStruct((1, ff), F),
            jax.ShapeDtypeStruct((96, width), F),
        ],
        scratch_shapes=[
            pltpu.VMEM((total, ff), BF),
            pltpu.VMEM((total, ff), BF),
            pltpu.VMEM(wa.shape, BF),
            pltpu.VMEM(wb.shape, BF),
            pltpu.VMEM(w2.shape, BF),
            pltpu.VMEM((total, width), F),
            pltpu.VMEM((total, width), BF),
            pltpu.VMEM(w2.shape, BF),
            *Scatter.scratch(96, width, False),
            pltpu.SemaphoreType.DMA((13,)),
            pltpu.SemaphoreType.DMA((1, 4)),
            pltpu.SemaphoreType.DMA((1, Scatter.SEMS)),
            pltpu.SemaphoreType.DMA((1, Scatter.SEMS)),
        ],
        compiler_params=pltpu.CompilerParams(collective_id=2, has_side_effects=True, vmem_limit_bytes=LIMIT),
    )(hat, inv, cotangent, vec, act, slope, norm, att, wa, wb, w2)


def backward_fused_kernel(widths, *refs):
    ins, (gv_ref, gib_ref, g1_ref) = refs[:11], refs[11:14]
    gt_ref, o_wide, o_inner, o_vec, o_ib = refs[14], refs[15:19], refs[19], refs[20], refs[21]
    scratch, cols_s = refs[22:25], refs[25]
    rest = list(refs[26:])
    local, send, recv = rest[-3:]
    j, b = pl.program_id(0), pl.program_id(1)
    step = 2 * j + b
    width = ins[8].shape[2]
    place = Place()
    take = lambda n: [rest.pop(0) for _ in range(n)]
    quad_s, stage = take(3), take(1)[0]
    sources = [g1_ref, *quad_s]
    groups = []
    for i, (src, wide) in enumerate(zip(sources, widths)):
        out = stage.at[:, pl.ds(0, wide)]
        groups.append(Scatter(place, src, take(9), out, send.at[i], recv.at[i], local.at[i], wide))
    g1, q0, q1, q2 = groups

    def give_rest():
        g1.finish()
        o_wide[3][...] = stage[:, :width]
        o_inner[...] = stage[:, width : widths[0]]

    def give_quad(k):
        groups[1 + k].finish()
        for i in range(3):
            o_wide[i][:, k * QUAD : (k + 1) * QUAD] = stage[:, i * QUAD : (i + 1) * QUAD]
        if k == 2:
            o_vec[...] = stage[:, 3 * QUAD : 3 * QUAD + 128].T[:8]
            o_ib[...] = stage[0:1, 3 * QUAD + 128 : 4 * QUAD]

    def keep(grad):
        for k in range(3):

            @pl.when(j == k)
            def _():
                for i in range(3):
                    quad_s[k][:, :, i * QUAD : (i + 1) * QUAD] = grad(i).reshape(CHIPS, 48, QUAD)
                if k == 2:
                    both = vector_cols(scratch[2], gv_ref, gib_ref, cols_s)
                    quad_s[k][:, :, 3 * QUAD :] = both.reshape(CHIPS, 48, QUAD)

    late, soon = (3, 2), (1, 0)
    all4 = late + soon
    plan = {
        (0, 0): [place.barrier, *each(g1.from_sibling, *all4)],
        (0, 2): each(g1.to_diagonal, 3),
        (0, 4): each(g1.to_diagonal, 2, 1, 0),
        (1, 2): each(g1.to_neighbours, 3),
        (1, 4): [*each(g1.to_neighbours, 2, 1, 0), *each(q0.from_sibling, *all4)],
        (2, 2): each(g1.along_z, 3),
        (2, 4): [*each(g1.along_z, 2), *each(q0.to_diagonal, *all4)],
        (3, 2): each(g1.along_z, 1),
        (3, 4): [*each(g1.along_z, 0), *each(q0.to_neighbours, *all4), *each(q1.from_sibling, *all4)],
        (4, 2): each(q1.to_diagonal, *all4),
        (4, 4): [*each(q0.along_z, *all4), *each(q1.to_neighbours, *all4)],
        (5, 2): [g1.owner],
        (5, 4): [
            *each(q2.from_sibling, *all4), *each(q1.along_z, *all4), q0.owner, *each(q2.to_diagonal, *all4),
            give_rest, functools.partial(give_quad, 0), *each(q2.to_neighbours, *all4), q1.owner,
            *each(q2.along_z, *all4), functools.partial(give_quad, 1), q2.owner, functools.partial(give_quad, 2),
            *[g.drain for g in groups],
        ],
    }
    backward_body(j, b, ins, keep, gt_ref, scratch, functools.partial(at_slots, plan, step))


def backward_fused(seg_lengths, alignment, q, k, v, att, gatt, lse, low, gfirst, w0, gv, gib, g1):
    docs, slots, width = low.shape
    quads = width // QUAD
    quad = pl.BlockSpec((1, slots, QUAD), lambda j, b: (b, 0, j))
    doc = pl.BlockSpec((1, slots, width), lambda j, b: (b, 0, 0))
    whole = lambda *shape: once(shape, lambda j, b: (0,) * len(shape))
    n1 = g1.shape[2]
    widths = (n1, 3 * QUAD, 3 * QUAD, 4 * QUAD)
    bufs = []
    for wide in widths:
        bufs += Scatter.scratch(48, wide // 2, True)
    n = len(widths)
    shard = jax.ShapeDtypeStruct((24, width), F)
    return pl.pallas_call(
        functools.partial(backward_fused_kernel, widths),
        grid=(quads, docs),
        in_specs=[
            SMEM,
            whole(*alignment.shape),
            quad,
            quad,
            quad,
            quad,
            quad,
            pl.BlockSpec((1, 1, 8, slots), lambda j, b: (b, j, 0, 0)),
            doc,
            pl.BlockSpec((1, slots, width), lambda j, b: (jnp.where(j == 0, b, 1), 0, 0)),
            whole(*w0.shape),
            whole(*gv.shape),
            whole(*gib.shape),
            ANY,
        ],
        out_specs=[
            pl.BlockSpec((1, slots, width), lambda j, b: (jnp.where(j == quads - 1, b, 0), 0, 0)),
            *[whole(24, width)] * 4,
            whole(24, n1 - width),
            whole(8, 24),
            whole(1, 128),
        ],
        out_shape=[
            jax.ShapeDtypeStruct((docs, slots, width), BF),
            shard,
            shard,
            shard,
            shard,
            jax.ShapeDtypeStruct((24, n1 - width), F),
            jax.ShapeDtypeStruct((8, 24), F),
            jax.ShapeDtypeStruct((1, 128), F),
        ],
        scratch_shapes=[
            pltpu.VMEM((docs, slots, width), F),
            pltpu.VMEM((3, width, QUAD), F),
            pltpu.VMEM((8, width), F),
            pltpu.VMEM((width, 128), F),
            *[pltpu.VMEM((CHIPS, 48, wide), BF) for wide in widths[1:]],
            pltpu.VMEM((24, n1), F),
            *bufs,
            pltpu.SemaphoreType.DMA((n, 4)),
            pltpu.SemaphoreType.DMA((n, Scatter.SEMS)),
            pltpu.SemaphoreType.DMA((n, Scatter.SEMS)),
        ],
        compiler_params=pltpu.CompilerParams(collective_id=1, has_side_effects=True, vmem_limit_bytes=LIMIT),
    )(seg_lengths, alignment, q, k, v, att, gatt, lse, low, gfirst, w0, gv, gib, g1)


def deliver_kernel(count, *refs):
    ins, sums, gib = refs[:count], refs[count], refs[count + 1]
    outs, vecs, ib_out = refs[count + 2 : 2 * count + 2], refs[2 * count + 2 : 2 * count + 10], refs[2 * count + 10]
    held, sem_in, sem_out = refs[2 * count + 11 : 3 * count + 11], refs[-2], refs[-1]
    loads = [pltpu.make_async_copy(a, b, sem_in.at[i]) for i, (a, b) in enumerate(zip(ins, held))]
    stores = [pltpu.make_async_copy(a, b, sem_out.at[i]) for i, (a, b) in enumerate(zip(held, outs))]
    for c in loads:
        c.start()
    for k, out in enumerate(vecs):
        out[...] = sums[k, :]
    ib_out[...] = gib[0, : ib_out.shape[0]]
    for i in range(count):
        loads[i].wait()
        stores[i].start()
    for c in stores:
        c.wait()


def deliver(arrays, sums, gib, share):
    n = len(arrays)
    return pl.pallas_call(
        functools.partial(deliver_kernel, n),
        out_shape=[jax.ShapeDtypeStruct(a.shape, a.dtype) for a in arrays]
        + [jax.ShapeDtypeStruct((sums.shape[1],), F)] * 8
        + [jax.ShapeDtypeStruct((share,), F)],
        in_specs=[ANY] * n + [VMEM] * 2,
        out_specs=[ANY] * n + [VMEM] * 9,
        scratch_shapes=[pltpu.VMEM(a.shape, a.dtype) for a in arrays] + [pltpu.SemaphoreType.DMA((n,))] * 2,
        compiler_params=pltpu.CompilerParams(vmem_limit_bytes=LIMIT),
    )(*arrays, sums, gib)


def own_kernels(shard_rows, docs):
    return lax.axis_size("dp") == PLANES and lax.axis_size("fsdp") == 8 and shard_rows == 24 and docs == 2


def shards(
    tokens, cotangent, seg_lengths, alignment, query_weight, query_bias, key_weight, value_weight, value_bias,
    out_weight, out_bias, first_gain, first_shift, inner_weight, inner_bias, outer_weight, outer_bias, second_gain,
    second_shift,
):
    docs, slots, width = tokens.shape
    rows = query_weight.shape[0]
    every = ("dp", "fsdp")
    vectors = (query_bias, value_bias, out_bias, first_gain, first_shift, outer_bias, second_gain, second_shift)
    weights = (query_weight, key_weight, value_weight, out_weight, inner_weight, outer_weight)
    flat = lambda t: t.reshape(docs * slots, width)
    whole = lambda t: t.reshape(docs, slots, width)
    if own_kernels(rows, docs):
        packed = jnp.concatenate((*vectors, inner_bias)).astype(F)[None]
        low, q, k, v, att, lse, hat, inv, norm, act, slope, vec, w0, wa, wb, w2 = forward_fused(
            seg_lengths, tokens, alignment, *weights, packed
        )
        encoded, gfirst, gatt, g1, gvec, ginner, gouter = middle(
            hat, inv, flat(cotangent), vec, act, slope, norm, flat(att), wa, wb, w2
        )
        grad_tokens, gq, gk, gv, gout, ginn, sums, gib = backward_fused(
            seg_lengths, alignment, q, k, v, att, whole(gatt), lse, low, whole(gfirst), w0.reshape(width, -1), gvec,
            ginner, g1.reshape(CHIPS, 48, -1),
        )
        whole_encoded = whole(encoded)
        whole_encoded, grad_tokens, gq, gk, gv, gout, ginn, gouter, *sums, gib = deliver(
            (whole_encoded, grad_tokens, gq, gk, gv, gout, ginn, gouter), sums, gib, inner_bias.shape[0]
        )
    else:
        gather = lambda s: lax.all_gather(s, every, axis=0, tiled=True)
        owned = lambda g: lax.psum_scatter(g.astype(F), every, scatter_dimension=0, tiled=True)
        wq, wk, wv, wo, wi, w2 = (gather(w) for w in weights)
        w0, w1 = jnp.concatenate([wq, wk, wv], axis=1), jnp.concatenate([wo, wi], axis=1)
        vec = jnp.stack([gather(t).astype(F) for t in vectors])
        inner_row = gather(inner_bias).astype(F)[None]
        base, low, q, k, v, att, lse = forward_attention(seg_lengths, tokens, alignment, w0, vec)
        encoded, gfirst, gatt, g1, g2, gvec, ginner = mlp_both(
            flat(att), flat(base), flat(cotangent), w1, w2, vec, inner_row
        )
        gq, gk, gv, two, grad_tokens = backward_attention(
            seg_lengths, alignment, q, k, v, att, whole(gatt), lse, low, whole(gfirst), w0
        )
        gq, gk, gv, g1, gouter = (owned(g) for g in (gq, gk, gv, g1, g2))
        gout, ginn = g1[:, :width], g1[:, width:]
        sums = tuple(owned(two[i] if i < 2 else gvec[i]) for i in range(8))
        gib = owned(ginner[0])
        whole_encoded = whole(encoded)
    return (
        whole_encoded, grad_tokens, gq, sums[0], gk, gv, sums[1], gout, sums[2], sums[3], sums[4], ginn, gib, gouter,
        sums[5], sums[6], sums[7],
    )


def solution(mesh):
    in_specs = (
        P(("dp", "fsdp"), None, None),
        P(("dp", "fsdp"), None, None),
        P(("dp", "fsdp")),
        P(("dp", "fsdp"), None),
        P(("dp", "fsdp"), None),
        P(("dp", "fsdp")),
        P(("dp", "fsdp"), None),
        P(("dp", "fsdp"), None),
        P(("dp", "fsdp")),
        P(("dp", "fsdp"), None),
        P(("dp", "fsdp")),
        P(("dp", "fsdp")),
        P(("dp", "fsdp")),
        P(("dp", "fsdp"), None),
        P(("dp", "fsdp")),
        P(("dp", "fsdp"), None),
        P(("dp", "fsdp")),
        P(("dp", "fsdp")),
        P(("dp", "fsdp")),
    )
    out_specs = (
        P(("dp", "fsdp"), None, None),
        P(("dp", "fsdp"), None, None),
        P(("dp", "fsdp"), None),
        P(("dp", "fsdp")),
        P(("dp", "fsdp"), None),
        P(("dp", "fsdp"), None),
        P(("dp", "fsdp")),
        P(("dp", "fsdp"), None),
        P(("dp", "fsdp")),
        P(("dp", "fsdp")),
        P(("dp", "fsdp")),
        P(("dp", "fsdp"), None),
        P(("dp", "fsdp")),
        P(("dp", "fsdp"), None),
        P(("dp", "fsdp")),
        P(("dp", "fsdp")),
        P(("dp", "fsdp")),
    )
    return jax.shard_map(shards, mesh=mesh, in_specs=in_specs, out_specs=out_specs, check_vma=False)
```

```python
import functools
import jax
import jax.numpy as jnp
from jax import lax
from jax.experimental import pallas as pl
from jax.experimental.pallas import tpu as pltpu
from jax.sharding import PartitionSpec as P

MESH = pl.DeviceIdType.MESH
ANY = pl.BlockSpec(memory_space=pl.ANY)
VMEM = pl.BlockSpec(memory_space=pltpu.VMEM)
PLANES = 4
CHIPS = 16


class Place:
    def __init__(self):
        self.z = lax.axis_index("dp")
        self.f = lax.axis_index("fsdp")
        self.core = self.f % 2
        self.x = (self.f // 2) % 2
        self.y = self.f // 4
        self.sib = self.f + 1 - 2 * self.core
        self.xn = self.f + 2 - 4 * self.x
        self.yn = self.f + 4 - 8 * self.y
        self.spot = self.f // 2
        self.spot_x = self.xn // 2
        self.spot_y = self.yn // 2
        self.spot_d = 3 - self.spot

    def plane(self, back):
        return (self.z + PLANES - back) % PLANES

    def coming(self, k):
        return (self.z, 1 + self.z % 2, (self.z + 2) % PLANES, 3 * ((self.z + 1) % 2))[k]

    def ahead(self, step):
        return (self.z + step) % PLANES

    def barrier(self):
        bar = pltpu.get_barrier_semaphore()
        for other in self.partners():
            pl.semaphore_signal(bar, inc=1, device_id=other, device_id_type=MESH)
        pl.semaphore_wait(bar, 3 + PLANES - 1)

    def partners(self):
        return [(self.z, self.sib), (self.z, self.xn), (self.z, self.yn)] + [
            (self.ahead(k), self.f) for k in range(1, PLANES)
        ]


def remote(src, dst, send, recv, dev):
    return pltpu.make_async_remote_copy(
        src_ref=src, dst_ref=dst, send_sem=send, recv_sem=recv, device_id=dev, device_id_type=MESH
    )


class Gather:
    SEMS = 29

    def __init__(self, place, full, own, send, recv, local, width=None):
        self.p, self.full, self.own = place, full, own
        self.send, self.recv, self.local = send, recv, local
        self.half = None if width is None else width // 2
        self.rows = own.shape[0]
        self.started = []

    def view(self, chip, r0=0, r1=None, core=None):
        core = self.p.core if core is None else core
        r1 = self.rows if r1 is None else r1
        if self.half is None:
            return self.full.at[chip, core, pl.ds(r0, r1 - r0), :]
        cols = pl.ds(pl.multiple_of(core * self.half, 128), self.half)
        return self.full.at[chip, pl.ds(r0, r1 - r0), cols]

    def block(self, plane, core):
        if self.half is None:
            return self.full.at[pl.ds(4 * plane, 4), core]
        cols = pl.ds(pl.multiple_of(core * self.half, 128), self.half)
        return self.full.at[pl.ds(4 * plane, 4), :, cols]

    def cut(self, k):
        if self.rows == 96:
            return 48
        return 32 if k % 2 == 0 else 16

    def copy(self, src, dst, index, dev, send=None):
        return remote(src, dst, self.send.at[index if send is None else send], self.recv.at[index], dev)

    def start(self, make, when=None):
        if when is None:
            make().start()
        else:
            pl.when(when())(lambda: make().start())
        self.started.append((make, when))

    def drain(self):
        for make, when in self.started:
            if when is None:
                make().wait_send()
            else:
                pl.when(when())(lambda: make().wait_send())

    def chip(self, k, spot):
        return 4 * self.p.coming(k) + spot

    def own_copy(self):
        return pltpu.make_async_copy(self.own, self.view(self.chip(0, self.p.spot)), self.local)

    def along_z(self):
        p = self.p
        mine = lambda: self.view(self.chip(0, p.spot))
        self.own_copy().start()
        self.start(lambda: self.copy(self.own, mine(), p.z, (p.z - 1, p.f), 24), lambda: p.z > 0)
        self.start(lambda: self.copy(self.own, mine(), p.z, (p.z + 1, p.f), 25), lambda: p.z < PLANES - 1)

    def onward(self, k, when=None):
        p = self.p
        piece = lambda: self.view(self.chip(k, p.spot))
        goal = lambda: p.z + jnp.where(p.coming(k) < p.z, 1, -1)
        goes = lambda: (goal() >= 0) & (goal() < PLANES)
        wait = lambda: self.copy(piece(), piece(), p.coming(k), (p.z, p.f)).wait_recv()
        both = goes if when is None else lambda: when() & goes()
        if when is None:
            wait()
        else:
            pl.when(when())(wait)
        self.start(lambda: self.copy(piece(), piece(), p.coming(k), (goal(), p.f), 25 + k), both)

    def to_neighbours(self, k):
        p = self.p
        piece = lambda: self.view(self.chip(k, p.spot))
        middle = lambda: p.z % 3 != 0
        if k == 1:
            self.onward(1)
            self.onward(3, middle)
        elif k == 2:
            self.onward(2)
        elif k == 3:
            self.onward(3, lambda: p.z % 3 == 0)
        src = piece if k else lambda: self.own
        self.start(lambda: self.copy(src(), piece(), 4 + k, (p.z, p.xn)))
        self.start(lambda: self.copy(src(), piece(), 8 + k, (p.z, p.yn)))

    def to_diagonal(self, k):
        p, cut = self.p, self.cut(k)
        cx, cy = lambda: self.chip(k, p.spot_x), lambda: self.chip(k, p.spot_y)
        full_x, full_y = self.view(cx()), self.view(cy())
        self.copy(full_x, full_x, 4 + k, (p.z, p.xn)).wait_recv()
        part_x = lambda: self.view(cx(), 0, cut)
        self.start(lambda: self.copy(part_x(), part_x(), 12 + k, (p.z, p.yn)))
        self.copy(full_y, full_y, 8 + k, (p.z, p.yn)).wait_recv()
        part_y = lambda: self.view(cy(), cut, self.rows)
        self.start(lambda: self.copy(part_y(), part_y(), 16 + k, (p.z, p.xn)))

    def to_core(self, k):
        p, cut = self.p, self.cut(k)
        cd = self.chip(k, p.spot_d)
        a, b = self.view(cd, 0, cut), self.view(cd, cut, self.rows)
        self.copy(a, a, 12 + k, (p.z, p.yn)).wait_recv()
        self.copy(b, b, 16 + k, (p.z, p.xn)).wait_recv()
        if k == 0:
            self.own_copy().wait()
        blk = lambda: self.block(p.coming(k), p.core)
        self.start(lambda: self.copy(blk(), blk(), 20 + k, (p.z, p.sib)))

    def finish(self):
        p = self.p
        for k in range(PLANES):
            blk = self.block(p.coming(k), 1 - p.core)
            self.copy(blk, blk, 20 + k, (p.z, p.sib)).wait_recv()


def build_own(place, shard, land, own):
    half = own.shape[1]
    first = place.core == 0
    for c0 in range(0, half, 128):
        mine = shard[:, pl.ds(pl.multiple_of(place.core * half + c0, 128), 128)]
        other = land[:, c0 : c0 + 128]
        top = jnp.where(first, mine, other)
        bottom = jnp.where(first, other, mine)
        own[:, c0 : c0 + 128] = jnp.concatenate([top, bottom], axis=0).astype(own.dtype)


class Pair:
    def __init__(self, place, shard, land, own, send, recv):
        half = own.shape[1]
        src = lambda: shard.at[:, pl.ds(pl.multiple_of((1 - place.core) * half, 128), half)]
        self.c = lambda: remote(src(), land, send, recv, (place.z, place.sib))
        self.args = (place, shard, land, own)

    def start(self):
        self.c().start()

    def done(self):
        self.c().wait()
        build_own(*self.args)


class Scatter:
    SEMS = 4 + 4 + 4 + 4 + 4 + 3 + 1

    def __init__(self, place, full, bufs, out, send, recv, local, width=None):
        self.p, self.full, self.out = place, full, out
        self.sums, self.from_core, self.la, self.lb, self.lx, self.ly, self.lz = bufs[:7]
        if width is not None:
            self.total, self.last = bufs[7:]
        self.send, self.recv, self.local = send, recv, local
        self.half = None if width is None else width // 2
        self.rows = self.sums.shape[1]
        self.started = []

    @staticmethod
    def scratch(rows, cols, two_rows):
        bf = jnp.bfloat16
        shapes = [
            pltpu.VMEM((CHIPS, rows, cols), bf),
            pltpu.VMEM((CHIPS, rows, cols), bf),
            pltpu.VMEM((4, rows - 16, cols), bf),
            pltpu.VMEM((4, rows - 16, cols), bf),
            pltpu.VMEM((4, rows, cols), bf),
            pltpu.VMEM((4, rows, cols), bf),
            pltpu.VMEM((3, rows, cols), bf),
        ]
        if two_rows:
            shapes += [pltpu.VMEM((rows, cols), jnp.float32), pltpu.VMEM((rows // 2, cols), jnp.float32)]
        return shapes

    def chip(self, back, spot):
        return 4 * self.p.plane(back) + spot

    cut = Gather.cut
    copy = Gather.copy
    start = Gather.start
    drain = Gather.drain
    block = Gather.block

    def from_sibling(self, back):
        p = self.p
        blk = lambda: pl.ds(4 * p.plane(back), 4)
        c = pltpu.make_async_copy(self.block(p.plane(back), p.core), self.sums.at[blk()], self.local.at[back])
        c.start()
        self.start(
            lambda: self.copy(
                self.block(p.plane(back), 1 - p.core), self.from_core.at[blk()], back, (p.z, p.sib)
            )
        )

    def to_diagonal(self, back):
        p, cut, rows = self.p, self.cut(back), self.rows
        blk = pl.ds(4 * p.plane(back), 4)
        pltpu.make_async_copy(self.block(p.plane(back), p.core), self.sums.at[blk], self.local.at[back]).wait()
        self.copy(self.from_core.at[blk], self.from_core.at[blk], back, (p.z, p.sib)).wait_recv()
        for j in range(4):
            at = 4 * p.plane(back) + j
            self.sums[at] = self.sums[at] + self.from_core[at]
        cd = lambda: self.chip(back, p.spot_d)
        self.start(
            lambda: self.copy(
                self.sums.at[cd(), pl.ds(0, cut)], self.la.at[back, pl.ds(0, cut)], 4 + back, (p.z, p.xn)
            )
        )
        self.start(
            lambda: self.copy(
                self.sums.at[cd(), pl.ds(cut, rows - cut)],
                self.lb.at[back, pl.ds(0, rows - cut)],
                8 + back,
                (p.z, p.yn),
            )
        )

    def to_neighbours(self, back):
        p, cut, rows = self.p, self.cut(back), self.rows
        cx, cy = self.chip(back, p.spot_x), self.chip(back, p.spot_y)
        a, b = self.la.at[back, pl.ds(0, cut)], self.lb.at[back, pl.ds(0, rows - cut)]
        self.copy(a, a, 4 + back, (p.z, p.xn)).wait_recv()
        self.sums[cy, 0:cut] = self.sums[cy, 0:cut] + a[...]
        to_y = lambda: self.sums.at[self.chip(back, p.spot_y)]
        self.start(lambda: self.copy(to_y(), self.ly.at[back], 16 + back, (p.z, p.yn)))
        self.copy(b, b, 8 + back, (p.z, p.yn)).wait_recv()
        self.sums[cx, cut:rows] = self.sums[cx, cut:rows] + b[...]
        to_x = lambda: self.sums.at[self.chip(back, p.spot_x)]
        self.start(lambda: self.copy(to_x(), self.lx.at[back], 12 + back, (p.z, p.xn)))

    def along_z(self, back):
        p = self.p
        c0 = self.chip(back, p.spot)
        lx, ly = self.lx.at[back], self.ly.at[back]
        self.copy(lx, lx, 12 + back, (p.z, p.xn)).wait_recv()
        self.copy(ly, ly, 16 + back, (p.z, p.yn)).wait_recv()
        f = jnp.float32
        got = self.sums[c0].astype(f) + lx[...].astype(f) + ly[...].astype(f)
        self.sums[c0] = got.astype(jnp.bfloat16)
        if back:
            mine = lambda: self.sums.at[self.chip(back, p.spot)]
            self.start(lambda: self.copy(mine(), self.lz.at[back - 1], 20 + back - 1, (p.plane(back), p.f)))

    def owner(self):
        p = self.p
        f = jnp.float32
        for k in range(3):
            self.copy(self.lz.at[k], self.lz.at[k], 20 + k, (p.z, p.f)).wait_recv()
        total = self.mine().astype(f)
        for k in range(3):
            total = total + self.lz[k].astype(f)
        if self.half is None:
            self.out[...] = total
            return
        self.total[...] = total
        rows = self.rows // 2
        theirs = lambda: self.total.at[pl.ds(pl.multiple_of((1 - p.core) * rows, 8), rows)]
        self.start(lambda: self.copy(theirs(), self.last, 23, (p.z, p.sib)))

    def mine(self):
        return self.sums[self.chip(0, self.p.spot)]

    def finish(self):
        if self.half is None:
            return
        p, half = self.p, self.half
        rows = self.rows // 2
        self.copy(self.last, self.last, 23, (p.z, p.sib)).wait_recv()
        mine = pl.ds(pl.multiple_of(p.core * rows, 8), rows)
        self.out[:, pl.ds(pl.multiple_of(p.core * half, 128), half)] = self.total[mine]
        self.out[:, pl.ds(pl.multiple_of((1 - p.core) * half, 128), half)] = self.last[...]


F = jnp.float32
BF = jnp.bfloat16
NN = (((1,), (0,)), ((), ()))
NT = (((1,), (1,)), ((), ()))
TN = (((0,), (0,)), ((), ()))
SMEM = pl.BlockSpec(memory_space=pltpu.SMEM)
HEADS = 12
HEAD_DIM = 64
QUAD = 4 * HEAD_DIM
scale = HEAD_DIM**-0.5
norm_eps = 1e-05
masked_score = -1000000000.0
LIMIT = 60 * 2**20


def dot(left, right, dims):
    return lax.dot_general(left, right, dims, preferred_element_type=F)


def once(shape, index):
    return pl.BlockSpec(shape, index, pipeline_mode=pl.Buffered(1))


def key_bias(count):
    row = lax.broadcasted_iota(jnp.int32, (128, 1), 0)
    return jnp.where(row < count, 0.0, masked_score).astype(F)


def masked(scores, text, bias):
    return jnp.concatenate([scores[:text], scores[text:] + bias], axis=0)


def head_lanes(h):
    lane = lax.broadcasted_iota(jnp.int32, (1, 128), 1)
    return (lane < HEAD_DIM) if h == 0 else (lane >= HEAD_DIM)


def pair_forward(q2, k2, v2, text, bias, between):
    vt = v2.T
    outs, logs = [], []
    for h in range(2):
        qh = jnp.where(head_lanes(h), q2, BF(0))
        scores = masked(dot(k2, qh, NT), text, bias)
        top = jnp.max(scores, axis=0, keepdims=True)
        expo = jnp.exp(scores - top)
        total = jnp.sum(expo, axis=0, keepdims=True)
        outs.append(dot(vt[HEAD_DIM * h : HEAD_DIM * (h + 1)], expo.astype(BF), NN) * (1.0 / total))
        logs.append(top + jnp.log(total))
        if h == 0:
            between()
    return jnp.concatenate(outs, axis=0).T.astype(BF), logs


def pair_backward(q2, k2, v2, o2, do2, logs, text, bias, between):
    prod = (do2.astype(F) * o2.astype(F)).T
    kt = (k2 * BF(scale)).T
    dq, dk, dv = [], [], []
    for h in range(2):
        rows = slice(HEAD_DIM * h, HEAD_DIM * (h + 1))
        qh = jnp.where(head_lanes(h), q2, BF(0))
        doh = jnp.where(head_lanes(h), do2, BF(0))
        delta = jnp.sum(prod[rows], axis=0, keepdims=True)
        probs = jnp.exp(masked(dot(k2, qh, NT), text, bias) - logs[h])
        grads = (probs * (dot(v2, doh, NT) - delta)).astype(BF)
        dv.append(dot(probs.astype(BF), do2, NN))
        dk.append(dot(grads, q2, NN))
        dq.append(dot(kt[rows], grads, NN))
        if h == 0:
            between()
    first = head_lanes(0)
    return (
        jnp.concatenate(dq, axis=0).T.astype(BF),
        jnp.where(first, dk[0], dk[1]).astype(BF),
        jnp.where(first, dv[0], dv[1]).astype(BF),
    )


def member_of(align, segs):
    return (align == lax.broadcasted_iota(jnp.int32, (segs, align.shape[1]), 0)).astype(F)


def forward_body(b, j, len_ref, tok_ref, al_ref, w_cols, bias_ref, outs, low_s, hook=lambda at: None):
    base_ref, low_ref, q_ref, k_ref, v_ref, att_ref, lse_ref = outs
    text, width = al_ref.shape[1], tok_ref.shape[2]
    segs = tok_ref.shape[1] - text

    @pl.when(j == 0)
    def _():
        member = member_of(al_ref[pl.ds(b, 1), :], segs)
        counts = jnp.maximum(jnp.sum(member, axis=1, keepdims=True), 1.0)
        tok = tok_ref[0]
        pooled = dot(member.astype(BF), tok[:text], NN) / counts
        seg_base = tok[text:].astype(F) + pooled
        base_ref[0, :text] = tok[:text].astype(F)
        base_ref[0, text:] = seg_base
        low_ref[0, :text] = tok[:text]
        low_ref[0, text:] = seg_base.astype(BF)
        low_s[:text] = tok[:text]
        low_s[text:] = seg_base.astype(BF)

    hook(0)
    low = low_s[...]
    parts = []
    for i, ref in enumerate((q_ref, k_ref, v_ref)):
        at = i * width + j * QUAD
        rows = dot(low, w_cols(pl.ds(pl.multiple_of(at, QUAD), QUAD)), NN)
        if i != 1:
            rows = rows + bias_ref[i // 2 : i // 2 + 1, pl.ds(pl.multiple_of(j * QUAD, QUAD), QUAD)]
        rows = rows.astype(BF)
        if i == 0:
            rows = rows * BF(scale)
        ref[0] = rows
        parts.append(rows)
    bias = key_bias(len_ref[b])
    for pr in range(2):
        cols = slice(128 * pr, 128 * pr + 128)
        out, logs = pair_forward(parts[0][:, cols], parts[1][:, cols], parts[2][:, cols], text, bias, lambda: hook(1 + 2 * pr))
        att_ref[0, :, cols] = out
        for h in range(2):
            lse_ref[0, 0, 2 * pr + h : 2 * pr + h + 1, :] = logs[h]
        hook(2 + 2 * pr)


def forward_kernel(len_ref, tok_ref, al_ref, w_ref, bias_ref, *rest):
    w_cols = lambda cols: w_ref[:, cols]
    forward_body(pl.program_id(0), pl.program_id(1), len_ref, tok_ref, al_ref, w_cols, bias_ref, rest[:7], rest[7])


def forward_attention(seg_lengths, tokens, alignment, w0, biases):
    docs, slots, width = tokens.shape
    quads = width // QUAD
    doc = pl.BlockSpec((1, slots, width), lambda b, j: (b, 0, 0))
    quad = pl.BlockSpec((1, slots, QUAD), lambda b, j: (b, 0, j))
    wide = jax.ShapeDtypeStruct((docs, slots, width), BF)
    return pl.pallas_call(
        forward_kernel,
        grid=(docs, quads),
        in_specs=[
            SMEM,
            doc,
            once(alignment.shape, lambda b, j: (0, 0)),
            once(w0.shape, lambda b, j: (0, 0)),
            once(biases.shape, lambda b, j: (0, 0)),
        ],
        out_specs=[doc, doc, quad, quad, quad, quad, pl.BlockSpec((1, 1, 8, slots), lambda b, j: (b, j, 0, 0))],
        out_shape=[
            jax.ShapeDtypeStruct((docs, slots, width), F),
            wide,
            wide,
            wide,
            wide,
            wide,
            jax.ShapeDtypeStruct((docs, quads, 8, slots), F),
        ],
        scratch_shapes=[pltpu.VMEM((slots, width), BF)],
        compiler_params=pltpu.CompilerParams(vmem_limit_bytes=LIMIT),
    )(seg_lengths, tokens, alignment, w0, biases)


def normal_parts(pre):
    size = jnp.abs(pre)
    dens = jnp.exp2(pre * pre * (-0.5 * 1.4426950408889634))
    t = 1.0 / (1.0 + (0.3275911 * 0.7071067811865476) * size)
    poly = t * (
        0.5 * 0.254829592
        + t * (0.5 * -0.284496736 + t * (0.5 * 1.421413741 + t * (0.5 * -1.453152027 + t * (0.5 * 1.061405429))))
    )
    tail = poly * dens
    return jnp.where(pre >= 0, 1.0 - tail, tail), dens * 0.3989422804014327


def norm_parts(values_in):
    mean = jnp.mean(values_in, axis=-1, keepdims=True)
    centred = values_in - mean
    inverse = lax.rsqrt(jnp.mean(centred * centred, axis=-1, keepdims=True) + norm_eps)
    return centred * inverse, inverse


def norm_back(grad_hat, hat, inverse):
    return inverse * (
        grad_hat
        - jnp.mean(grad_hat, axis=-1, keepdims=True)
        - hat * jnp.mean(grad_hat * hat, axis=-1, keepdims=True)
    )


def col_sum(values):
    return jnp.sum(values, axis=0, keepdims=True)


def mlp_norm(att, base, w_out, vec):
    first = base + dot(att, w_out(), NN) + vec(2)
    hat, inv = norm_parts(first)
    return hat, inv, (hat * vec(3) + vec(4)).astype(BF)


def mlp_units(low, w_in, inner_bias, put, first, ff_cut=768, hook=lambda at: None):
    chunks = inner_bias.shape[1] // ff_cut
    pre_of = lambda c: dot(low, w_in(first + c * ff_cut, ff_cut), NN) + inner_bias[:, c * ff_cut : (c + 1) * ff_cut]
    pre = pre_of(0)
    for c in range(chunks):
        later = pre_of(c + 1) if c + 1 < chunks else None
        phi, dens = normal_parts(pre)
        put(slice(c * ff_cut, (c + 1) * ff_cut), (pre * phi).astype(BF), (phi + pre * dens).astype(BF))
        pre = later
        hook(1 + c)


def mlp_second(hat1, act, w_outer, cot, vec, ff_cut=768):
    second = hat1 * vec(3) + vec(4) + vec(5)
    for c in range(act.shape[1] // ff_cut):
        second = second + dot(act[:, c * ff_cut : (c + 1) * ff_cut], w_outer(c * ff_cut, ff_cut), NN)
    hat, inv = norm_parts(second)
    grad_y = cot.astype(F)
    sums = (col_sum(grad_y * hat), col_sum(grad_y))
    return (hat * vec(6) + vec(7)).astype(BF), norm_back(grad_y * vec(6), hat, inv), sums


def mlp_back(grad_second, gmlp, hat1, inv1, slope, w_outer, w_out, w_in, vec, put, ff_cut=768, hook=lambda at: None):
    grad_normed = grad_second
    chunks = slope.shape[1] // ff_cut
    act_of = lambda c: dot(gmlp, w_outer(c * ff_cut, ff_cut), NT)
    gact = act_of(0)
    for c in range(chunks):
        later = act_of(c + 1) if c + 1 < chunks else None
        cols = slice(c * ff_cut, (c + 1) * ff_cut)
        gpre = (gact * slope[:, cols].astype(F)).astype(BF)
        put("pre", cols, gpre)
        grad_normed = grad_normed + dot(gpre, w_in(c * ff_cut, ff_cut), NT)
        gact = later
        if c == 1:
            hook(1)
    grad_first = norm_back(grad_normed * vec(3), hat1, inv1)
    low = grad_first.astype(BF)
    put("first", grad_first, low, col_sum(grad_normed * hat1), col_sum(grad_normed))
    return dot(low, w_out(), NT).astype(BF)


def mlp_kernel(
    tiles, att_ref, base_ref, cot_ref, w1_ref, w2_ref, vec_ref, ib_ref,
    enc_ref, gf_ref, ga_ref, g1_ref, g2_ref, gv_ref, gib_ref,
    att_s, norm_s, act_s, slope_s, gmlp_s, gpre_s, gbr_s,
):
    i = pl.program_id(0)
    rows, width = att_ref.shape

    @pl.when(i == 0)
    def _():
        gv_ref[...] = jnp.zeros_like(gv_ref)
        gib_ref[...] = jnp.zeros_like(gib_ref)

    @pl.when(i < tiles)
    def _():
        at = pl.ds(pl.multiple_of(i * rows, rows), rows)
        vec = lambda k: vec_ref[k : k + 1, :]
        w_out = lambda: w1_ref[:, :width]
        w_in = lambda c, n: w1_ref[:, width + c : width + c + n]
        w_outer = lambda c, n: w2_ref[c : c + n, :]

        def put_units(cols, act, slope):
            act_s[at, cols], slope_s[:, cols] = act, slope

        def put(kind, *got):
            if kind == "pre":
                gpre_s[at, got[0]] = got[1]
                gib_ref[:, got[0]] += col_sum(got[1].astype(F))
            else:
                gf_ref[...], gbr_s[at] = got[:2]
                gv_ref[2:3] += col_sum(got[1].astype(F))
                gv_ref[3:4] += got[2]
                gv_ref[4:5] += got[3]

        att_s[at] = att_ref[...]
        hat1, inv1, low = mlp_norm(att_ref[...], base_ref[...], w_out, vec)
        norm_s[at] = low
        mlp_units(low, w_in, ib_ref[...], put_units, 0)
        enc_ref[...], grad_second, sums = mlp_second(hat1, act_s[at], w_outer, cot_ref[...], vec)
        gmlp = grad_second.astype(BF)
        gmlp_s[at] = gmlp
        gv_ref[5:6] += col_sum(gmlp.astype(F))
        gv_ref[6:7] += sums[0]
        gv_ref[7:8] += sums[1]
        ga_ref[...] = mlp_back(
            grad_second, gmlp, hat1, inv1, slope_s[...], w_outer, w_out, w_in, vec, put
        )

    @pl.when((i >= tiles) & (i < tiles + 4))
    def _():
        cols = pl.ds(pl.multiple_of((i - tiles) * width, width), width)
        g2_ref[...] = dot(act_s[:, cols], gmlp_s[...], TN).astype(BF)

    @pl.when((i >= tiles + 4) & (i < tiles + 8))
    def _():
        cols = pl.ds(pl.multiple_of((i - tiles - 4) * width, width), width)
        g1_ref[...] = dot(norm_s[...], gpre_s[:, cols], TN).astype(BF)

    @pl.when(i == tiles + 8)
    def _():
        g1_ref[...] = dot(att_s[...], gbr_s[...], TN).astype(BF)


def mlp_both(attended, base, cotangent, w1, w2, vec, inner_bias, rows=320):
    total, width = attended.shape
    ff = inner_bias.shape[1]
    tiles = total // rows
    tile = pl.BlockSpec((rows, width), lambda i: (jnp.minimum(i, tiles - 1), 0))
    whole = lambda shape: once(shape, lambda i: (0, 0))
    return pl.pallas_call(
        functools.partial(mlp_kernel, tiles),
        grid=(tiles + 9,),
        in_specs=[tile, tile, tile, whole(w1.shape), whole(w2.shape), whole(vec.shape), whole(inner_bias.shape)],
        out_specs=[
            tile,
            tile,
            tile,
            pl.BlockSpec((width, width), lambda i: (0, jnp.where(i == tiles + 8, 0, jnp.clip(i - tiles - 4, 0, 3) + 1))),
            pl.BlockSpec((width, width), lambda i: (jnp.clip(i - tiles, 0, 3), 0)),
            whole((8, width)),
            whole((1, ff)),
        ],
        out_shape=[
            jax.ShapeDtypeStruct((total, width), BF),
            jax.ShapeDtypeStruct((total, width), F),
            jax.ShapeDtypeStruct((total, width), BF),
            jax.ShapeDtypeStruct((width, width + ff), BF),
            jax.ShapeDtypeStruct((ff, width), BF),
            jax.ShapeDtypeStruct((8, width), F),
            jax.ShapeDtypeStruct((1, ff), F),
        ],
        scratch_shapes=[
            pltpu.VMEM((total, width), BF),
            pltpu.VMEM((total, width), BF),
            pltpu.VMEM((total, ff), BF),
            pltpu.VMEM((rows, ff), BF),
            pltpu.VMEM((total, width), BF),
            pltpu.VMEM((total, ff), BF),
            pltpu.VMEM((total, width), BF),
        ],
        compiler_params=pltpu.CompilerParams(vmem_limit_bytes=LIMIT),
    )(attended, base, cotangent, w1, w2, vec, inner_bias)


def backward_body(j, b, refs, keep, gt_ref, scratch, hook=lambda at: None, later=None):
    len_ref, al_ref, q_ref, k_ref, v_ref, o_ref, do_ref, lse_ref, low_ref, gf_ref, w_ref = refs
    gbase_s, acc_s, vsum_s = scratch
    text, width = al_ref.shape[1], low_ref.shape[2]
    quads = width // QUAD
    align = al_ref[pl.ds(b, 1), :]

    hook(0)
    bias = key_bias(len_ref[b])
    parts = [[], [], []]
    for pr in range(2):
        cols = slice(128 * pr, 128 * pr + 128)
        logs = [lse_ref[0, 0, 2 * pr + h : 2 * pr + h + 1, :] for h in range(2)]
        got = pair_backward(
            q_ref[0, :, cols], k_ref[0, :, cols], v_ref[0, :, cols], o_ref[0, :, cols], do_ref[0, :, cols], logs, text, bias,
            lambda: hook(1 + 2 * pr),
        )
        for i in range(3):
            parts[i].append(got[i])
        if pr == 0:
            hook(2)
    quad_grads = [jnp.concatenate(p, axis=1) for p in parts]
    cols = pl.ds(pl.multiple_of(j * QUAD, QUAD), QUAD)

    if later is None:

        @pl.when(j == 0)
        def _():
            gbase_s[b] = gf_ref[0]

        gbase = gbase_s[b]
        for i in range(3):
            at = pl.ds(pl.multiple_of(i * width + j * QUAD, QUAD), QUAD)
            gbase = gbase + dot(quad_grads[i], w_ref[:, at], NT)
        gbase_s[b] = gbase
    else:
        later(quad_grads)

    low = low_ref[0]
    weight = [dot(low, g, TN) for g in quad_grads]
    sums = [col_sum(quad_grads[0].astype(F)), col_sum(quad_grads[2].astype(F))]

    @pl.when(b == 0)
    def _():
        for i in range(3):
            acc_s[i] = weight[i]
        for i in range(2):
            vsum_s[i : i + 1, cols] = sums[i]

    @pl.when(b == 1)
    def _():
        for i in range(2):
            vsum_s[i : i + 1, cols] += sums[i]
        keep(lambda i: (acc_s[i] + weight[i]).astype(BF))

    if later is None:

        @pl.when(j == quads - 1)
        def _():
            gt_ref[0] = token_grads(gbase, align, text)

    hook(4)


def token_grads(gbase, align, text):
    member = member_of(align, gbase.shape[0] - text)
    counts = jnp.maximum(jnp.sum(member, axis=1, keepdims=True), 1.0)
    share = gbase[text:] / counts
    high = share.astype(BF)
    rest = (share - high.astype(F)).astype(BF)
    sel = member.astype(BF)
    spread = dot(sel, high, TN) + dot(sel, rest, TN)
    return jnp.concatenate([gbase[:text] + spread, gbase[text:]], axis=0).astype(BF)


def vector_cols(vsum_s, gv_ref, gib_ref, cols_s):
    width = gv_ref.shape[1]
    rows = jnp.concatenate([vsum_s[:2], gv_ref[2:], jnp.zeros((120, width), F)], axis=0)
    cols_s[...] = jnp.zeros_like(cols_s)
    share = gib_ref.shape[1] * 24 // width
    for d in range(width // 24):
        cols_s[24 * d : 24 * d + 1, :share] = gib_ref[:, d * share : (d + 1) * share]
    return jnp.concatenate([rows.T, cols_s[...]], axis=1).astype(BF)


def backward_kernel(*refs):
    vsum_ref, gt_ref = refs[14:16]

    def keep(grad):
        for i in range(3):
            refs[11 + i][...] = grad(i)

    backward_body(pl.program_id(0), pl.program_id(1), refs[:11], keep, gt_ref, [refs[16], refs[17], vsum_ref])


def backward_attention(seg_lengths, alignment, q, k, v, att, gatt, lse, low, gfirst, w0):
    docs, slots, width = low.shape
    quads = width // QUAD
    quad = pl.BlockSpec((1, slots, QUAD), lambda j, b: (b, 0, j))
    doc = pl.BlockSpec((1, slots, width), lambda j, b: (b, 0, 0))
    wide = jax.ShapeDtypeStruct((width, width), BF)
    col = pl.BlockSpec((width, QUAD), lambda j, b: (0, j))
    return pl.pallas_call(
        backward_kernel,
        grid=(quads, docs),
        in_specs=[
            SMEM,
            once(alignment.shape, lambda j, b: (0, 0)),
            quad,
            quad,
            quad,
            quad,
            quad,
            pl.BlockSpec((1, 1, 8, slots), lambda j, b: (b, j, 0, 0)),
            doc,
            pl.BlockSpec((1, slots, width), lambda j, b: (jnp.where(j == 0, b, 1), 0, 0)),
            once(w0.shape, lambda j, b: (0, 0)),
        ],
        out_specs=[
            col,
            col,
            col,
            once((8, width), lambda j, b: (0, 0)),
            pl.BlockSpec((1, slots, width), lambda j, b: (jnp.where(j == quads - 1, b, 0), 0, 0)),
        ],
        out_shape=[wide, wide, wide, jax.ShapeDtypeStruct((8, width), F), jax.ShapeDtypeStruct((docs, slots, width), BF)],
        scratch_shapes=[
            pltpu.VMEM((docs, slots, width), F),
            pltpu.VMEM((3, width, QUAD), F),
        ],
        compiler_params=pltpu.CompilerParams(vmem_limit_bytes=LIMIT),
    )(seg_lengths, alignment, q, k, v, att, gatt, lse, low, gfirst, w0)


def at_slots(plan, step, slot):
    for (when, where), calls in plan.items():
        if where == slot:

            @pl.when(step == when)
            def _():
                for call in calls:
                    call()


def each(fn, *backs):
    return [functools.partial(fn, k) for k in backs]


TILE = 320
TILES = 4
ATTEND = 6


def forward_fused_kernel(
    len_ref, tok_ref, al_ref, wq, wk, wv, wo, wi, s2, vp, *rest
):
    low_ref, q_ref, k_ref, v_ref, att_ref, lse_ref = rest[:6]
    hat_ref, inv_ref, norm_ref, act_ref, slope_ref, vec_ref, w0, wa, wb, w2 = rest[6:16]
    (
        low_s, base_s, att_s, norm_s, w0_s, wa_s, wb_s, ib_s, cols_s, s0, sa, sb, land0, landa, landb, own0, owna, ownb,
        pair_sem, local, send, recv,
    ) = rest[16:]
    step = pl.program_id(0)
    width, ff = tok_ref.shape[2], wi.shape[1]
    place = Place()
    pairs = [
        Pair(place, s0, land0, own0, pair_sem.at[0], pair_sem.at[1]),
        Pair(place, sa, landa, owna, pair_sem.at[2], pair_sem.at[3]),
        Pair(place, sb, landb, ownb, pair_sem.at[4], pair_sem.at[5]),
    ]
    g0 = Gather(place, w0_s, own0, send.at[0], recv.at[0], local.at[0], w0.shape[2])
    ga = Gather(place, wa_s, owna, send.at[1], recv.at[1], local.at[1], wa.shape[2])
    gb = Gather(place, wb_s, ownb, send.at[2], recv.at[2], local.at[2], wb.shape[2])
    g2 = Gather(place, w2, s2, send.at[3], recv.at[3], local.at[3])
    saves = [
        lambda: pltpu.make_async_copy(w0_s, w0, local.at[4]),
        lambda: pltpu.make_async_copy(wa_s, wa, local.at[5]),
        lambda: pltpu.make_async_copy(wb_s, wb, local.at[6]),
    ]
    half = ff // 2
    start_of = lambda k: lambda: saves[k]().start()
    wait_of = lambda k: lambda: saves[k]().wait()

    def pack():
        for i, ref in enumerate((wq, wk, wv)):
            s0[:, i * width : (i + 1) * width] = ref[...].astype(F)
        cols_s[:128] = jnp.zeros((128, 128), F)
        for k in range(8):
            cols_s[k : k + 1, :24] = vp[:, 24 * k : 24 * k + 24]
        s0[:, 3 * width : 3 * width + 128] = cols_s[:128].T[:24]
        s0[:, 3 * width + 128 :] = jnp.zeros((24, 128), F)
        share = ff * 24 // width
        s0[0:1, 3 * width + 128 : 3 * width + 128 + share] = vp[:, 192 : 192 + share]

    def pack_rest():
        sa[:, :width] = wo[...].astype(F)
        sa[:, width:] = wi[:, :half].astype(F)
        sb[...] = wi[:, half:].astype(F)

    def vectors():
        cols = w0_s[:, :, 3 * width : 3 * width + 128].reshape(width, 128).astype(F)
        vec_ref[...] = cols.T[:8]
        cols_s[...] = w0_s[:, :, 3 * width + 128 :].reshape(width, 128).astype(F)
        share = ff * 24 // width
        for d in range(width // 24):
            ib_s[:, d * share : (d + 1) * share] = cols_s[24 * d : 24 * d + 1, :share]

    attend_plan = {
        (0, -1): [
            pack, place.barrier, pairs[0].start, pack_rest, pairs[1].start, pairs[2].start, pairs[0].done, g0.along_z,
            functools.partial(g0.to_neighbours, 0), pairs[1].done, pairs[2].done,
        ],
        (0, 0): [
            *each(g0.to_neighbours, 1), *each(g0.to_diagonal, 0), *each(g0.to_neighbours, 2), *each(g0.to_diagonal, 1),
            *each(g0.to_neighbours, 3), ga.along_z, *each(g0.to_core, 0), *each(g0.to_diagonal, 2),
            *each(ga.to_neighbours, 0), *each(g0.to_core, 1), *each(g0.to_diagonal, 3), *each(g0.to_core, 2, 3),
            *each(ga.to_neighbours, 1), g0.finish, start_of(0), vectors,
        ],
        (0, 1): [*each(ga.to_diagonal, 0), *each(ga.to_neighbours, 2)],
        (0, 2): [gb.along_z],
        (0, 3): each(ga.to_diagonal, 1),
        (0, 4): [*each(ga.to_neighbours, 3), *each(gb.to_neighbours, 0)],
        (1, 1): each(ga.to_core, 0),
        (1, 2): [*each(ga.to_diagonal, 2), *each(gb.to_neighbours, 1)],
        (1, 4): each(ga.to_core, 1),
        (2, 1): [*each(ga.to_diagonal, 3), *each(gb.to_neighbours, 2)],
        (2, 2): each(gb.to_diagonal, 0),
        (2, 3): [g2.along_z, *each(ga.to_core, 2)],
        (2, 4): [*each(gb.to_neighbours, 3), *each(gb.to_diagonal, 1)],
        (3, 1): [*each(ga.to_core, 3), *each(g2.to_neighbours, 0)],
        (3, 3): [*each(gb.to_diagonal, 2), *each(gb.to_core, 0)],
        (3, 4): each(g2.to_neighbours, 1),
        (4, 1): [*each(gb.to_diagonal, 3), *each(gb.to_core, 1)],
        (4, 3): [*each(g2.to_diagonal, 0), *each(gb.to_core, 2)],
        (4, 4): each(g2.to_neighbours, 2),
        (5, 1): [*each(gb.to_core, 3), *each(g2.to_diagonal, 1)],
        (5, 3): each(g2.to_neighbours, 3),
    }
    mlp_plan = {
        (6, 0): [ga.finish, start_of(1)],
        (6, 1): each(g2.to_core, 0),
        (6, 5): each(g2.to_diagonal, 2),
        (7, 2): each(g2.to_core, 1),
        (8, 1): each(g2.to_diagonal, 3),
        (9, 1): each(g2.to_core, 2),
        (10, 0): [gb.finish, start_of(2)],
        (10, 2): each(g2.to_core, 3),
        (13, 5): [
            g2.finish, wait_of(0), wait_of(1), wait_of(2), g0.drain, ga.drain, gb.drain, g2.drain,
        ],
    }

    @pl.when(step < ATTEND)
    def _():
        at_slots(attend_plan, step, -1)
        b, j = step // 3, step % 3
        outs = (base_s.at[pl.ds(b, 1)], low_ref, q_ref, k_ref, v_ref, att_ref, lse_ref)
        w_cols = lambda cols: w0_s[:, :, cols].reshape(width, QUAD)
        hook = functools.partial(at_slots, attend_plan, step)
        forward_body(b, j, len_ref, tok_ref, al_ref, w_cols, vec_ref, outs, low_s, hook)
        att_s[b, :, pl.ds(pl.multiple_of(j * QUAD, QUAD), QUAD)] = att_ref[0]

    @pl.when(step >= ATTEND)
    def _():
        hook = functools.partial(at_slots, mlp_plan, step)
        hook(0)
        first_plan = {at: calls for at, calls in mlp_plan.items() if at[0] < ATTEND + TILES}
        second_plan = {at: calls for at, calls in mlp_plan.items() if at[0] >= ATTEND + TILES}
        t = (step - ATTEND) % TILES
        here = pl.ds(pl.multiple_of(t * TILE, TILE), TILE)
        vec = lambda k: vec_ref[k : k + 1, :]

        def put(cols, act, slope):
            act_ref[:, cols], slope_ref[:, cols] = act, slope

        @pl.when(step < ATTEND + TILES)
        def _():
            rows = pl.ds(pl.multiple_of((t % 2) * TILE, TILE), TILE)
            w_out = lambda: wa_s[:, :, :width].reshape(width, width)
            w_in = lambda c, n: wa_s[:, :, width + c : width + c + n].reshape(width, n)
            hat, inv, low = mlp_norm(att_s[t // 2, rows], base_s[t // 2, rows], w_out, vec)
            hat_ref[...] = hat
            inv_ref[...] = jnp.broadcast_to(inv, inv_ref.shape)
            norm_ref[...] = low
            norm_s[here] = low
            mlp_units(low, w_in, ib_s[:, :half], put, 0, hook=functools.partial(at_slots, first_plan, step))

        @pl.when(step >= ATTEND + TILES)
        def _():
            w_in = lambda c, n: wb_s[:, :, c : c + n].reshape(width, n)
            mlp_units(norm_s[here], w_in, ib_s[:, half:], put, 0, hook=functools.partial(at_slots, second_plan, step))

        hook(5)


def forward_fused(seg_lengths, tokens, alignment, wq, wk, wv, wo, wi, s2, vp):
    docs, slots, width = tokens.shape
    ff = wi.shape[1]
    quads = width // QUAD
    n0, na, nb = 3 * width + 256, width + ff // 2, ff // 2
    total = docs * slots
    last = ATTEND - 1
    doc_of = lambda s: jnp.minimum(s, last) // quads
    doc = pl.BlockSpec((1, slots, width), lambda s: (doc_of(s), 0, 0))
    quad = pl.BlockSpec((1, slots, QUAD), lambda s: (doc_of(s), 0, jnp.minimum(s, last) % quads))
    wide = jax.ShapeDtypeStruct((docs, slots, width), BF)
    full = lambda *shape: once(shape, lambda s: (0,) * len(shape))
    tile = lambda n: pl.BlockSpec((TILE, n), lambda s: (jnp.clip(s - ATTEND, 0, TILES - 1), 0))
    past = lambda s: jnp.maximum(s - ATTEND, 0)
    units = pl.BlockSpec((TILE, ff // 2), lambda s: (past(s) % TILES, past(s) // TILES))
    ins = (alignment, wq, wk, wv, wo, wi, s2, vp)
    return pl.pallas_call(
        forward_fused_kernel,
        grid=(ATTEND + 2 * TILES,),
        in_specs=[SMEM, doc] + [full(*a.shape) for a in ins],
        out_specs=[
            doc, quad, quad, quad, quad,
            pl.BlockSpec((1, 1, 8, slots), lambda s: (doc_of(s), jnp.minimum(s, last) % quads, 0, 0)),
            tile(width), tile(128), tile(width), units, units, full(8, width),
        ]
        + [ANY] * 4,
        out_shape=[
            wide,
            wide,
            wide,
            wide,
            wide,
            jax.ShapeDtypeStruct((docs, quads, 8, slots), F),
            jax.ShapeDtypeStruct((total, width), F),
            jax.ShapeDtypeStruct((total, 128), F),
            jax.ShapeDtypeStruct((total, width), BF),
            jax.ShapeDtypeStruct((total, ff), BF),
            jax.ShapeDtypeStruct((total, ff), BF),
            jax.ShapeDtypeStruct((8, width), F),
            *[jax.ShapeDtypeStruct((CHIPS, 48, n), BF) for n in (n0, na, nb)],
            jax.ShapeDtypeStruct((CHIPS, 2, 96, width), BF),
        ],
        scratch_shapes=[
            pltpu.VMEM((slots, width), BF),
            pltpu.VMEM((docs, slots, width), F),
            pltpu.VMEM((docs, slots, width), BF),
            pltpu.VMEM((total, width), BF),
            *[pltpu.VMEM((CHIPS, 48, n), BF) for n in (n0, na, nb)],
            pltpu.VMEM((1, ff), F),
            pltpu.VMEM((width, 128), F),
            *[pltpu.VMEM((24, n), F) for n in (n0, na, nb)],
            *[pltpu.VMEM((24, n // 2), F) for n in (n0, na, nb)],
            *[pltpu.VMEM((48, n // 2), BF) for n in (n0, na, nb)],
            pltpu.SemaphoreType.DMA((6,)),
            pltpu.SemaphoreType.DMA((7,)),
            pltpu.SemaphoreType.DMA((4, Gather.SEMS)),
            pltpu.SemaphoreType.DMA((4, Gather.SEMS)),
        ],
        compiler_params=pltpu.CompilerParams(collective_id=0, has_side_effects=True, vmem_limit_bytes=LIMIT),
    )(seg_lengths, tokens, *ins)


def middle_kernel(hat_ref, inv_ref, cot_ref, vec_ref, *rest):
    act_h, slope_h, norm_h, att_h, wa_h, wb_h, w2_h = rest[:7]
    enc_ref, gf_ref, ga_ref, g1_ref, gv_ref, gib_ref, o_outer = rest[7:14]
    act_s, slope_s, wa_s, wb_s, w2_s, gsec_s, gmlp_s, g2_s = rest[14:22]
    bufs = rest[22:29]
    load_sem, local, send, recv = rest[29:]
    i = pl.program_id(0)
    rows, width = hat_ref.shape
    norm_s, att_s, gbr_s = (act_s.at[:, pl.ds(k * width, width)] for k in range(3))
    tiles = act_s.shape[0] // rows
    place = Place()
    g2 = Scatter(place, g2_s, bufs, o_outer, send.at[0], recv.at[0], local.at[0])

    cut = lambda t: pl.ds(t * rows, rows)
    loads = [lambda: pltpu.make_async_copy(w2_h, w2_s, load_sem.at[0])]
    for t in range(tiles):
        loads.append(lambda t=t: pltpu.make_async_copy(act_h.at[cut(t)], act_s.at[cut(t)], load_sem.at[1 + t]))
    for t in range(tiles):
        loads.append(lambda t=t: pltpu.make_async_copy(slope_h.at[cut(t)], slope_s.at[cut(t)], load_sem.at[5 + t]))
    loads += [
        lambda: pltpu.make_async_copy(wa_h, wa_s, load_sem.at[9]),
        lambda: pltpu.make_async_copy(norm_h, norm_s, load_sem.at[10]),
        lambda: pltpu.make_async_copy(att_h, att_s, load_sem.at[11]),
        lambda: pltpu.make_async_copy(wb_h, wb_s, load_sem.at[12]),
    ]
    wait = lambda k: lambda: loads[k]().wait()
    loads_start = lambda k: lambda: loads[k]().start()

    def begin():
        for load in loads[:2]:
            load().start()
        gv_ref[...] = jnp.zeros_like(gv_ref)
        gib_ref[...] = jnp.zeros_like(gib_ref)
        place.barrier()

    plan = {
        (0, 0): [begin, wait(0), wait(1), *map(loads_start, (2, 3, 4))],
        (1, 0): [wait(2)],
        (2, 0): [wait(3)],
        (3, 0): [wait(4), *map(loads_start, (9, 12, 5))],
        (5, 0): [*map(loads_start, (6, 7, 8))],
        (4, 2): each(g2.from_sibling, 3),
        (5, 2): each(g2.from_sibling, 2),
        (6, 2): each(g2.from_sibling, 1),
        (7, 2): each(g2.from_sibling, 0),
        (6, 0): each(g2.to_diagonal, 3),
        (7, 0): each(g2.to_diagonal, 2),
        (8, 0): [loads_start(10), loads_start(11), wait(9), wait(12), wait(5), *each(g2.to_diagonal, 1)],
        (8, 1): [*each(g2.to_diagonal, 0), *each(g2.to_neighbours, 3)],
        (8, 2): each(g2.to_neighbours, 2),
        (9, 0): [wait(6)],
        (9, 1): each(g2.to_neighbours, 1),
        (9, 2): each(g2.to_neighbours, 0),
        (10, 0): [wait(7)],
        (10, 1): each(g2.along_z, 3),
        (10, 2): each(g2.along_z, 2),
        (11, 0): [wait(8)],
        (11, 2): each(g2.along_z, 1),
        (12, 0): [wait(10)],
        (12, 2): each(g2.along_z, 0),
        (16, 0): [wait(11)],
        (16, 2): [g2.owner, g2.drain],
    }
    hook = functools.partial(at_slots, plan, i)
    hook(0)
    vec = lambda k: vec_ref[k : k + 1, :]
    w_outer = lambda c, n: w2_s[c * CHIPS // act_s.shape[1] : (c + n) * CHIPS // act_s.shape[1]].reshape(n, width)

    @pl.when(i < tiles)
    def _():
        at = pl.ds(pl.multiple_of(i * rows, rows), rows)
        enc_ref[...], grad_second, sums = mlp_second(hat_ref[...], act_s[at], w_outer, cot_ref[...], vec)
        gsec_s[at] = grad_second
        gmlp = grad_second.astype(BF)
        gmlp_s[at] = gmlp
        gv_ref[5:6] += col_sum(gmlp.astype(F))
        gv_ref[6:7] += sums[0]
        gv_ref[7:8] += sums[1]

    @pl.when((i >= tiles) & (i < 2 * tiles))
    def _():
        plane = place.plane(2 * tiles - 1 - i)
        cols = pl.ds(pl.multiple_of(plane * width, width), width)
        g2_s[pl.ds(4 * plane, 4)] = dot(act_s[:, cols], gmlp_s[...], TN).astype(BF).reshape(4, 2, 96, width)

    @pl.when((i >= 2 * tiles) & (i < 3 * tiles))
    def _():
        at = pl.ds(pl.multiple_of((i - 2 * tiles) * rows, rows), rows)

        def put(kind, *got):
            if kind == "pre":
                slope_s[at, got[0]] = got[1]
                gib_ref[:, got[0]] += col_sum(got[1].astype(F))
            else:
                gf_ref[...], gbr_s[at] = got[:2]
                gv_ref[2:3] += col_sum(got[1].astype(F))
                gv_ref[3:4] += got[2]
                gv_ref[4:5] += got[3]

        half = wb_s.shape[2]
        w_out = lambda: wa_s[:, :, :width].reshape(width, width)

        def w_in(c, n):
            part = wa_s[:, :, width + c : width + c + n] if c < half else wb_s[:, :, c - half : c - half + n]
            return part.reshape(width, n)

        ga_ref[...] = mlp_back(
            gsec_s[at], gmlp_s[at], hat_ref[...], inv_ref[:, 0:1], slope_s[at], w_outer, w_out, w_in, vec, put, hook=hook
        )

    @pl.when((i >= 3 * tiles) & (i < 4 * tiles))
    def _():
        cols = pl.ds(pl.multiple_of((i - 3 * tiles) * width, width), width)
        g1_ref[...] = dot(norm_s[...], slope_s[:, cols], TN).astype(BF)

    @pl.when(i == 4 * tiles)
    def _():
        g1_ref[...] = dot(att_s[...], gbr_s[...], TN).astype(BF)

    hook(2)


def middle(hat, inv, cotangent, vec, act, slope, norm, att, wa, wb, w2):
    total, width = hat.shape
    ff = act.shape[1]
    tiles = total // TILE
    early = lambda n: pl.BlockSpec((TILE, n), lambda i: (jnp.minimum(i, tiles - 1), 0))
    late = lambda n: pl.BlockSpec((TILE, n), lambda i: (jnp.clip(i - 2 * tiles, 0, tiles - 1), 0))
    full = lambda *shape: once(shape, lambda i: (0,) * len(shape))
    return pl.pallas_call(
        middle_kernel,
        grid=(4 * tiles + 1,),
        in_specs=[
            pl.BlockSpec(
                (TILE, width),
                lambda i: (jnp.where(i < 2 * tiles, jnp.minimum(i, tiles - 1), jnp.minimum(i - 2 * tiles, tiles - 1)), 0),
            ),
            late(128),
            early(width),
            full(8, width),
        ]
        + [ANY] * 7,
        out_specs=[
            early(width),
            late(width),
            late(width),
            pl.BlockSpec((width, width), lambda i: (0, jnp.where(i == 4 * tiles, 0, jnp.clip(i - 3 * tiles, 0, 3) + 1))),
            full(8, width),
            full(1, ff),
            full(96, width),
        ],
        out_shape=[
            jax.ShapeDtypeStruct((total, width), BF),
            jax.ShapeDtypeStruct((total, width), F),
            jax.ShapeDtypeStruct((total, width), BF),
            jax.ShapeDtypeStruct((width, width + ff), BF),
            jax.ShapeDtypeStruct((8, width), F),
            jax.ShapeDtypeStruct((1, ff), F),
            jax.ShapeDtypeStruct((96, width), F),
        ],
        scratch_shapes=[
            pltpu.VMEM((total, ff), BF),
            pltpu.VMEM((total, ff), BF),
            pltpu.VMEM(wa.shape, BF),
            pltpu.VMEM(wb.shape, BF),
            pltpu.VMEM(w2.shape, BF),
            pltpu.VMEM((total, width), F),
            pltpu.VMEM((total, width), BF),
            pltpu.VMEM(w2.shape, BF),
            *Scatter.scratch(96, width, False),
            pltpu.SemaphoreType.DMA((13,)),
            pltpu.SemaphoreType.DMA((1, 4)),
            pltpu.SemaphoreType.DMA((1, Scatter.SEMS)),
            pltpu.SemaphoreType.DMA((1, Scatter.SEMS)),
        ],
        compiler_params=pltpu.CompilerParams(collective_id=2, has_side_effects=True, vmem_limit_bytes=LIMIT),
    )(hat, inv, cotangent, vec, act, slope, norm, att, wa, wb, w2)


def backward_fused_kernel(widths, *refs):
    ins, (gv_ref, gib_ref, g1_ref) = refs[:11], refs[11:14]
    gt_ref, o_wide, o_inner, o_vec, o_ib = refs[14], refs[15:19], refs[19], refs[20], refs[21]
    scratch, cols_s, gqkv_s, w_s, gf_sem = refs[22:25], refs[25], refs[26], refs[27], refs[28]
    rest = list(refs[29:])
    local, send, recv = rest[-3:]
    j, b = pl.program_id(0), pl.program_id(1)
    step = 2 * j + b
    width = ins[8].shape[2]
    place = Place()
    take = lambda n: [rest.pop(0) for _ in range(n)]
    quad_s, stage = take(3), take(1)[0]
    sources = [g1_ref, *quad_s]
    groups = []
    for i, (src, wide) in enumerate(zip(sources, widths)):
        out = stage.at[:, pl.ds(0, wide)]
        groups.append(Scatter(place, src, take(9), out, send.at[i], recv.at[i], local.at[i], wide))
    g1, q0, q1, q2 = groups

    def give_rest():
        g1.finish()
        o_wide[3][...] = stage[:, :width]
        o_inner[...] = stage[:, width : widths[0]]

    def give_quad(k):
        groups[1 + k].finish()
        for i in range(3):
            o_wide[i][:, k * QUAD : (k + 1) * QUAD] = stage[:, i * QUAD : (i + 1) * QUAD]
        if k == 2:
            o_vec[...] = stage[:, 3 * QUAD : 3 * QUAD + 128].T[:8]
            o_ib[...] = stage[0:1, 3 * QUAD + 128 : 4 * QUAD]

    def keep(grad):
        for k in range(3):

            @pl.when(j == k)
            def _():
                for i in range(3):
                    quad_s[k][:, :, i * QUAD : (i + 1) * QUAD] = grad(i).reshape(CHIPS, 48, QUAD)
                if k == 2:
                    both = vector_cols(scratch[2], gv_ref, gib_ref, cols_s)
                    quad_s[k][:, :, 3 * QUAD :] = both.reshape(CHIPS, 48, QUAD)

    al_ref, gf_h, w_h, gf_s = ins[1], ins[9], ins[10], scratch[0]
    load_w = lambda: pltpu.make_async_copy(w_h, w_s, gf_sem.at[1])
    load = lambda: pltpu.make_async_copy(gf_h, gf_s, gf_sem.at[0])

    def later(grads):
        for i, grad in enumerate(grads):
            gqkv_s[b, :, pl.ds(pl.multiple_of(i * width + j * QUAD, QUAD), QUAD)] = grad

    def tokens_of(doc):
        gbase = gf_s[doc] + dot(gqkv_s[doc], w_s[:, : 3 * width], NT)
        gt_ref[doc] = token_grads(gbase, al_ref[doc : doc + 1, :], al_ref.shape[1])

    late, soon = (3, 2), (1, 0)
    all4 = late + soon
    plan = {
        (0, 0): [place.barrier, *each(g1.from_sibling, *all4), lambda: load().start(), lambda: load_w().start()],
        (0, 2): each(g1.to_diagonal, 3),
        (0, 4): each(g1.to_diagonal, 2, 1, 0),
        (1, 2): each(g1.to_neighbours, 3),
        (1, 4): [*each(g1.to_neighbours, 2, 1, 0), *each(q0.from_sibling, *all4)],
        (2, 2): each(g1.along_z, 3),
        (2, 4): [*each(g1.along_z, 2), *each(q0.to_diagonal, *all4)],
        (3, 2): each(g1.along_z, 1),
        (3, 4): [*each(g1.along_z, 0), *each(q0.to_neighbours, *all4), *each(q1.from_sibling, *all4)],
        (4, 2): each(q1.to_diagonal, *all4),
        (4, 4): [*each(q0.along_z, *all4), *each(q1.to_neighbours, *all4)],
        (5, 2): [g1.owner],
        (5, 4): [
            *each(q2.from_sibling, *all4), lambda: load().wait(), lambda: load_w().wait(), *each(q2.to_diagonal, *all4),
            *each(q1.along_z, *all4), functools.partial(tokens_of, 0), *each(q2.to_neighbours, *all4),
            functools.partial(tokens_of, 1), *each(q2.along_z, *all4), q0.owner, q1.owner, give_rest,
            functools.partial(give_quad, 0), functools.partial(give_quad, 1), q2.owner, functools.partial(give_quad, 2),
            *[g.drain for g in groups],
        ],
    }
    backward_body(j, b, ins, keep, gt_ref, scratch, functools.partial(at_slots, plan, step), later)


def backward_fused(seg_lengths, alignment, q, k, v, att, gatt, lse, low, gfirst, w0, gv, gib, g1):
    docs, slots, width = low.shape
    quads = width // QUAD
    quad = pl.BlockSpec((1, slots, QUAD), lambda j, b: (b, 0, j))
    doc = pl.BlockSpec((1, slots, width), lambda j, b: (b, 0, 0))
    whole = lambda *shape: once(shape, lambda j, b: (0,) * len(shape))
    n1 = g1.shape[2]
    widths = (n1, 3 * QUAD, 3 * QUAD, 4 * QUAD)
    bufs = []
    for wide in widths:
        bufs += Scatter.scratch(48, wide // 2, True)
    n = len(widths)
    shard = jax.ShapeDtypeStruct((24, width), F)
    return pl.pallas_call(
        functools.partial(backward_fused_kernel, widths),
        grid=(quads, docs),
        in_specs=[
            SMEM,
            whole(*alignment.shape),
            quad,
            quad,
            quad,
            quad,
            quad,
            pl.BlockSpec((1, 1, 8, slots), lambda j, b: (b, j, 0, 0)),
            doc,
            ANY,
            ANY,
            whole(*gv.shape),
            whole(*gib.shape),
            ANY,
        ],
        out_specs=[
            whole(docs, slots, width),
            *[whole(24, width)] * 4,
            whole(24, n1 - width),
            whole(8, 24),
            whole(1, 128),
        ],
        out_shape=[
            jax.ShapeDtypeStruct((docs, slots, width), BF),
            shard,
            shard,
            shard,
            shard,
            jax.ShapeDtypeStruct((24, n1 - width), F),
            jax.ShapeDtypeStruct((8, 24), F),
            jax.ShapeDtypeStruct((1, 128), F),
        ],
        scratch_shapes=[
            pltpu.VMEM((docs, slots, width), F),
            pltpu.VMEM((3, width, QUAD), F),
            pltpu.VMEM((8, width), F),
            pltpu.VMEM((width, 128), F),
            pltpu.VMEM((docs, slots, 3 * width), BF),
            pltpu.VMEM(w0.shape, BF),
            pltpu.SemaphoreType.DMA((2,)),
            *[pltpu.VMEM((CHIPS, 48, wide), BF) for wide in widths[1:]],
            pltpu.VMEM((24, n1), F),
            *bufs,
            pltpu.SemaphoreType.DMA((n, 4)),
            pltpu.SemaphoreType.DMA((n, Scatter.SEMS)),
            pltpu.SemaphoreType.DMA((n, Scatter.SEMS)),
        ],
        compiler_params=pltpu.CompilerParams(collective_id=1, has_side_effects=True, vmem_limit_bytes=LIMIT),
    )(seg_lengths, alignment, q, k, v, att, gatt, lse, low, gfirst, w0, gv, gib, g1)


def deliver_kernel(count, *refs):
    ins, sums, gib = refs[:count], refs[count], refs[count + 1]
    outs, vecs, ib_out = refs[count + 2 : 2 * count + 2], refs[2 * count + 2 : 2 * count + 10], refs[2 * count + 10]
    held, sem_in, sem_out = refs[2 * count + 11 : 3 * count + 11], refs[-2], refs[-1]
    loads = [pltpu.make_async_copy(a, b, sem_in.at[i]) for i, (a, b) in enumerate(zip(ins, held))]
    stores = [pltpu.make_async_copy(a, b, sem_out.at[i]) for i, (a, b) in enumerate(zip(held, outs))]
    for c in loads:
        c.start()
    for k, out in enumerate(vecs):
        out[...] = sums[k, :]
    ib_out[...] = gib[0, : ib_out.shape[0]]
    for i in range(count):
        loads[i].wait()
        stores[i].start()
    for c in stores:
        c.wait()


def deliver(arrays, sums, gib, share):
    n = len(arrays)
    return pl.pallas_call(
        functools.partial(deliver_kernel, n),
        out_shape=[jax.ShapeDtypeStruct(a.shape, a.dtype) for a in arrays]
        + [jax.ShapeDtypeStruct((sums.shape[1],), F)] * 8
        + [jax.ShapeDtypeStruct((share,), F)],
        in_specs=[ANY] * n + [VMEM] * 2,
        out_specs=[ANY] * n + [VMEM] * 9,
        scratch_shapes=[pltpu.VMEM(a.shape, a.dtype) for a in arrays] + [pltpu.SemaphoreType.DMA((n,))] * 2,
        compiler_params=pltpu.CompilerParams(vmem_limit_bytes=LIMIT),
    )(*arrays, sums, gib)


def own_kernels(shard_rows, docs):
    return lax.axis_size("dp") == PLANES and lax.axis_size("fsdp") == 8 and shard_rows == 24 and docs == 2


def shards(
    tokens, cotangent, seg_lengths, alignment, query_weight, query_bias, key_weight, value_weight, value_bias,
    out_weight, out_bias, first_gain, first_shift, inner_weight, inner_bias, outer_weight, outer_bias, second_gain,
    second_shift,
):
    docs, slots, width = tokens.shape
    rows = query_weight.shape[0]
    every = ("dp", "fsdp")
    vectors = (query_bias, value_bias, out_bias, first_gain, first_shift, outer_bias, second_gain, second_shift)
    weights = (query_weight, key_weight, value_weight, out_weight, inner_weight, outer_weight)
    flat = lambda t: t.reshape(docs * slots, width)
    whole = lambda t: t.reshape(docs, slots, width)
    if own_kernels(rows, docs):
        packed = jnp.concatenate((*vectors, inner_bias)).astype(F)[None]
        low, q, k, v, att, lse, hat, inv, norm, act, slope, vec, w0, wa, wb, w2 = forward_fused(
            seg_lengths, tokens, alignment, *weights, packed
        )
        encoded, gfirst, gatt, g1, gvec, ginner, gouter = middle(
            hat, inv, flat(cotangent), vec, act, slope, norm, flat(att), wa, wb, w2
        )
        grad_tokens, gq, gk, gv, gout, ginn, sums, gib = backward_fused(
            seg_lengths, alignment, q, k, v, att, whole(gatt), lse, low, whole(gfirst), w0.reshape(width, -1), gvec,
            ginner, g1.reshape(CHIPS, 48, -1),
        )
        whole_encoded = whole(encoded)
        whole_encoded, grad_tokens, gq, gk, gv, gout, ginn, gouter, *sums, gib = deliver(
            (whole_encoded, grad_tokens, gq, gk, gv, gout, ginn, gouter), sums, gib, inner_bias.shape[0]
        )
    else:
        gather = lambda s: lax.all_gather(s, every, axis=0, tiled=True)
        owned = lambda g: lax.psum_scatter(g.astype(F), every, scatter_dimension=0, tiled=True)
        wq, wk, wv, wo, wi, w2 = (gather(w) for w in weights)
        w0, w1 = jnp.concatenate([wq, wk, wv], axis=1), jnp.concatenate([wo, wi], axis=1)
        vec = jnp.stack([gather(t).astype(F) for t in vectors])
        inner_row = gather(inner_bias).astype(F)[None]
        base, low, q, k, v, att, lse = forward_attention(seg_lengths, tokens, alignment, w0, vec)
        encoded, gfirst, gatt, g1, g2, gvec, ginner = mlp_both(
            flat(att), flat(base), flat(cotangent), w1, w2, vec, inner_row
        )
        gq, gk, gv, two, grad_tokens = backward_attention(
            seg_lengths, alignment, q, k, v, att, whole(gatt), lse, low, whole(gfirst), w0
        )
        gq, gk, gv, g1, gouter = (owned(g) for g in (gq, gk, gv, g1, g2))
        gout, ginn = g1[:, :width], g1[:, width:]
        sums = tuple(owned(two[i] if i < 2 else gvec[i]) for i in range(8))
        gib = owned(ginner[0])
        whole_encoded = whole(encoded)
    return (
        whole_encoded, grad_tokens, gq, sums[0], gk, gv, sums[1], gout, sums[2], sums[3], sums[4], ginn, gib, gouter,
        sums[5], sums[6], sums[7],
    )


def solution(mesh):
    in_specs = (
        P(("dp", "fsdp"), None, None),
        P(("dp", "fsdp"), None, None),
        P(("dp", "fsdp")),
        P(("dp", "fsdp"), None),
        P(("dp", "fsdp"), None),
        P(("dp", "fsdp")),
        P(("dp", "fsdp"), None),
        P(("dp", "fsdp"), None),
        P(("dp", "fsdp")),
        P(("dp", "fsdp"), None),
        P(("dp", "fsdp")),
        P(("dp", "fsdp")),
        P(("dp", "fsdp")),
        P(("dp", "fsdp"), None),
        P(("dp", "fsdp")),
        P(("dp", "fsdp"), None),
        P(("dp", "fsdp")),
        P(("dp", "fsdp")),
        P(("dp", "fsdp")),
    )
    out_specs = (
        P(("dp", "fsdp"), None, None),
        P(("dp", "fsdp"), None, None),
        P(("dp", "fsdp"), None),
        P(("dp", "fsdp")),
        P(("dp", "fsdp"), None),
        P(("dp", "fsdp"), None),
        P(("dp", "fsdp")),
        P(("dp", "fsdp"), None),
        P(("dp", "fsdp")),
        P(("dp", "fsdp")),
        P(("dp", "fsdp")),
        P(("dp", "fsdp"), None),
        P(("dp", "fsdp")),
        P(("dp", "fsdp"), None),
        P(("dp", "fsdp")),
        P(("dp", "fsdp")),
        P(("dp", "fsdp")),
    )
    return jax.shard_map(shards, mesh=mesh, in_specs=in_specs, out_specs=out_specs, check_vma=False)
```

```python
import functools
import jax
import jax.numpy as jnp
from jax import lax
from jax.experimental import pallas as pl
from jax.experimental.pallas import tpu as pltpu
from jax.sharding import PartitionSpec as P

MESH = pl.DeviceIdType.MESH
ANY = pl.BlockSpec(memory_space=pl.ANY)
VMEM = pl.BlockSpec(memory_space=pltpu.VMEM)
PLANES = 4
CHIPS = 16


class Place:
    def __init__(self):
        self.z = lax.axis_index("dp")
        self.f = lax.axis_index("fsdp")
        self.core = self.f % 2
        self.x = (self.f // 2) % 2
        self.y = self.f // 4
        self.sib = self.f + 1 - 2 * self.core
        self.xn = self.f + 2 - 4 * self.x
        self.yn = self.f + 4 - 8 * self.y
        self.spot = self.f // 2
        self.spot_x = self.xn // 2
        self.spot_y = self.yn // 2
        self.spot_d = 3 - self.spot

    def plane(self, back):
        return (self.z + PLANES - back) % PLANES

    def coming(self, k):
        return (self.z, 1 + self.z % 2, (self.z + 2) % PLANES, 3 * ((self.z + 1) % 2))[k]

    def ahead(self, step):
        return (self.z + step) % PLANES

    def greet(self):
        bar = pltpu.get_barrier_semaphore()
        for other in self.partners():
            pl.semaphore_signal(bar, inc=1, device_id=other, device_id_type=MESH)

    def met(self):
        pl.semaphore_wait(pltpu.get_barrier_semaphore(), 3 + PLANES - 1)

    def barrier(self):
        self.greet()
        self.met()

    def partners(self):
        return [(self.z, self.sib), (self.z, self.xn), (self.z, self.yn)] + [
            (self.ahead(k), self.f) for k in range(1, PLANES)
        ]


def remote(src, dst, send, recv, dev):
    return pltpu.make_async_remote_copy(
        src_ref=src, dst_ref=dst, send_sem=send, recv_sem=recv, device_id=dev, device_id_type=MESH
    )


class Gather:
    SEMS = 29

    def __init__(self, place, full, own, send, recv, local, width=None):
        self.p, self.full, self.own = place, full, own
        self.send, self.recv, self.local = send, recv, local
        self.half = None if width is None else width // 2
        self.rows = own.shape[0]
        self.started = []

    def view(self, chip, r0=0, r1=None, core=None):
        core = self.p.core if core is None else core
        r1 = self.rows if r1 is None else r1
        if self.half is None:
            return self.full.at[chip, core, pl.ds(r0, r1 - r0), :]
        cols = pl.ds(pl.multiple_of(core * self.half, 128), self.half)
        return self.full.at[chip, pl.ds(r0, r1 - r0), cols]

    def block(self, plane, core):
        if self.half is None:
            return self.full.at[pl.ds(4 * plane, 4), core]
        cols = pl.ds(pl.multiple_of(core * self.half, 128), self.half)
        return self.full.at[pl.ds(4 * plane, 4), :, cols]

    def cut(self, k):
        if self.rows == 96:
            return 48
        return 32 if k % 2 == 0 else 16

    def copy(self, src, dst, index, dev, send=None):
        return remote(src, dst, self.send.at[index if send is None else send], self.recv.at[index], dev)

    def start(self, make, when=None):
        if when is None:
            make().start()
        else:
            pl.when(when())(lambda: make().start())
        self.started.append((make, when))

    def drain(self):
        for make, when in self.started:
            if when is None:
                make().wait_send()
            else:
                pl.when(when())(lambda: make().wait_send())

    def chip(self, k, spot):
        return 4 * self.p.coming(k) + spot

    def own_copy(self):
        return pltpu.make_async_copy(self.own, self.view(self.chip(0, self.p.spot)), self.local)

    def along_z(self):
        p = self.p
        mine = lambda: self.view(self.chip(0, p.spot))
        self.own_copy().start()
        self.start(lambda: self.copy(self.own, mine(), p.z, (p.z - 1, p.f), 24), lambda: p.z > 0)
        self.start(lambda: self.copy(self.own, mine(), p.z, (p.z + 1, p.f), 25), lambda: p.z < PLANES - 1)

    def onward(self, k, when=None):
        p = self.p
        piece = lambda: self.view(self.chip(k, p.spot))
        goal = lambda: p.z + jnp.where(p.coming(k) < p.z, 1, -1)
        goes = lambda: (goal() >= 0) & (goal() < PLANES)
        wait = lambda: self.copy(piece(), piece(), p.coming(k), (p.z, p.f)).wait_recv()
        both = goes if when is None else lambda: when() & goes()
        if when is None:
            wait()
        else:
            pl.when(when())(wait)
        self.start(lambda: self.copy(piece(), piece(), p.coming(k), (goal(), p.f), 25 + k), both)

    def to_neighbours(self, k):
        p = self.p
        piece = lambda: self.view(self.chip(k, p.spot))
        middle = lambda: p.z % 3 != 0
        if k == 1:
            self.onward(1)
            self.onward(3, middle)
        elif k == 2:
            self.onward(2)
        elif k == 3:
            self.onward(3, lambda: p.z % 3 == 0)
        src = piece if k else lambda: self.own
        self.start(lambda: self.copy(src(), piece(), 4 + k, (p.z, p.xn)))
        self.start(lambda: self.copy(src(), piece(), 8 + k, (p.z, p.yn)))

    def to_diagonal(self, k):
        p, cut = self.p, self.cut(k)
        cx, cy = lambda: self.chip(k, p.spot_x), lambda: self.chip(k, p.spot_y)
        full_x, full_y = self.view(cx()), self.view(cy())
        self.copy(full_x, full_x, 4 + k, (p.z, p.xn)).wait_recv()
        part_x = lambda: self.view(cx(), 0, cut)
        self.start(lambda: self.copy(part_x(), part_x(), 12 + k, (p.z, p.yn)))
        self.copy(full_y, full_y, 8 + k, (p.z, p.yn)).wait_recv()
        part_y = lambda: self.view(cy(), cut, self.rows)
        self.start(lambda: self.copy(part_y(), part_y(), 16 + k, (p.z, p.xn)))

    def to_core(self, k):
        p, cut = self.p, self.cut(k)
        cd = self.chip(k, p.spot_d)
        a, b = self.view(cd, 0, cut), self.view(cd, cut, self.rows)
        self.copy(a, a, 12 + k, (p.z, p.yn)).wait_recv()
        self.copy(b, b, 16 + k, (p.z, p.xn)).wait_recv()
        if k == 0:
            self.own_copy().wait()
        blk = lambda: self.block(p.coming(k), p.core)
        self.start(lambda: self.copy(blk(), blk(), 20 + k, (p.z, p.sib)))

    def finish(self):
        p = self.p
        for k in range(PLANES):
            blk = self.block(p.coming(k), 1 - p.core)
            self.copy(blk, blk, 20 + k, (p.z, p.sib)).wait_recv()


def build_own(place, shard, land, own):
    half = own.shape[1]
    first = place.core == 0
    for c0 in range(0, half, 128):
        mine = shard[:, pl.ds(pl.multiple_of(place.core * half + c0, 128), 128)]
        other = land[:, c0 : c0 + 128]
        top = jnp.where(first, mine, other)
        bottom = jnp.where(first, other, mine)
        own[:, c0 : c0 + 128] = jnp.concatenate([top, bottom], axis=0).astype(own.dtype)


class Pair:
    def __init__(self, place, shard, land, own, send, recv):
        half = own.shape[1]
        src = lambda: shard.at[:, pl.ds(pl.multiple_of((1 - place.core) * half, 128), half)]
        self.c = lambda: remote(src(), land, send, recv, (place.z, place.sib))
        self.args = (place, shard, land, own)

    def start(self):
        self.c().start()

    def done(self):
        self.c().wait()
        build_own(*self.args)


class Scatter:
    SEMS = 4 + 4 + 4 + 4 + 4 + 3 + 1

    def __init__(self, place, full, bufs, out, send, recv, local, width=None):
        self.p, self.full, self.out = place, full, out
        self.sums, self.from_core, self.la, self.lb, self.lx, self.ly, self.lz = bufs[:7]
        if width is not None:
            self.total, self.last = bufs[7:]
        self.send, self.recv, self.local = send, recv, local
        self.half = None if width is None else width // 2
        self.rows = self.sums.shape[1]
        self.started = []

    @staticmethod
    def scratch(rows, cols, two_rows):
        bf = jnp.bfloat16
        shapes = [
            pltpu.VMEM((CHIPS, rows, cols), bf),
            pltpu.VMEM((CHIPS, rows, cols), bf),
            pltpu.VMEM((4, rows - 16, cols), bf),
            pltpu.VMEM((4, rows - 16, cols), bf),
            pltpu.VMEM((4, rows, cols), bf),
            pltpu.VMEM((4, rows, cols), bf),
            pltpu.VMEM((3, rows, cols), bf),
        ]
        if two_rows:
            shapes += [pltpu.VMEM((rows, cols), jnp.float32), pltpu.VMEM((rows // 2, cols), jnp.float32)]
        return shapes

    def chip(self, back, spot):
        return 4 * self.p.plane(back) + spot

    cut = Gather.cut
    copy = Gather.copy
    start = Gather.start
    drain = Gather.drain
    block = Gather.block

    def from_sibling(self, back):
        p = self.p
        blk = lambda: pl.ds(4 * p.plane(back), 4)
        c = pltpu.make_async_copy(self.block(p.plane(back), p.core), self.sums.at[blk()], self.local.at[back])
        c.start()
        self.start(
            lambda: self.copy(
                self.block(p.plane(back), 1 - p.core), self.from_core.at[blk()], back, (p.z, p.sib)
            )
        )

    def to_diagonal(self, back):
        p, cut, rows = self.p, self.cut(back), self.rows
        blk = pl.ds(4 * p.plane(back), 4)
        pltpu.make_async_copy(self.block(p.plane(back), p.core), self.sums.at[blk], self.local.at[back]).wait()
        self.copy(self.from_core.at[blk], self.from_core.at[blk], back, (p.z, p.sib)).wait_recv()
        for j in range(4):
            at = 4 * p.plane(back) + j
            self.sums[at] = self.sums[at] + self.from_core[at]
        cd = lambda: self.chip(back, p.spot_d)
        self.start(
            lambda: self.copy(
                self.sums.at[cd(), pl.ds(0, cut)], self.la.at[back, pl.ds(0, cut)], 4 + back, (p.z, p.xn)
            )
        )
        self.start(
            lambda: self.copy(
                self.sums.at[cd(), pl.ds(cut, rows - cut)],
                self.lb.at[back, pl.ds(0, rows - cut)],
                8 + back,
                (p.z, p.yn),
            )
        )

    def to_neighbours(self, back):
        p, cut, rows = self.p, self.cut(back), self.rows
        cx, cy = self.chip(back, p.spot_x), self.chip(back, p.spot_y)
        a, b = self.la.at[back, pl.ds(0, cut)], self.lb.at[back, pl.ds(0, rows - cut)]
        self.copy(a, a, 4 + back, (p.z, p.xn)).wait_recv()
        self.sums[cy, 0:cut] = self.sums[cy, 0:cut] + a[...]
        to_y = lambda: self.sums.at[self.chip(back, p.spot_y)]
        self.start(lambda: self.copy(to_y(), self.ly.at[back], 16 + back, (p.z, p.yn)))
        self.copy(b, b, 8 + back, (p.z, p.yn)).wait_recv()
        self.sums[cx, cut:rows] = self.sums[cx, cut:rows] + b[...]
        to_x = lambda: self.sums.at[self.chip(back, p.spot_x)]
        self.start(lambda: self.copy(to_x(), self.lx.at[back], 12 + back, (p.z, p.xn)))

    def along_z(self, back):
        p = self.p
        c0 = self.chip(back, p.spot)
        lx, ly = self.lx.at[back], self.ly.at[back]
        self.copy(lx, lx, 12 + back, (p.z, p.xn)).wait_recv()
        self.copy(ly, ly, 16 + back, (p.z, p.yn)).wait_recv()
        f = jnp.float32
        got = self.sums[c0].astype(f) + lx[...].astype(f) + ly[...].astype(f)
        self.sums[c0] = got.astype(jnp.bfloat16)
        if back:
            mine = lambda: self.sums.at[self.chip(back, p.spot)]
            self.start(lambda: self.copy(mine(), self.lz.at[back - 1], 20 + back - 1, (p.plane(back), p.f)))

    def owner(self):
        p = self.p
        f = jnp.float32
        for k in range(3):
            self.copy(self.lz.at[k], self.lz.at[k], 20 + k, (p.z, p.f)).wait_recv()
        total = self.mine().astype(f)
        for k in range(3):
            total = total + self.lz[k].astype(f)
        if self.half is None:
            self.out[...] = total
            return
        self.total[...] = total
        rows = self.rows // 2
        theirs = lambda: self.total.at[pl.ds(pl.multiple_of((1 - p.core) * rows, 8), rows)]
        self.start(lambda: self.copy(theirs(), self.last, 23, (p.z, p.sib)))

    def mine(self):
        return self.sums[self.chip(0, self.p.spot)]

    def finish(self):
        if self.half is None:
            return
        p, half = self.p, self.half
        rows = self.rows // 2
        self.copy(self.last, self.last, 23, (p.z, p.sib)).wait_recv()
        mine = pl.ds(pl.multiple_of(p.core * rows, 8), rows)
        self.out[:, pl.ds(pl.multiple_of(p.core * half, 128), half)] = self.total[mine]
        self.out[:, pl.ds(pl.multiple_of((1 - p.core) * half, 128), half)] = self.last[...]


F = jnp.float32
BF = jnp.bfloat16
NN = (((1,), (0,)), ((), ()))
NT = (((1,), (1,)), ((), ()))
TN = (((0,), (0,)), ((), ()))
SMEM = pl.BlockSpec(memory_space=pltpu.SMEM)
HEADS = 12
HEAD_DIM = 64
QUAD = 4 * HEAD_DIM
scale = HEAD_DIM**-0.5
norm_eps = 1e-05
masked_score = -1000000000.0
LIMIT = 60 * 2**20


def dot(left, right, dims):
    return lax.dot_general(left, right, dims, preferred_element_type=F)


def once(shape, index):
    return pl.BlockSpec(shape, index, pipeline_mode=pl.Buffered(1))


def key_bias(count):
    row = lax.broadcasted_iota(jnp.int32, (128, 1), 0)
    return jnp.where(row < count, 0.0, masked_score).astype(F)


def masked(scores, text, bias):
    return jnp.concatenate([scores[:text], scores[text:] + bias], axis=0)


def head_lanes(h):
    lane = lax.broadcasted_iota(jnp.int32, (1, 128), 1)
    return (lane < HEAD_DIM) if h == 0 else (lane >= HEAD_DIM)


def pair_forward(q2, k2, v2, text, bias, between):
    vt = v2.T
    outs, logs = [], []
    for h in range(2):
        qh = jnp.where(head_lanes(h), q2, BF(0))
        scores = masked(dot(k2, qh, NT), text, bias)
        top = jnp.max(scores, axis=0, keepdims=True)
        expo = jnp.exp(scores - top)
        total = jnp.sum(expo, axis=0, keepdims=True)
        outs.append(dot(vt[HEAD_DIM * h : HEAD_DIM * (h + 1)], expo.astype(BF), NN) * (1.0 / total))
        logs.append(top + jnp.log(total))
        if h == 0:
            between()
    return jnp.concatenate(outs, axis=0).T.astype(BF), logs


def pair_backward(q2, k2, v2, o2, do2, logs, text, bias, between):
    prod = (do2.astype(F) * o2.astype(F)).T
    kt = (k2 * BF(scale)).T
    dq, dk, dv = [], [], []
    for h in range(2):
        rows = slice(HEAD_DIM * h, HEAD_DIM * (h + 1))
        qh = jnp.where(head_lanes(h), q2, BF(0))
        doh = jnp.where(head_lanes(h), do2, BF(0))
        delta = jnp.sum(prod[rows], axis=0, keepdims=True)
        probs = jnp.exp(masked(dot(k2, qh, NT), text, bias) - logs[h])
        grads = (probs * (dot(v2, doh, NT) - delta)).astype(BF)
        dv.append(dot(probs.astype(BF), do2, NN))
        dk.append(dot(grads, q2, NN))
        dq.append(dot(kt[rows], grads, NN))
        if h == 0:
            between()
    first = head_lanes(0)
    return (
        jnp.concatenate(dq, axis=0).T.astype(BF),
        jnp.where(first, dk[0], dk[1]).astype(BF),
        jnp.where(first, dv[0], dv[1]).astype(BF),
    )


def member_of(align, segs):
    return (align == lax.broadcasted_iota(jnp.int32, (segs, align.shape[1]), 0)).astype(F)


def forward_body(b, j, len_ref, tok_ref, al_ref, w_cols, bias_ref, outs, low_s, hook=lambda at: None):
    base_ref, low_ref, q_ref, k_ref, v_ref, att_ref, lse_ref = outs
    text, width = al_ref.shape[1], tok_ref.shape[2]
    segs = tok_ref.shape[1] - text

    @pl.when(j == 0)
    def _():
        member = member_of(al_ref[pl.ds(b, 1), :], segs)
        counts = jnp.maximum(jnp.sum(member, axis=1, keepdims=True), 1.0)
        tok = tok_ref[0]
        pooled = dot(member.astype(BF), tok[:text], NN) / counts
        seg_base = tok[text:].astype(F) + pooled
        base_ref[0, :text] = tok[:text].astype(F)
        base_ref[0, text:] = seg_base
        low_ref[0, :text] = tok[:text]
        low_ref[0, text:] = seg_base.astype(BF)
        low_s[:text] = tok[:text]
        low_s[text:] = seg_base.astype(BF)

    hook(0)
    low = low_s[...]
    parts = []
    for i, ref in enumerate((q_ref, k_ref, v_ref)):
        at = i * width + j * QUAD
        rows = dot(low, w_cols(pl.ds(pl.multiple_of(at, QUAD), QUAD)), NN)
        if i != 1:
            rows = rows + bias_ref[i // 2 : i // 2 + 1, pl.ds(pl.multiple_of(j * QUAD, QUAD), QUAD)]
        rows = rows.astype(BF)
        if i == 0:
            rows = rows * BF(scale)
        ref[0] = rows
        parts.append(rows)
    bias = key_bias(len_ref[b])
    for pr in range(2):
        cols = slice(128 * pr, 128 * pr + 128)
        out, logs = pair_forward(parts[0][:, cols], parts[1][:, cols], parts[2][:, cols], text, bias, lambda: hook(1 + 2 * pr))
        att_ref[0, :, cols] = out
        for h in range(2):
            lse_ref[0, 0, 2 * pr + h : 2 * pr + h + 1, :] = logs[h]
        hook(2 + 2 * pr)


def forward_kernel(len_ref, tok_ref, al_ref, w_ref, bias_ref, *rest):
    w_cols = lambda cols: w_ref[:, cols]
    forward_body(pl.program_id(0), pl.program_id(1), len_ref, tok_ref, al_ref, w_cols, bias_ref, rest[:7], rest[7])


def forward_attention(seg_lengths, tokens, alignment, w0, biases):
    docs, slots, width = tokens.shape
    quads = width // QUAD
    doc = pl.BlockSpec((1, slots, width), lambda b, j: (b, 0, 0))
    quad = pl.BlockSpec((1, slots, QUAD), lambda b, j: (b, 0, j))
    wide = jax.ShapeDtypeStruct((docs, slots, width), BF)
    return pl.pallas_call(
        forward_kernel,
        grid=(docs, quads),
        in_specs=[
            SMEM,
            doc,
            once(alignment.shape, lambda b, j: (0, 0)),
            once(w0.shape, lambda b, j: (0, 0)),
            once(biases.shape, lambda b, j: (0, 0)),
        ],
        out_specs=[doc, doc, quad, quad, quad, quad, pl.BlockSpec((1, 1, 8, slots), lambda b, j: (b, j, 0, 0))],
        out_shape=[
            jax.ShapeDtypeStruct((docs, slots, width), F),
            wide,
            wide,
            wide,
            wide,
            wide,
            jax.ShapeDtypeStruct((docs, quads, 8, slots), F),
        ],
        scratch_shapes=[pltpu.VMEM((slots, width), BF)],
        compiler_params=pltpu.CompilerParams(vmem_limit_bytes=LIMIT),
    )(seg_lengths, tokens, alignment, w0, biases)


def normal_parts(pre):
    size = jnp.abs(pre)
    dens = jnp.exp2(pre * pre * (-0.5 * 1.4426950408889634))
    t = 1.0 / (1.0 + (0.3275911 * 0.7071067811865476) * size)
    poly = t * (
        0.5 * 0.254829592
        + t * (0.5 * -0.284496736 + t * (0.5 * 1.421413741 + t * (0.5 * -1.453152027 + t * (0.5 * 1.061405429))))
    )
    tail = poly * dens
    return jnp.where(pre >= 0, 1.0 - tail, tail), dens * 0.3989422804014327


def norm_parts(values_in):
    mean = jnp.mean(values_in, axis=-1, keepdims=True)
    centred = values_in - mean
    inverse = lax.rsqrt(jnp.mean(centred * centred, axis=-1, keepdims=True) + norm_eps)
    return centred * inverse, inverse


def norm_back(grad_hat, hat, inverse):
    return inverse * (
        grad_hat
        - jnp.mean(grad_hat, axis=-1, keepdims=True)
        - hat * jnp.mean(grad_hat * hat, axis=-1, keepdims=True)
    )


def col_sum(values):
    return jnp.sum(values, axis=0, keepdims=True)


def mlp_norm(att, base, w_out, vec):
    first = base + dot(att, w_out(), NN) + vec(2)
    hat, inv = norm_parts(first)
    return hat, inv, (hat * vec(3) + vec(4)).astype(BF)


def mlp_units(low, w_in, inner_bias, put, first, ff_cut=768, hook=lambda at: None):
    chunks = inner_bias.shape[1] // ff_cut
    pre_of = lambda c: dot(low, w_in(first + c * ff_cut, ff_cut), NN) + inner_bias[:, c * ff_cut : (c + 1) * ff_cut]
    pre = pre_of(0)
    for c in range(chunks):
        later = pre_of(c + 1) if c + 1 < chunks else None
        phi, dens = normal_parts(pre)
        put(slice(c * ff_cut, (c + 1) * ff_cut), (pre * phi).astype(BF), (phi + pre * dens).astype(BF))
        pre = later
        hook(1 + c)


def mlp_second(hat1, act, w_outer, cot, vec, ff_cut=768):
    second = hat1 * vec(3) + vec(4) + vec(5)
    for c in range(act.shape[1] // ff_cut):
        second = second + dot(act[:, c * ff_cut : (c + 1) * ff_cut], w_outer(c * ff_cut, ff_cut), NN)
    hat, inv = norm_parts(second)
    grad_y = cot.astype(F)
    sums = (col_sum(grad_y * hat), col_sum(grad_y))
    return (hat * vec(6) + vec(7)).astype(BF), norm_back(grad_y * vec(6), hat, inv), sums


def mlp_back(grad_second, gmlp, hat1, inv1, slope, w_outer, w_out, w_in, vec, put, ff_cut=768, hook=lambda at: None):
    grad_normed = grad_second
    chunks = slope.shape[1] // ff_cut
    act_of = lambda c: dot(gmlp, w_outer(c * ff_cut, ff_cut), NT)
    gact = act_of(0)
    for c in range(chunks):
        later = act_of(c + 1) if c + 1 < chunks else None
        cols = slice(c * ff_cut, (c + 1) * ff_cut)
        gpre = (gact * slope[:, cols].astype(F)).astype(BF)
        put("pre", cols, gpre)
        grad_normed = grad_normed + dot(gpre, w_in(c * ff_cut, ff_cut), NT)
        gact = later
        if c == 1:
            hook(1)
    grad_first = norm_back(grad_normed * vec(3), hat1, inv1)
    low = grad_first.astype(BF)
    put("first", grad_first, low, col_sum(grad_normed * hat1), col_sum(grad_normed))
    return dot(low, w_out(), NT).astype(BF)


def mlp_kernel(
    tiles, att_ref, base_ref, cot_ref, w1_ref, w2_ref, vec_ref, ib_ref,
    enc_ref, gf_ref, ga_ref, g1_ref, g2_ref, gv_ref, gib_ref,
    att_s, norm_s, act_s, slope_s, gmlp_s, gpre_s, gbr_s,
):
    i = pl.program_id(0)
    rows, width = att_ref.shape

    @pl.when(i == 0)
    def _():
        gv_ref[...] = jnp.zeros_like(gv_ref)
        gib_ref[...] = jnp.zeros_like(gib_ref)

    @pl.when(i < tiles)
    def _():
        at = pl.ds(pl.multiple_of(i * rows, rows), rows)
        vec = lambda k: vec_ref[k : k + 1, :]
        w_out = lambda: w1_ref[:, :width]
        w_in = lambda c, n: w1_ref[:, width + c : width + c + n]
        w_outer = lambda c, n: w2_ref[c : c + n, :]

        def put_units(cols, act, slope):
            act_s[at, cols], slope_s[:, cols] = act, slope

        def put(kind, *got):
            if kind == "pre":
                gpre_s[at, got[0]] = got[1]
                gib_ref[:, got[0]] += col_sum(got[1].astype(F))
            else:
                gf_ref[...], gbr_s[at] = got[:2]
                gv_ref[2:3] += col_sum(got[1].astype(F))
                gv_ref[3:4] += got[2]
                gv_ref[4:5] += got[3]

        att_s[at] = att_ref[...]
        hat1, inv1, low = mlp_norm(att_ref[...], base_ref[...], w_out, vec)
        norm_s[at] = low
        mlp_units(low, w_in, ib_ref[...], put_units, 0)
        enc_ref[...], grad_second, sums = mlp_second(hat1, act_s[at], w_outer, cot_ref[...], vec)
        gmlp = grad_second.astype(BF)
        gmlp_s[at] = gmlp
        gv_ref[5:6] += col_sum(gmlp.astype(F))
        gv_ref[6:7] += sums[0]
        gv_ref[7:8] += sums[1]
        ga_ref[...] = mlp_back(
            grad_second, gmlp, hat1, inv1, slope_s[...], w_outer, w_out, w_in, vec, put
        )

    @pl.when((i >= tiles) & (i < tiles + 4))
    def _():
        cols = pl.ds(pl.multiple_of((i - tiles) * width, width), width)
        g2_ref[...] = dot(act_s[:, cols], gmlp_s[...], TN).astype(BF)

    @pl.when((i >= tiles + 4) & (i < tiles + 8))
    def _():
        cols = pl.ds(pl.multiple_of((i - tiles - 4) * width, width), width)
        g1_ref[...] = dot(norm_s[...], gpre_s[:, cols], TN).astype(BF)

    @pl.when(i == tiles + 8)
    def _():
        g1_ref[...] = dot(att_s[...], gbr_s[...], TN).astype(BF)


def mlp_both(attended, base, cotangent, w1, w2, vec, inner_bias, rows=320):
    total, width = attended.shape
    ff = inner_bias.shape[1]
    tiles = total // rows
    tile = pl.BlockSpec((rows, width), lambda i: (jnp.minimum(i, tiles - 1), 0))
    whole = lambda shape: once(shape, lambda i: (0, 0))
    return pl.pallas_call(
        functools.partial(mlp_kernel, tiles),
        grid=(tiles + 9,),
        in_specs=[tile, tile, tile, whole(w1.shape), whole(w2.shape), whole(vec.shape), whole(inner_bias.shape)],
        out_specs=[
            tile,
            tile,
            tile,
            pl.BlockSpec((width, width), lambda i: (0, jnp.where(i == tiles + 8, 0, jnp.clip(i - tiles - 4, 0, 3) + 1))),
            pl.BlockSpec((width, width), lambda i: (jnp.clip(i - tiles, 0, 3), 0)),
            whole((8, width)),
            whole((1, ff)),
        ],
        out_shape=[
            jax.ShapeDtypeStruct((total, width), BF),
            jax.ShapeDtypeStruct((total, width), F),
            jax.ShapeDtypeStruct((total, width), BF),
            jax.ShapeDtypeStruct((width, width + ff), BF),
            jax.ShapeDtypeStruct((ff, width), BF),
            jax.ShapeDtypeStruct((8, width), F),
            jax.ShapeDtypeStruct((1, ff), F),
        ],
        scratch_shapes=[
            pltpu.VMEM((total, width), BF),
            pltpu.VMEM((total, width), BF),
            pltpu.VMEM((total, ff), BF),
            pltpu.VMEM((rows, ff), BF),
            pltpu.VMEM((total, width), BF),
            pltpu.VMEM((total, ff), BF),
            pltpu.VMEM((total, width), BF),
        ],
        compiler_params=pltpu.CompilerParams(vmem_limit_bytes=LIMIT),
    )(attended, base, cotangent, w1, w2, vec, inner_bias)


def backward_body(j, b, refs, keep, gt_ref, scratch, hook=lambda at: None, later=None):
    len_ref, al_ref, q_ref, k_ref, v_ref, o_ref, do_ref, lse_ref, low_ref, gf_ref, w_ref = refs
    gbase_s, acc_s, vsum_s = scratch
    text, width = al_ref.shape[1], low_ref.shape[2]
    quads = width // QUAD
    align = al_ref[pl.ds(b, 1), :]

    hook(0)
    bias = key_bias(len_ref[b])
    parts = [[], [], []]
    for pr in range(2):
        cols = slice(128 * pr, 128 * pr + 128)
        logs = [lse_ref[0, 0, 2 * pr + h : 2 * pr + h + 1, :] for h in range(2)]
        got = pair_backward(
            q_ref[0, :, cols], k_ref[0, :, cols], v_ref[0, :, cols], o_ref[0, :, cols], do_ref[0, :, cols], logs, text, bias,
            lambda: hook(1 + 2 * pr),
        )
        for i in range(3):
            parts[i].append(got[i])
        if pr == 0:
            hook(2)
    quad_grads = [jnp.concatenate(p, axis=1) for p in parts]
    cols = pl.ds(pl.multiple_of(j * QUAD, QUAD), QUAD)

    if later is None:

        @pl.when(j == 0)
        def _():
            gbase_s[b] = gf_ref[0]

        gbase = gbase_s[b]
        for i in range(3):
            at = pl.ds(pl.multiple_of(i * width + j * QUAD, QUAD), QUAD)
            gbase = gbase + dot(quad_grads[i], w_ref[:, at], NT)
        gbase_s[b] = gbase
    else:
        later(quad_grads)

    low = low_ref[0]
    weight = [dot(low, g, TN) for g in quad_grads]
    sums = [col_sum(quad_grads[0].astype(F)), col_sum(quad_grads[2].astype(F))]

    @pl.when(b == 0)
    def _():
        for i in range(3):
            acc_s[i] = weight[i]
        for i in range(2):
            vsum_s[i : i + 1, cols] = sums[i]

    @pl.when(b == 1)
    def _():
        for i in range(2):
            vsum_s[i : i + 1, cols] += sums[i]
        keep(lambda i: (acc_s[i] + weight[i]).astype(BF))

    if later is None:

        @pl.when(j == quads - 1)
        def _():
            gt_ref[0] = token_grads(gbase, align, text)

    hook(4)


def token_grads(gbase, align, text):
    member = member_of(align, gbase.shape[0] - text)
    counts = jnp.maximum(jnp.sum(member, axis=1, keepdims=True), 1.0)
    share = gbase[text:] / counts
    high = share.astype(BF)
    rest = (share - high.astype(F)).astype(BF)
    sel = member.astype(BF)
    spread = dot(sel, high, TN) + dot(sel, rest, TN)
    return jnp.concatenate([gbase[:text] + spread, gbase[text:]], axis=0).astype(BF)


def vector_cols(vsum_s, gv_ref, gib_ref, cols_s):
    width = gv_ref.shape[1]
    rows = jnp.concatenate([vsum_s[:2], gv_ref[2:], jnp.zeros((120, width), F)], axis=0)
    cols_s[...] = jnp.zeros_like(cols_s)
    share = gib_ref.shape[1] * 24 // width
    for d in range(width // 24):
        cols_s[24 * d : 24 * d + 1, :share] = gib_ref[:, d * share : (d + 1) * share]
    return jnp.concatenate([rows.T, cols_s[...]], axis=1).astype(BF)


def backward_kernel(*refs):
    vsum_ref, gt_ref = refs[14:16]

    def keep(grad):
        for i in range(3):
            refs[11 + i][...] = grad(i)

    backward_body(pl.program_id(0), pl.program_id(1), refs[:11], keep, gt_ref, [refs[16], refs[17], vsum_ref])


def backward_attention(seg_lengths, alignment, q, k, v, att, gatt, lse, low, gfirst, w0):
    docs, slots, width = low.shape
    quads = width // QUAD
    quad = pl.BlockSpec((1, slots, QUAD), lambda j, b: (b, 0, j))
    doc = pl.BlockSpec((1, slots, width), lambda j, b: (b, 0, 0))
    wide = jax.ShapeDtypeStruct((width, width), BF)
    col = pl.BlockSpec((width, QUAD), lambda j, b: (0, j))
    return pl.pallas_call(
        backward_kernel,
        grid=(quads, docs),
        in_specs=[
            SMEM,
            once(alignment.shape, lambda j, b: (0, 0)),
            quad,
            quad,
            quad,
            quad,
            quad,
            pl.BlockSpec((1, 1, 8, slots), lambda j, b: (b, j, 0, 0)),
            doc,
            pl.BlockSpec((1, slots, width), lambda j, b: (jnp.where(j == 0, b, 1), 0, 0)),
            once(w0.shape, lambda j, b: (0, 0)),
        ],
        out_specs=[
            col,
            col,
            col,
            once((8, width), lambda j, b: (0, 0)),
            pl.BlockSpec((1, slots, width), lambda j, b: (jnp.where(j == quads - 1, b, 0), 0, 0)),
        ],
        out_shape=[wide, wide, wide, jax.ShapeDtypeStruct((8, width), F), jax.ShapeDtypeStruct((docs, slots, width), BF)],
        scratch_shapes=[
            pltpu.VMEM((docs, slots, width), F),
            pltpu.VMEM((3, width, QUAD), F),
        ],
        compiler_params=pltpu.CompilerParams(vmem_limit_bytes=LIMIT),
    )(seg_lengths, alignment, q, k, v, att, gatt, lse, low, gfirst, w0)


def at_slots(plan, step, slot):
    for (when, where), calls in plan.items():
        if where == slot:

            @pl.when(step == when)
            def _():
                for call in calls:
                    call()


def each(fn, *backs):
    return [functools.partial(fn, k) for k in backs]


TILE = 320
TILES = 4
ATTEND = 6


def forward_fused_kernel(
    len_ref, tok_ref, al_ref, wq, wk, wv, wo, wi, s2, vp, *rest
):
    low_ref, q_ref, k_ref, v_ref, att_ref, lse_ref = rest[:6]
    hat_ref, inv_ref, norm_ref, act_ref, slope_ref, vec_ref, w0, wa, wb, w2 = rest[6:16]
    (
        low_s, base_s, att_s, norm_s, w0_s, wa_s, wb_s, ib_s, cols_s, s0, sa, sb, land0, landa, landb, own0, owna, ownb,
        pair_sem, local, send, recv,
    ) = rest[16:]
    step = pl.program_id(0)
    width, ff = tok_ref.shape[2], wi.shape[1]
    place = Place()
    pairs = [
        Pair(place, s0, land0, own0, pair_sem.at[0], pair_sem.at[1]),
        Pair(place, sa, landa, owna, pair_sem.at[2], pair_sem.at[3]),
        Pair(place, sb, landb, ownb, pair_sem.at[4], pair_sem.at[5]),
    ]
    g0 = Gather(place, w0_s, own0, send.at[0], recv.at[0], local.at[0], w0.shape[2])
    ga = Gather(place, wa_s, owna, send.at[1], recv.at[1], local.at[1], wa.shape[2])
    gb = Gather(place, wb_s, ownb, send.at[2], recv.at[2], local.at[2], wb.shape[2])
    g2 = Gather(place, w2, s2, send.at[3], recv.at[3], local.at[3])
    saves = [
        lambda: pltpu.make_async_copy(w0_s, w0, local.at[4]),
        lambda: pltpu.make_async_copy(wa_s, wa, local.at[5]),
        lambda: pltpu.make_async_copy(wb_s, wb, local.at[6]),
    ]
    half = ff // 2
    start_of = lambda k: lambda: saves[k]().start()
    wait_of = lambda k: lambda: saves[k]().wait()

    def pack():
        for i, ref in enumerate((wq, wk, wv)):
            s0[:, i * width : (i + 1) * width] = ref[...].astype(F)
        cols_s[:128] = jnp.zeros((128, 128), F)
        values = vp[...].astype(F)
        for k in range(8):
            cols_s[k : k + 1, :24] = values[:, 24 * k : 24 * k + 24]
        s0[:, 3 * width : 3 * width + 128] = cols_s[:128].T[:24]
        s0[:, 3 * width + 128 :] = jnp.zeros((24, 128), F)
        share = ff * 24 // width
        s0[0:1, 3 * width + 128 : 3 * width + 128 + share] = values[:, 192 : 192 + share]

    def pack_rest():
        sa[:, :width] = wo[...].astype(F)
        sa[:, width:] = wi[:, :half].astype(F)
        sb[...] = wi[:, half:].astype(F)

    def vectors():
        cols = w0_s[:, :, 3 * width : 3 * width + 128].reshape(width, 128).astype(F)
        vec_ref[...] = cols.T[:8]
        cols_s[...] = w0_s[:, :, 3 * width + 128 :].reshape(width, 128).astype(F)
        share = ff * 24 // width
        for d in range(width // 24):
            ib_s[:, d * share : (d + 1) * share] = cols_s[24 * d : 24 * d + 1, :share]

    attend_plan = {
        (0, -1): [
            place.greet, pack, place.met, pairs[0].start, pack_rest, pairs[1].start, pairs[2].start, pairs[0].done, g0.along_z,
            functools.partial(g0.to_neighbours, 0), pairs[1].done, pairs[2].done,
        ],
        (0, 0): [
            *each(g0.to_neighbours, 1), *each(g0.to_diagonal, 0), *each(g0.to_neighbours, 2), *each(g0.to_diagonal, 1),
            *each(g0.to_neighbours, 3), ga.along_z, *each(g0.to_core, 0), *each(g0.to_diagonal, 2),
            *each(ga.to_neighbours, 0), *each(g0.to_core, 1), *each(g0.to_diagonal, 3), *each(g0.to_core, 2, 3),
            *each(ga.to_neighbours, 1), g0.finish, start_of(0), vectors,
        ],
        (0, 1): [*each(ga.to_diagonal, 0), *each(ga.to_neighbours, 2)],
        (0, 2): [gb.along_z],
        (0, 3): each(ga.to_diagonal, 1),
        (0, 4): [*each(ga.to_neighbours, 3), *each(gb.to_neighbours, 0)],
        (1, 1): each(ga.to_core, 0),
        (1, 2): [*each(ga.to_diagonal, 2), *each(gb.to_neighbours, 1)],
        (1, 4): each(ga.to_core, 1),
        (2, 1): [*each(ga.to_diagonal, 3), *each(gb.to_neighbours, 2)],
        (2, 2): each(gb.to_diagonal, 0),
        (2, 3): [g2.along_z, *each(ga.to_core, 2)],
        (2, 4): [*each(gb.to_neighbours, 3), *each(gb.to_diagonal, 1)],
        (3, 1): [*each(ga.to_core, 3), *each(g2.to_neighbours, 0)],
        (3, 3): [*each(gb.to_diagonal, 2), *each(gb.to_core, 0)],
        (3, 4): each(g2.to_neighbours, 1),
        (4, 1): [*each(gb.to_diagonal, 3), *each(gb.to_core, 1)],
        (4, 3): [*each(g2.to_diagonal, 0), *each(gb.to_core, 2)],
        (4, 4): each(g2.to_neighbours, 2),
        (5, 1): [*each(gb.to_core, 3), *each(g2.to_diagonal, 1)],
        (5, 3): each(g2.to_neighbours, 3),
    }
    mlp_plan = {
        (6, 0): [ga.finish, start_of(1)],
        (6, 1): each(g2.to_core, 0),
        (6, 5): each(g2.to_diagonal, 2),
        (7, 2): each(g2.to_core, 1),
        (8, 1): each(g2.to_diagonal, 3),
        (9, 1): each(g2.to_core, 2),
        (10, 0): [gb.finish, start_of(2)],
        (10, 2): each(g2.to_core, 3),
        (13, 5): [
            g2.finish, wait_of(0), wait_of(1), wait_of(2), g0.drain, ga.drain, gb.drain, g2.drain,
        ],
    }

    @pl.when(step < ATTEND)
    def _():
        at_slots(attend_plan, step, -1)
        b, j = step // 3, step % 3
        outs = (base_s.at[pl.ds(b, 1)], low_ref, q_ref, k_ref, v_ref, att_ref, lse_ref)
        w_cols = lambda cols: w0_s[:, :, cols].reshape(width, QUAD)
        hook = functools.partial(at_slots, attend_plan, step)
        forward_body(b, j, len_ref, tok_ref, al_ref, w_cols, vec_ref, outs, low_s, hook)
        att_s[b, :, pl.ds(pl.multiple_of(j * QUAD, QUAD), QUAD)] = att_ref[0]

    @pl.when(step >= ATTEND)
    def _():
        hook = functools.partial(at_slots, mlp_plan, step)
        hook(0)
        first_plan = {at: calls for at, calls in mlp_plan.items() if at[0] < ATTEND + TILES}
        second_plan = {at: calls for at, calls in mlp_plan.items() if at[0] >= ATTEND + TILES}
        t = (step - ATTEND) % TILES
        here = pl.ds(pl.multiple_of(t * TILE, TILE), TILE)
        vec = lambda k: vec_ref[k : k + 1, :]

        def put(cols, act, slope):
            act_ref[:, cols], slope_ref[:, cols] = act, slope

        @pl.when(step < ATTEND + TILES)
        def _():
            rows = pl.ds(pl.multiple_of((t % 2) * TILE, TILE), TILE)
            w_out = lambda: wa_s[:, :, :width].reshape(width, width)
            w_in = lambda c, n: wa_s[:, :, width + c : width + c + n].reshape(width, n)
            hat, inv, low = mlp_norm(att_s[t // 2, rows], base_s[t // 2, rows], w_out, vec)
            hat_ref[...] = hat
            inv_ref[...] = jnp.broadcast_to(inv, inv_ref.shape)
            norm_ref[...] = low
            norm_s[here] = low
            mlp_units(low, w_in, ib_s[:, :half], put, 0, hook=functools.partial(at_slots, first_plan, step))

        @pl.when(step >= ATTEND + TILES)
        def _():
            w_in = lambda c, n: wb_s[:, :, c : c + n].reshape(width, n)
            mlp_units(norm_s[here], w_in, ib_s[:, half:], put, 0, hook=functools.partial(at_slots, second_plan, step))

        hook(5)


def forward_fused(seg_lengths, tokens, alignment, wq, wk, wv, wo, wi, s2, vp):
    docs, slots, width = tokens.shape
    ff = wi.shape[1]
    quads = width // QUAD
    n0, na, nb = 3 * width + 256, width + ff // 2, ff // 2
    total = docs * slots
    last = ATTEND - 1
    doc_of = lambda s: jnp.minimum(s, last) // quads
    doc = pl.BlockSpec((1, slots, width), lambda s: (doc_of(s), 0, 0))
    quad = pl.BlockSpec((1, slots, QUAD), lambda s: (doc_of(s), 0, jnp.minimum(s, last) % quads))
    wide = jax.ShapeDtypeStruct((docs, slots, width), BF)
    full = lambda *shape: once(shape, lambda s: (0,) * len(shape))
    tile = lambda n: pl.BlockSpec((TILE, n), lambda s: (jnp.clip(s - ATTEND, 0, TILES - 1), 0))
    past = lambda s: jnp.maximum(s - ATTEND, 0)
    units = pl.BlockSpec((TILE, ff // 2), lambda s: (past(s) % TILES, past(s) // TILES))
    ins = (alignment, wq, wk, wv, wo, wi, s2, vp)
    return pl.pallas_call(
        forward_fused_kernel,
        grid=(ATTEND + 2 * TILES,),
        in_specs=[SMEM, doc] + [full(*a.shape) for a in ins],
        out_specs=[
            doc, quad, quad, quad, quad,
            pl.BlockSpec((1, 1, 8, slots), lambda s: (doc_of(s), jnp.minimum(s, last) % quads, 0, 0)),
            tile(width), tile(128), tile(width), units, units, full(8, width),
        ]
        + [ANY] * 4,
        out_shape=[
            wide,
            wide,
            wide,
            wide,
            wide,
            jax.ShapeDtypeStruct((docs, quads, 8, slots), F),
            jax.ShapeDtypeStruct((total, width), F),
            jax.ShapeDtypeStruct((total, 128), F),
            jax.ShapeDtypeStruct((total, width), BF),
            jax.ShapeDtypeStruct((total, ff), BF),
            jax.ShapeDtypeStruct((total, ff), BF),
            jax.ShapeDtypeStruct((8, width), F),
            *[jax.ShapeDtypeStruct((CHIPS, 48, n), BF) for n in (n0, na, nb)],
            jax.ShapeDtypeStruct((CHIPS, 2, 96, width), BF),
        ],
        scratch_shapes=[
            pltpu.VMEM((slots, width), BF),
            pltpu.VMEM((docs, slots, width), F),
            pltpu.VMEM((docs, slots, width), BF),
            pltpu.VMEM((total, width), BF),
            *[pltpu.VMEM((CHIPS, 48, n), BF) for n in (n0, na, nb)],
            pltpu.VMEM((1, ff), F),
            pltpu.VMEM((width, 128), F),
            *[pltpu.VMEM((24, n), F) for n in (n0, na, nb)],
            *[pltpu.VMEM((24, n // 2), F) for n in (n0, na, nb)],
            *[pltpu.VMEM((48, n // 2), BF) for n in (n0, na, nb)],
            pltpu.SemaphoreType.DMA((6,)),
            pltpu.SemaphoreType.DMA((7,)),
            pltpu.SemaphoreType.DMA((4, Gather.SEMS)),
            pltpu.SemaphoreType.DMA((4, Gather.SEMS)),
        ],
        compiler_params=pltpu.CompilerParams(collective_id=0, has_side_effects=True, vmem_limit_bytes=LIMIT),
    )(seg_lengths, tokens, *ins)


def middle_kernel(hat_ref, inv_ref, cot_ref, vec_ref, *rest):
    act_h, slope_h, norm_h, att_h, wa_h, wb_h, w2_h = rest[:7]
    enc_ref, gf_ref, ga_ref, g1_ref, gv_ref, gib_ref, o_outer = rest[7:14]
    act_s, slope_s, wa_s, wb_s, w2_s, gsec_s, gmlp_s, g2_s = rest[14:22]
    bufs = rest[22:29]
    load_sem, local, send, recv = rest[29:]
    i = pl.program_id(0)
    rows, width = hat_ref.shape
    norm_s, att_s, gbr_s = (act_s.at[:, pl.ds(k * width, width)] for k in range(3))
    tiles = act_s.shape[0] // rows
    place = Place()
    g2 = Scatter(place, g2_s, bufs, o_outer, send.at[0], recv.at[0], local.at[0])

    cut = lambda t: pl.ds(t * rows, rows)
    loads = [lambda: pltpu.make_async_copy(w2_h, w2_s, load_sem.at[0])]
    for t in range(tiles):
        loads.append(lambda t=t: pltpu.make_async_copy(act_h.at[cut(t)], act_s.at[cut(t)], load_sem.at[1 + t]))
    for t in range(tiles):
        loads.append(lambda t=t: pltpu.make_async_copy(slope_h.at[cut(t)], slope_s.at[cut(t)], load_sem.at[5 + t]))
    loads += [
        lambda: pltpu.make_async_copy(wa_h, wa_s, load_sem.at[9]),
        lambda: pltpu.make_async_copy(norm_h, norm_s, load_sem.at[10]),
        lambda: pltpu.make_async_copy(att_h, att_s, load_sem.at[11]),
        lambda: pltpu.make_async_copy(wb_h, wb_s, load_sem.at[12]),
    ]
    wait = lambda k: lambda: loads[k]().wait()
    loads_start = lambda k: lambda: loads[k]().start()

    def begin():
        for load in loads[:2]:
            load().start()
        gv_ref[...] = jnp.zeros_like(gv_ref)
        gib_ref[...] = jnp.zeros_like(gib_ref)
        place.barrier()

    plan = {
        (0, 0): [begin, wait(0), wait(1), *map(loads_start, (2, 3, 4))],
        (1, 0): [wait(2)],
        (2, 0): [wait(3)],
        (3, 0): [wait(4), *map(loads_start, (9, 12, 5))],
        (5, 0): [*map(loads_start, (6, 7, 8))],
        (4, 2): each(g2.from_sibling, 3),
        (5, 2): each(g2.from_sibling, 2),
        (6, 2): each(g2.from_sibling, 1),
        (7, 2): each(g2.from_sibling, 0),
        (6, 0): each(g2.to_diagonal, 3),
        (7, 0): each(g2.to_diagonal, 2),
        (8, 0): [loads_start(10), loads_start(11), wait(9), wait(12), wait(5), *each(g2.to_diagonal, 1)],
        (8, 1): [*each(g2.to_diagonal, 0), *each(g2.to_neighbours, 3)],
        (8, 2): each(g2.to_neighbours, 2),
        (9, 0): [wait(6)],
        (9, 1): each(g2.to_neighbours, 1),
        (9, 2): each(g2.to_neighbours, 0),
        (10, 0): [wait(7)],
        (10, 1): each(g2.along_z, 3),
        (10, 2): each(g2.along_z, 2),
        (11, 0): [wait(8)],
        (11, 2): each(g2.along_z, 1),
        (12, 0): [wait(10)],
        (12, 2): each(g2.along_z, 0),
        (16, 0): [wait(11)],
        (16, 2): [g2.owner, g2.drain],
    }
    hook = functools.partial(at_slots, plan, i)
    hook(0)
    vec = lambda k: vec_ref[k : k + 1, :]
    w_outer = lambda c, n: w2_s[c * CHIPS // act_s.shape[1] : (c + n) * CHIPS // act_s.shape[1]].reshape(n, width)

    @pl.when(i < tiles)
    def _():
        at = pl.ds(pl.multiple_of(i * rows, rows), rows)
        enc_ref[...], grad_second, sums = mlp_second(hat_ref[...], act_s[at], w_outer, cot_ref[...], vec)
        gsec_s[at] = grad_second
        gmlp = grad_second.astype(BF)
        gmlp_s[at] = gmlp
        gv_ref[5:6] += col_sum(gmlp.astype(F))
        gv_ref[6:7] += sums[0]
        gv_ref[7:8] += sums[1]

    @pl.when((i >= tiles) & (i < 2 * tiles))
    def _():
        plane = place.plane(2 * tiles - 1 - i)
        cols = pl.ds(pl.multiple_of(plane * width, width), width)
        g2_s[pl.ds(4 * plane, 4)] = dot(act_s[:, cols], gmlp_s[...], TN).astype(BF).reshape(4, 2, 96, width)

    @pl.when((i >= 2 * tiles) & (i < 3 * tiles))
    def _():
        at = pl.ds(pl.multiple_of((i - 2 * tiles) * rows, rows), rows)

        def put(kind, *got):
            if kind == "pre":
                slope_s[at, got[0]] = got[1]
                gib_ref[:, got[0]] += col_sum(got[1].astype(F))
            else:
                gf_ref[...], gbr_s[at] = got[:2]
                gv_ref[2:3] += col_sum(got[1].astype(F))
                gv_ref[3:4] += got[2]
                gv_ref[4:5] += got[3]

        half = wb_s.shape[2]
        w_out = lambda: wa_s[:, :, :width].reshape(width, width)

        def w_in(c, n):
            part = wa_s[:, :, width + c : width + c + n] if c < half else wb_s[:, :, c - half : c - half + n]
            return part.reshape(width, n)

        ga_ref[...] = mlp_back(
            gsec_s[at], gmlp_s[at], hat_ref[...], inv_ref[:, 0:1], slope_s[at], w_outer, w_out, w_in, vec, put, hook=hook
        )

    @pl.when((i >= 3 * tiles) & (i < 4 * tiles))
    def _():
        cols = pl.ds(pl.multiple_of((i - 3 * tiles) * width, width), width)
        g1_ref[...] = dot(norm_s[...], slope_s[:, cols], TN).astype(BF)

    @pl.when(i == 4 * tiles)
    def _():
        g1_ref[...] = dot(att_s[...], gbr_s[...], TN).astype(BF)

    hook(2)


def middle(hat, inv, cotangent, vec, act, slope, norm, att, wa, wb, w2):
    total, width = hat.shape
    ff = act.shape[1]
    tiles = total // TILE
    early = lambda n: pl.BlockSpec((TILE, n), lambda i: (jnp.minimum(i, tiles - 1), 0))
    late = lambda n: pl.BlockSpec((TILE, n), lambda i: (jnp.clip(i - 2 * tiles, 0, tiles - 1), 0))
    full = lambda *shape: once(shape, lambda i: (0,) * len(shape))
    return pl.pallas_call(
        middle_kernel,
        grid=(4 * tiles + 1,),
        in_specs=[
            pl.BlockSpec(
                (TILE, width),
                lambda i: (jnp.where(i < 2 * tiles, jnp.minimum(i, tiles - 1), jnp.minimum(i - 2 * tiles, tiles - 1)), 0),
            ),
            late(128),
            early(width),
            full(8, width),
        ]
        + [ANY] * 7,
        out_specs=[
            early(width),
            late(width),
            late(width),
            pl.BlockSpec((width, width), lambda i: (0, jnp.where(i == 4 * tiles, 0, jnp.clip(i - 3 * tiles, 0, 3) + 1))),
            full(8, width),
            full(1, ff),
            full(96, width),
        ],
        out_shape=[
            jax.ShapeDtypeStruct((total, width), BF),
            jax.ShapeDtypeStruct((total, width), F),
            jax.ShapeDtypeStruct((total, width), BF),
            jax.ShapeDtypeStruct((width, width + ff), BF),
            jax.ShapeDtypeStruct((8, width), F),
            jax.ShapeDtypeStruct((1, ff), F),
            jax.ShapeDtypeStruct((96, width), F),
        ],
        scratch_shapes=[
            pltpu.VMEM((total, ff), BF),
            pltpu.VMEM((total, ff), BF),
            pltpu.VMEM(wa.shape, BF),
            pltpu.VMEM(wb.shape, BF),
            pltpu.VMEM(w2.shape, BF),
            pltpu.VMEM((total, width), F),
            pltpu.VMEM((total, width), BF),
            pltpu.VMEM(w2.shape, BF),
            *Scatter.scratch(96, width, False),
            pltpu.SemaphoreType.DMA((13,)),
            pltpu.SemaphoreType.DMA((1, 4)),
            pltpu.SemaphoreType.DMA((1, Scatter.SEMS)),
            pltpu.SemaphoreType.DMA((1, Scatter.SEMS)),
        ],
        compiler_params=pltpu.CompilerParams(collective_id=2, has_side_effects=True, vmem_limit_bytes=LIMIT),
    )(hat, inv, cotangent, vec, act, slope, norm, att, wa, wb, w2)


def backward_fused_kernel(widths, *refs):
    ins, (gv_ref, gib_ref, g1_ref) = refs[:11], refs[11:14]
    gt_ref, o_wide, o_inner, o_vec, o_ib = refs[14], refs[15:19], refs[19], refs[20], refs[21]
    scratch, cols_s, gqkv_s, w_s, gf_sem = refs[22:25], refs[25], refs[26], refs[27], refs[28]
    rest = list(refs[29:])
    local, send, recv = rest[-3:]
    j, b = pl.program_id(0), pl.program_id(1)
    step = 2 * j + b
    width = ins[8].shape[2]
    place = Place()
    take = lambda n: [rest.pop(0) for _ in range(n)]
    quad_s, stage = take(3), take(1)[0]
    sources = [g1_ref, *quad_s]
    groups = []
    for i, (src, wide) in enumerate(zip(sources, widths)):
        out = stage.at[:, pl.ds(0, wide)]
        groups.append(Scatter(place, src, take(9), out, send.at[i], recv.at[i], local.at[i], wide))
    g1, q0, q1, q2 = groups

    def give_rest():
        g1.finish()
        o_wide[3][...] = stage[:, :width]
        o_inner[...] = stage[:, width : widths[0]]

    def give_quad(k):
        groups[1 + k].finish()
        for i in range(3):
            o_wide[i][:, k * QUAD : (k + 1) * QUAD] = stage[:, i * QUAD : (i + 1) * QUAD]
        if k == 2:
            o_vec[...] = stage[:, 3 * QUAD : 3 * QUAD + 128].T[:8]
            o_ib[...] = stage[0:1, 3 * QUAD + 128 : 4 * QUAD]

    def keep(grad):
        for k in range(3):

            @pl.when(j == k)
            def _():
                for i in range(3):
                    quad_s[k][:, :, i * QUAD : (i + 1) * QUAD] = grad(i).reshape(CHIPS, 48, QUAD)
                if k == 2:
                    both = vector_cols(scratch[2], gv_ref, gib_ref, cols_s)
                    quad_s[k][:, :, 3 * QUAD :] = both.reshape(CHIPS, 48, QUAD)

    al_ref, gf_h, w_h, gf_s = ins[1], ins[9], ins[10], scratch[0]
    load_w = lambda: pltpu.make_async_copy(w_h, w_s, gf_sem.at[1])
    load = lambda: pltpu.make_async_copy(gf_h, gf_s, gf_sem.at[0])

    def later(grads):
        for i, grad in enumerate(grads):
            gqkv_s[b, :, pl.ds(pl.multiple_of(i * width + j * QUAD, QUAD), QUAD)] = grad

    def tokens_of(doc):
        gbase = gf_s[doc] + dot(gqkv_s[doc], w_s[:, : 3 * width], NT)
        gt_ref[doc] = token_grads(gbase, al_ref[doc : doc + 1, :], al_ref.shape[1])

    late, soon = (3, 2), (1, 0)
    all4 = late + soon
    plan = {
        (0, 0): [place.barrier, *each(g1.from_sibling, *all4), lambda: load().start(), lambda: load_w().start()],
        (0, 2): each(g1.to_diagonal, 3),
        (0, 4): each(g1.to_diagonal, 2, 1, 0),
        (1, 2): each(g1.to_neighbours, 3),
        (1, 4): [*each(g1.to_neighbours, 2, 1, 0), *each(q0.from_sibling, *all4)],
        (2, 2): each(g1.along_z, 3),
        (2, 4): [*each(g1.along_z, 2), *each(q0.to_diagonal, *all4)],
        (3, 2): each(g1.along_z, 1),
        (3, 4): [*each(g1.along_z, 0), *each(q0.to_neighbours, *all4), *each(q1.from_sibling, *all4)],
        (4, 2): each(q1.to_diagonal, *all4),
        (4, 4): [*each(q0.along_z, *all4), *each(q1.to_neighbours, *all4)],
        (5, 2): [g1.owner],
        (5, 4): [
            *each(q2.from_sibling, *all4), lambda: load().wait(), lambda: load_w().wait(), *each(q2.to_diagonal, *all4),
            *each(q1.along_z, *all4), functools.partial(tokens_of, 0), *each(q2.to_neighbours, *all4),
            functools.partial(tokens_of, 1), *each(q2.along_z, *all4), q0.owner, q1.owner, give_rest,
            functools.partial(give_quad, 0), functools.partial(give_quad, 1), q2.owner, functools.partial(give_quad, 2),
            *[g.drain for g in groups],
        ],
    }
    backward_body(j, b, ins, keep, gt_ref, scratch, functools.partial(at_slots, plan, step), later)


def backward_fused(seg_lengths, alignment, q, k, v, att, gatt, lse, low, gfirst, w0, gv, gib, g1):
    docs, slots, width = low.shape
    quads = width // QUAD
    quad = pl.BlockSpec((1, slots, QUAD), lambda j, b: (b, 0, j))
    doc = pl.BlockSpec((1, slots, width), lambda j, b: (b, 0, 0))
    whole = lambda *shape: once(shape, lambda j, b: (0,) * len(shape))
    n1 = g1.shape[2]
    widths = (n1, 3 * QUAD, 3 * QUAD, 4 * QUAD)
    bufs = []
    for wide in widths:
        bufs += Scatter.scratch(48, wide // 2, True)
    n = len(widths)
    shard = jax.ShapeDtypeStruct((24, width), F)
    return pl.pallas_call(
        functools.partial(backward_fused_kernel, widths),
        grid=(quads, docs),
        in_specs=[
            SMEM,
            whole(*alignment.shape),
            quad,
            quad,
            quad,
            quad,
            quad,
            pl.BlockSpec((1, 1, 8, slots), lambda j, b: (b, j, 0, 0)),
            doc,
            ANY,
            ANY,
            whole(*gv.shape),
            whole(*gib.shape),
            ANY,
        ],
        out_specs=[
            whole(docs, slots, width),
            *[whole(24, width)] * 4,
            whole(24, n1 - width),
            whole(8, 24),
            whole(1, 128),
        ],
        out_shape=[
            jax.ShapeDtypeStruct((docs, slots, width), BF),
            shard,
            shard,
            shard,
            shard,
            jax.ShapeDtypeStruct((24, n1 - width), F),
            jax.ShapeDtypeStruct((8, 24), F),
            jax.ShapeDtypeStruct((1, 128), F),
        ],
        scratch_shapes=[
            pltpu.VMEM((docs, slots, width), F),
            pltpu.VMEM((3, width, QUAD), F),
            pltpu.VMEM((8, width), F),
            pltpu.VMEM((width, 128), F),
            pltpu.VMEM((docs, slots, 3 * width), BF),
            pltpu.VMEM(w0.shape, BF),
            pltpu.SemaphoreType.DMA((2,)),
            *[pltpu.VMEM((CHIPS, 48, wide), BF) for wide in widths[1:]],
            pltpu.VMEM((24, n1), F),
            *bufs,
            pltpu.SemaphoreType.DMA((n, 4)),
            pltpu.SemaphoreType.DMA((n, Scatter.SEMS)),
            pltpu.SemaphoreType.DMA((n, Scatter.SEMS)),
        ],
        compiler_params=pltpu.CompilerParams(collective_id=1, has_side_effects=True, vmem_limit_bytes=LIMIT),
    )(seg_lengths, alignment, q, k, v, att, gatt, lse, low, gfirst, w0, gv, gib, g1)


def deliver_kernel(count, *refs):
    ins, sums, gib = refs[:count], refs[count], refs[count + 1]
    outs, vecs, ib_out = refs[count + 2 : 2 * count + 2], refs[2 * count + 2 : 2 * count + 10], refs[2 * count + 10]
    held, sem_in, sem_out = refs[2 * count + 11 : 3 * count + 11], refs[-2], refs[-1]
    loads = [pltpu.make_async_copy(a, b, sem_in.at[i]) for i, (a, b) in enumerate(zip(ins, held))]
    stores = [pltpu.make_async_copy(a, b, sem_out.at[i]) for i, (a, b) in enumerate(zip(held, outs))]
    for c in loads:
        c.start()
    for k, out in enumerate(vecs):
        out[...] = sums[k, :]
    ib_out[...] = gib[0, : ib_out.shape[0]]
    for i in range(count):
        loads[i].wait()
        stores[i].start()
    for c in stores:
        c.wait()


def deliver(arrays, sums, gib, share):
    n = len(arrays)
    return pl.pallas_call(
        functools.partial(deliver_kernel, n),
        out_shape=[jax.ShapeDtypeStruct(a.shape, a.dtype) for a in arrays]
        + [jax.ShapeDtypeStruct((sums.shape[1],), F)] * 8
        + [jax.ShapeDtypeStruct((share,), F)],
        in_specs=[ANY] * n + [VMEM] * 2,
        out_specs=[ANY] * n + [VMEM] * 9,
        scratch_shapes=[pltpu.VMEM(a.shape, a.dtype) for a in arrays] + [pltpu.SemaphoreType.DMA((n,))] * 2,
        compiler_params=pltpu.CompilerParams(vmem_limit_bytes=LIMIT),
    )(*arrays, sums, gib)


def own_kernels(shard_rows, docs):
    return lax.axis_size("dp") == PLANES and lax.axis_size("fsdp") == 8 and shard_rows == 24 and docs == 2


def shards(
    tokens, cotangent, seg_lengths, alignment, query_weight, query_bias, key_weight, value_weight, value_bias,
    out_weight, out_bias, first_gain, first_shift, inner_weight, inner_bias, outer_weight, outer_bias, second_gain,
    second_shift,
):
    docs, slots, width = tokens.shape
    rows = query_weight.shape[0]
    every = ("dp", "fsdp")
    vectors = (query_bias, value_bias, out_bias, first_gain, first_shift, outer_bias, second_gain, second_shift)
    weights = (query_weight, key_weight, value_weight, out_weight, inner_weight, outer_weight)
    flat = lambda t: t.reshape(docs * slots, width)
    whole = lambda t: t.reshape(docs, slots, width)
    if own_kernels(rows, docs):
        packed = jnp.concatenate((*vectors, inner_bias))[None]
        low, q, k, v, att, lse, hat, inv, norm, act, slope, vec, w0, wa, wb, w2 = forward_fused(
            seg_lengths, tokens, alignment, *weights, packed
        )
        encoded, gfirst, gatt, g1, gvec, ginner, gouter = middle(
            hat, inv, flat(cotangent), vec, act, slope, norm, flat(att), wa, wb, w2
        )
        grad_tokens, gq, gk, gv, gout, ginn, sums, gib = backward_fused(
            seg_lengths, alignment, q, k, v, att, whole(gatt), lse, low, whole(gfirst), w0.reshape(width, -1), gvec,
            ginner, g1.reshape(CHIPS, 48, -1),
        )
        whole_encoded = whole(encoded)
        whole_encoded, grad_tokens, gq, gk, gv, gout, ginn, gouter, *sums, gib = deliver(
            (whole_encoded, grad_tokens, gq, gk, gv, gout, ginn, gouter), sums, gib, inner_bias.shape[0]
        )
    else:
        gather = lambda s: lax.all_gather(s, every, axis=0, tiled=True)
        owned = lambda g: lax.psum_scatter(g.astype(F), every, scatter_dimension=0, tiled=True)
        wq, wk, wv, wo, wi, w2 = (gather(w) for w in weights)
        w0, w1 = jnp.concatenate([wq, wk, wv], axis=1), jnp.concatenate([wo, wi], axis=1)
        vec = jnp.stack([gather(t).astype(F) for t in vectors])
        inner_row = gather(inner_bias).astype(F)[None]
        base, low, q, k, v, att, lse = forward_attention(seg_lengths, tokens, alignment, w0, vec)
        encoded, gfirst, gatt, g1, g2, gvec, ginner = mlp_both(
            flat(att), flat(base), flat(cotangent), w1, w2, vec, inner_row
        )
        gq, gk, gv, two, grad_tokens = backward_attention(
            seg_lengths, alignment, q, k, v, att, whole(gatt), lse, low, whole(gfirst), w0
        )
        gq, gk, gv, g1, gouter = (owned(g) for g in (gq, gk, gv, g1, g2))
        gout, ginn = g1[:, :width], g1[:, width:]
        sums = tuple(owned(two[i] if i < 2 else gvec[i]) for i in range(8))
        gib = owned(ginner[0])
        whole_encoded = whole(encoded)
    return (
        whole_encoded, grad_tokens, gq, sums[0], gk, gv, sums[1], gout, sums[2], sums[3], sums[4], ginn, gib, gouter,
        sums[5], sums[6], sums[7],
    )


def solution(mesh):
    in_specs = (
        P(("dp", "fsdp"), None, None),
        P(("dp", "fsdp"), None, None),
        P(("dp", "fsdp")),
        P(("dp", "fsdp"), None),
        P(("dp", "fsdp"), None),
        P(("dp", "fsdp")),
        P(("dp", "fsdp"), None),
        P(("dp", "fsdp"), None),
        P(("dp", "fsdp")),
        P(("dp", "fsdp"), None),
        P(("dp", "fsdp")),
        P(("dp", "fsdp")),
        P(("dp", "fsdp")),
        P(("dp", "fsdp"), None),
        P(("dp", "fsdp")),
        P(("dp", "fsdp"), None),
        P(("dp", "fsdp")),
        P(("dp", "fsdp")),
        P(("dp", "fsdp")),
    )
    out_specs = (
        P(("dp", "fsdp"), None, None),
        P(("dp", "fsdp"), None, None),
        P(("dp", "fsdp"), None),
        P(("dp", "fsdp")),
        P(("dp", "fsdp"), None),
        P(("dp", "fsdp"), None),
        P(("dp", "fsdp")),
        P(("dp", "fsdp"), None),
        P(("dp", "fsdp")),
        P(("dp", "fsdp")),
        P(("dp", "fsdp")),
        P(("dp", "fsdp"), None),
        P(("dp", "fsdp")),
        P(("dp", "fsdp"), None),
        P(("dp", "fsdp")),
        P(("dp", "fsdp")),
        P(("dp", "fsdp")),
    )
    return jax.shard_map(shards, mesh=mesh, in_specs=in_specs, out_specs=out_specs, check_vma=False)
```
